512 devices in a mesh: row: 16 (over x, y_lo, core), blk: 32 (over z, y_hi).
Axes of the slice: x: 4, y: 8 (y_hi: 4, y_lo: 2; y = y_hi * 2 + y_lo), z: 8, core: 2. Of those that a mesh axis runs over, the one named last changes fastest.
Arguments:
- latent: float32 [28, 524288], P(None, ('row', 'blk')), may hold values from -3 to 3, as said below
- w_post: bfloat16 [28, 1024], replicated, may hold values from -1 to 1
- w_proj: bfloat16 [1024, 768], replicated, may hold values from -0.1875 to 0.1875
- gain: float32 [768], replicated, may hold values from 0.25 to 1.75
- text_embed: bfloat16 [1024, 768], P(('row', 'blk')), may hold values from -6 to 6
- labels: int32 [1024], P(('row', 'blk')), may hold values from 0 to 1023, each once
- logit_scale: float32 [1], replicated, may hold values from 20 to 40
- logit_bias: float32 [1], replicated, may hold values from -9 to -6
Outputs:
- grad_image: float32 [1024, 768], P(('row', 'blk'))
- grad_text: float32 [1024, 768], P(('row', 'blk'))
- scalars: float32 [3], replicated
The draws below stay inside these ranges and needn't reach their ends.
Inputs may be any that keep to these rules, and one draw needn't show every extreme that they name: Every entry of latent has magnitude 0.3 or more. `labels`: each of the 1024 texts is the match of exactly one image.
All inputs are finite; a program needn't handle non-finite values.
Results may differ from the reference program's by a relative error of at most 0.0015.
The reference program's roundings to bfloat16 on the way (of `code_bits`, `hidden` and `grad_bf`) count: a program that leaves them out, or rounds other values in their place, can miss the bound.
Values may be sent and summed in bfloat16 or wider, within the bound.
No kernel may reach another device: no remote copies, remote signals or barrier semaphores. Data moves between devices by JAX's collectives and lax.ppermute only.
A program may use at most 64 MiB of HBM per device.

```python
import math
import jax
import jax.numpy as jnp
from jax import lax

D = 768
C = 1024
L = 28
PATCH = 512
PAIR_DEV = 2
TOK_DEV = 1024
PAIRS = 1024
TOKENS = 524288


def draw_latent(key, part):
    key = jax.random.fold_in(key, 7)
    key_base, key_keep, key_size = jax.random.split(key, 3)
    bit_ids = jnp.arange(L, dtype=jnp.int32)
    pair_ids = jnp.arange(PAIRS, dtype=jnp.int32)
    phase = (pair_ids[None, :] * 1000 // PAIRS + bit_ids[:, None] * 1000 // L) % 1000
    threshold = 50 + phase * 600 // 1000
    base_bits = jax.random.randint(key_base, (L, PAIRS), 0, 1000) < threshold
    keep_bits = jax.random.randint(key_keep, (L, TOKENS), 0, 4) > 0
    positive = keep_bits == jnp.repeat(base_bits, PATCH, axis=1)
    place = jnp.repeat((pair_ids.astype(jnp.float32) + 1.0) / PAIRS, PATCH)[None, :]
    spread = jax.random.uniform(key_size, (L, TOKENS), jnp.float32)
    magnitude = 0.3 * jnp.exp(spread * place * math.log(10.0))
    return jnp.where(positive, magnitude, -magnitude).astype(jnp.float32)


def shard_levels(key, dims, shards, low, high):
    loudness, own = 1.0, jax.random.fold_in(key, 6)
    for axis_at, blocks in shards:
        heights = jnp.exp(jax.random.uniform(jax.random.fold_in(own, axis_at), (blocks,), jnp.float32, low / len(shards), high / len(shards)))
        loudness = loudness * jnp.repeat(heights, dims[axis_at] // blocks).reshape([-1 if axis == axis_at else 1 for axis in range(len(dims))])
    return loudness


def bell_draw(stream_key, extent, scale, bound, shards=(), kind=jnp.bfloat16):
    values = jax.random.normal(stream_key, extent, jnp.float32) * scale
    if len(shards) > 0:
        values = shard_levels(stream_key, extent, shards, -0.22, 0.18) * values
    return jnp.clip(values, min=-bound, max=bound).astype(kind)


def setup_inputs(seed: int = 0) -> dict:
    arg_keys = jax.random.split(jax.random.key(seed), 9)
    return {
        "latent": draw_latent(jax.random.fold_in(arg_keys[8], 71), 0),
        "w_post": bell_draw(arg_keys[1], (L, C), L ** -0.5, 1.0),
        "w_proj": bell_draw(arg_keys[2], (C, D), C ** -0.5, 0.1875),
        "gain": jnp.clip(1.0 + 0.15 * jax.random.normal(arg_keys[3], (D,), jnp.float32), 0.25, 1.75),
        "text_embed": bell_draw(arg_keys[4], (PAIRS, D), 1.0, 6.0, ((0, 512),)),
        "labels": jax.random.permutation(arg_keys[5], PAIRS).astype(jnp.int32),
        "logit_scale": jnp.clip(jnp.exp(jax.random.uniform(arg_keys[6], (1,), jnp.float32, math.log(20.0), math.log(40.0))), 20.0, 40.0),
        "logit_bias": jnp.clip(jax.random.uniform(arg_keys[7], (1,), jnp.float32, -9.0, -6.0), -9.0, -6.0),
    }


EPS = 1e-06
SHARPNESS = 4.0

def embed_block(code_bits, w_post, w_proj, gain, image_count):
    pre_act = lax.dot_general(code_bits, w_post, (((0,), (0,)), ((), ())), preferred_element_type=jnp.float32)
    hidden = jax.nn.gelu(pre_act).astype(jnp.bfloat16)
    projected = jnp.dot(hidden, w_proj, preferred_element_type=jnp.float32)
    normed = projected * lax.rsqrt(lax.optimization_barrier(jnp.mean(projected * projected, axis=-1, keepdims=True)) + EPS) * gain
    return lax.optimization_barrier(jnp.mean(normed.reshape(image_count, -1, normed.shape[-1]), axis=1))

def unit_rows(values):
    inverse = lax.rsqrt(lax.optimization_barrier(jnp.sum(values * values, axis=-1, keepdims=True)) + EPS)
    return (values * inverse, inverse)

def code_statistics(latent):
    bit_count = latent.shape[0]
    length = jnp.sqrt(lax.optimization_barrier(jnp.sum(latent * latent, axis=0, keepdims=True)))
    unit_code = latent / length
    quantized = jnp.where(latent > 0, 1.0, -1.0) / math.sqrt(bit_count)
    offset = unit_code - quantized
    commit = jnp.sum(offset * offset)
    sharp_logit = SHARPNESS * math.sqrt(bit_count) * unit_code
    bit_prob = jax.nn.sigmoid(sharp_logit)
    bit_rest = jax.nn.sigmoid(-sharp_logit)
    entropy = -jnp.sum(bit_prob * jax.nn.log_sigmoid(sharp_logit) + bit_rest * jax.nn.log_sigmoid(-sharp_logit))
    usage_sum = lax.optimization_barrier(jnp.sum(bit_prob, axis=1))
    return (commit, entropy, usage_sum)

def binary_entropy(mean_prob):
    return -jnp.sum(mean_prob * jnp.log(mean_prob) + (1.0 - mean_prob) * jnp.log(1.0 - mean_prob))

def reference(latent, w_post, w_proj, gain, text_embed, labels, logit_scale, logit_bias):
    code_bits = jnp.where(latent > 0, 1.0, -1.0).astype(jnp.bfloat16)
    groups = code_bits.reshape(L, PAIRS // PAIR_DEV, TOK_DEV).transpose(1, 0, 2)
    embeds = lax.map(lambda block_codes: embed_block(block_codes, w_post, w_proj, gain, PAIR_DEV), groups)
    embeds = embeds.reshape(PAIRS, D)
    image_unit, image_inv = unit_rows(embeds)
    text_unit, text_inv = unit_rows(text_embed.astype(jnp.float32))
    image_bf = image_unit.astype(jnp.bfloat16)
    text_bf = text_unit.astype(jnp.bfloat16)
    scale_value = logit_scale[0]
    bias_value = logit_bias[0]
    products = jnp.dot(image_bf, text_bf.T, preferred_element_type=jnp.float32)
    text_ids = jnp.arange(PAIRS, dtype=jnp.int32)
    pair_sign = jnp.where(labels[:, None] == text_ids[None, :], jnp.float32(1.0), jnp.float32(-1.0))
    margin = pair_sign * (scale_value * products + bias_value)
    pair_grad = -pair_sign * jax.nn.sigmoid(-margin)
    grad_bf = pair_grad.astype(jnp.bfloat16)
    image_dir = scale_value * jnp.dot(grad_bf, text_bf, preferred_element_type=jnp.float32)
    text_dir = scale_value * jnp.dot(grad_bf.T, image_bf, preferred_element_type=jnp.float32)
    grad_image = (image_dir - image_unit * lax.optimization_barrier(jnp.sum(image_unit * image_dir, axis=-1, keepdims=True))) * image_inv
    grad_text = (text_dir - text_unit * lax.optimization_barrier(jnp.sum(text_unit * text_dir, axis=-1, keepdims=True))) * text_inv
    commit, entropy, usage_sum = code_statistics(latent)
    scalars = jnp.stack([commit / TOKENS, entropy / TOKENS, binary_entropy(usage_sum / TOKENS)])
    return (grad_image, grad_text, scalars)
```

```python
import math

import jax
import jax.numpy as jnp
from jax import lax
from jax.sharding import PartitionSpec as P

EPS = 1e-06
SHARPNESS = 4.0
BITS = 28
SIDE = 128


def embed_block(code_bits, w_post, w_proj, gain, image_count):
    pre_act = lax.dot_general(
        code_bits, w_post, (((0,), (0,)), ((), ())), preferred_element_type=jnp.float32
    )
    hidden = jax.nn.gelu(pre_act).astype(jnp.bfloat16)
    projected = jnp.dot(hidden, w_proj, preferred_element_type=jnp.float32)
    normed = (
        projected * lax.rsqrt(jnp.mean(projected * projected, axis=-1, keepdims=True) + EPS) * gain
    )
    return jnp.mean(normed.reshape(image_count, -1, normed.shape[-1]), axis=1)


def unit_rows(values):
    inverse = lax.rsqrt(jnp.sum(values * values, axis=-1, keepdims=True) + EPS)
    return (values * inverse, inverse)


def code_statistics(latent):
    bit_count = latent.shape[0]
    length = jnp.sqrt(jnp.sum(latent * latent, axis=0, keepdims=True))
    unit_code = latent / length
    quantized = jnp.where(latent > 0, 1.0, -1.0) / math.sqrt(bit_count)
    offset = unit_code - quantized
    commit = jnp.sum(offset * offset)
    sharp_logit = SHARPNESS * math.sqrt(bit_count) * unit_code
    bit_prob = jax.nn.sigmoid(sharp_logit)
    bit_rest = jax.nn.sigmoid(-sharp_logit)
    entropy = -jnp.sum(
        bit_prob * jax.nn.log_sigmoid(sharp_logit) + bit_rest * jax.nn.log_sigmoid(-sharp_logit)
    )
    usage_sum = jnp.sum(bit_prob, axis=1)
    return (commit, entropy, usage_sum)


def binary_entropy(mean_prob):
    return -jnp.sum(mean_prob * jnp.log(mean_prob) + (1.0 - mean_prob) * jnp.log(1.0 - mean_prob))


def three_parts(values):
    first = lax.reduce_precision(values, 8, 7)
    rest = values - first
    second = lax.reduce_precision(rest, 8, 7)
    third = rest - second
    return (first, second, third)


def body(latent, w_post, w_proj, gain, text_embed, labels, logit_scale, logit_bias):
    pair_count, feat_width = text_embed.shape
    n_blk = lax.axis_size("blk")
    n_row = lax.axis_size("row")
    n_dev = n_blk * n_row
    my_dev = lax.axis_index("row") * n_blk + lax.axis_index("blk")
    total_tokens = latent.shape[1] * n_dev
    scale_value = logit_scale[0]
    bias_value = logit_bias[0]

    text_unit, text_inv = unit_rows(text_embed.astype(jnp.float32))
    text_bf = text_unit.astype(jnp.bfloat16)

    commit, entropy, usage = code_statistics(latent)
    sums = jnp.concatenate([commit[None], entropy[None], usage])
    side = jnp.zeros((pair_count, SIDE), jnp.float32)
    parts = jnp.concatenate(three_parts(sums))
    side = side.at[0, : parts.shape[0]].set(parts)
    label_high = labels // 32
    side = side.at[:, SIDE - 2].set(label_high.astype(jnp.float32))
    side = side.at[:, SIDE - 1].set((labels - label_high * 32).astype(jnp.float32))
    text_block = jnp.concatenate([text_bf, side.astype(jnp.bfloat16)], axis=1)

    over_row = lax.all_gather(text_block, "row", axis=0)
    over_blk = lax.all_gather(over_row, "blk", axis=1)
    all_block = over_blk.reshape(n_dev * pair_count, feat_width + SIDE)
    all_text = all_block[:, :feat_width]
    all_side = all_block[:, feat_width:].astype(jnp.float32)

    code_bits = jnp.where(latent > 0, 1.0, -1.0).astype(jnp.bfloat16)
    embeds = embed_block(code_bits, w_post, w_proj, gain, pair_count)
    image_unit, image_inv = unit_rows(embeds)
    image_bf = image_unit.astype(jnp.bfloat16)
    image_blk = lax.all_gather(image_bf, "blk", axis=0, tiled=True)
    all_image = lax.all_gather(image_blk, "row", axis=0, tiled=True)

    all_ids = jnp.arange(n_dev * pair_count, dtype=jnp.int32)
    my_ids = my_dev * pair_count + jnp.arange(pair_count, dtype=jnp.int32)
    all_labels = (all_side[:, SIDE - 2] * 32.0 + all_side[:, SIDE - 1]).astype(jnp.int32)

    def gradient(products, match):
        pair_sign = jnp.where(match, jnp.float32(1.0), jnp.float32(-1.0))
        margin = pair_sign * (scale_value * products + bias_value)
        return (-pair_sign * jax.nn.sigmoid(-margin)).astype(jnp.bfloat16)

    def finish(direction, unit, inverse):
        direction = scale_value * direction
        return (direction - unit * jnp.sum(unit * direction, axis=-1, keepdims=True)) * inverse

    image_dots = jnp.dot(image_bf, all_text.T, preferred_element_type=jnp.float32)
    image_grad = gradient(image_dots, labels[:, None] == all_ids[None, :])
    image_dir = jnp.dot(image_grad, all_text, preferred_element_type=jnp.float32)
    grad_image = finish(image_dir, image_unit, image_inv)

    text_dots = jnp.dot(text_bf, all_image.T, preferred_element_type=jnp.float32)
    text_grad = gradient(text_dots, my_ids[:, None] == all_labels[None, :])
    text_dir = jnp.dot(text_grad, all_image, preferred_element_type=jnp.float32)
    grad_text = finish(text_dir, text_unit, text_inv)

    totals = jnp.sum(all_side, axis=0)
    count = BITS + 2
    totals = totals[:count] + totals[count : 2 * count] + totals[2 * count : 3 * count]
    means = totals / total_tokens
    scalars = jnp.stack([means[0], means[1], binary_entropy(means[2:])])
    return (grad_image, grad_text, scalars)


def solution(mesh):
    return jax.shard_map(
        body,
        mesh=mesh,
        in_specs=(
            P(None, ("row", "blk")),
            P(),
            P(),
            P(),
            P(("row", "blk"), None),
            P(("row", "blk")),
            P(),
            P(),
        ),
        out_specs=(P(("row", "blk"), None), P(("row", "blk"), None), P()),
        check_vma=False,
    )
```

```python
import math

import jax
import jax.numpy as jnp
from jax import lax
from jax.sharding import PartitionSpec as P

EPS = 1e-06
SHARPNESS = 4.0
BITS = 28
SIDE = 128


def embed_block(code_bits, w_post, w_proj, gain, image_count):
    pre_act = lax.dot_general(
        code_bits, w_post, (((0,), (0,)), ((), ())), preferred_element_type=jnp.float32
    )
    hidden = jax.nn.gelu(pre_act).astype(jnp.bfloat16)
    projected = jnp.dot(hidden, w_proj, preferred_element_type=jnp.float32)
    normed = (
        projected * lax.rsqrt(jnp.mean(projected * projected, axis=-1, keepdims=True) + EPS) * gain
    )
    return jnp.mean(normed.reshape(image_count, -1, normed.shape[-1]), axis=1)


def unit_rows(values):
    inverse = lax.rsqrt(jnp.sum(values * values, axis=-1, keepdims=True) + EPS)
    return (values * inverse, inverse)


def code_statistics(latent):
    bit_count = latent.shape[0]
    length = jnp.sqrt(jnp.sum(latent * latent, axis=0, keepdims=True))
    unit_code = latent / length
    quantized = jnp.where(latent > 0, 1.0, -1.0) / math.sqrt(bit_count)
    offset = unit_code - quantized
    commit = jnp.sum(offset * offset)
    sharp_logit = SHARPNESS * math.sqrt(bit_count) * unit_code
    bit_prob = jax.nn.sigmoid(sharp_logit)
    bit_rest = jax.nn.sigmoid(-sharp_logit)
    entropy = -jnp.sum(
        bit_prob * jax.nn.log_sigmoid(sharp_logit) + bit_rest * jax.nn.log_sigmoid(-sharp_logit)
    )
    usage_sum = jnp.sum(bit_prob, axis=1)
    return (commit, entropy, usage_sum)


def binary_entropy(mean_prob):
    return -jnp.sum(mean_prob * jnp.log(mean_prob) + (1.0 - mean_prob) * jnp.log(1.0 - mean_prob))


def three_parts(values):
    first = lax.reduce_precision(values, 8, 7)
    rest = values - first
    second = lax.reduce_precision(rest, 8, 7)
    third = rest - second
    return (first, second, third)


def to_all(block, axis, count):
    return lax.all_to_all(jnp.broadcast_to(block[None], (count,) + block.shape), axis, 0, 0)


def body(latent, w_post, w_proj, gain, text_embed, labels, logit_scale, logit_bias):
    pair_count, feat_width = text_embed.shape
    n_blk = lax.axis_size("blk")
    n_row = lax.axis_size("row")
    n_dev = n_blk * n_row
    total_tokens = latent.shape[1] * n_dev
    scale_value = logit_scale[0]
    bias_value = logit_bias[0]

    text_unit, text_inv = unit_rows(text_embed.astype(jnp.float32))
    text_bf = text_unit.astype(jnp.bfloat16)
    group_text = to_all(text_bf, "blk", n_blk).reshape(n_blk * pair_count, feat_width)

    commit, entropy, usage = code_statistics(latent)
    sums = jnp.concatenate([commit[None], entropy[None], usage])
    side = jnp.zeros((pair_count, SIDE), jnp.float32)
    parts = jnp.concatenate(three_parts(sums))
    side = side.at[0, : parts.shape[0]].set(parts)
    label_high = labels // 32
    side = side.at[:, SIDE - 2].set(label_high.astype(jnp.float32))
    side = side.at[:, SIDE - 1].set((labels - label_high * 32).astype(jnp.float32))

    code_bits = jnp.where(latent > 0, 1.0, -1.0).astype(jnp.bfloat16)
    embeds = embed_block(code_bits, w_post, w_proj, gain, pair_count)
    image_unit, image_inv = unit_rows(embeds)
    image_bf = image_unit.astype(jnp.bfloat16)
    image_block = jnp.concatenate([image_bf, side.astype(jnp.bfloat16)], axis=1)
    group_block = to_all(image_block, "row", n_row).reshape(n_row * pair_count, feat_width + SIDE)
    group_image = group_block[:, :feat_width]
    group_side = group_block[:, feat_width:].astype(jnp.float32)
    group_labels = (group_side[:, SIDE - 2] * 32.0 + group_side[:, SIDE - 1]).astype(jnp.int32)
    group_sums = jnp.sum(group_side, axis=0, keepdims=True)

    text_count = n_blk * pair_count
    text_ids = lax.axis_index("row") * text_count + jnp.arange(text_count, dtype=jnp.int32)
    products = jnp.dot(group_image, group_text.T, preferred_element_type=jnp.float32)
    pair_sign = jnp.where(
        group_labels[:, None] == text_ids[None, :], jnp.float32(1.0), jnp.float32(-1.0)
    )
    margin = pair_sign * (scale_value * products + bias_value)
    grad_bf = (-pair_sign * jax.nn.sigmoid(-margin)).astype(jnp.bfloat16)
    image_part = jnp.dot(grad_bf, group_text, preferred_element_type=jnp.float32)
    text_part = jnp.dot(grad_bf.T, group_image, preferred_element_type=jnp.float32)
    text_part = jnp.concatenate(
        [text_part, jnp.broadcast_to(group_sums, (text_count, SIDE))], axis=1
    )

    def owner_sum(parts, axis, count):
        parts = parts.reshape(count, pair_count, parts.shape[-1])
        return jnp.sum(lax.all_to_all(parts, axis, 0, 0), axis=0)

    def finish(direction, unit, inverse):
        direction = scale_value * direction
        return (direction - unit * jnp.sum(unit * direction, axis=-1, keepdims=True)) * inverse

    image_dir = owner_sum(image_part, "row", n_row)
    text_dir = owner_sum(text_part, "blk", n_blk)
    grad_image = finish(image_dir, image_unit, image_inv)
    grad_text = finish(text_dir[:, :feat_width], text_unit, text_inv)

    totals = text_dir[0, feat_width:]
    count = BITS + 2
    totals = totals[:count] + totals[count : 2 * count] + totals[2 * count : 3 * count]
    means = totals / total_tokens
    scalars = jnp.stack([means[0], means[1], binary_entropy(means[2:])])
    return (grad_image, grad_text, scalars)


def solution(mesh):
    return jax.shard_map(
        body,
        mesh=mesh,
        in_specs=(
            P(None, ("row", "blk")),
            P(),
            P(),
            P(),
            P(("row", "blk"), None),
            P(("row", "blk")),
            P(),
            P(),
        ),
        out_specs=(P(("row", "blk"), None), P(("row", "blk"), None), P()),
        check_vma=False,
    )
```

```python
import functools
import math

import jax
import jax.numpy as jnp
from jax import lax
from jax.sharding import Mesh
from jax.sharding import PartitionSpec as P

EPS = 1e-06
SHARPNESS = 4.0
BITS = 28
SIDE = 128


def embed_block(code_bits, w_post, w_proj, gain, image_count):
    pre_act = lax.dot_general(
        code_bits, w_post, (((0,), (0,)), ((), ())), preferred_element_type=jnp.float32
    )
    hidden = jax.nn.gelu(pre_act).astype(jnp.bfloat16)
    projected = jnp.dot(hidden, w_proj, preferred_element_type=jnp.float32)
    normed = (
        projected * lax.rsqrt(jnp.mean(projected * projected, axis=-1, keepdims=True) + EPS) * gain
    )
    return jnp.mean(normed.reshape(image_count, -1, normed.shape[-1]), axis=1)


def unit_rows(values):
    inverse = lax.rsqrt(jnp.sum(values * values, axis=-1, keepdims=True) + EPS)
    return (values * inverse, inverse)


def code_statistics(latent):
    bit_count = latent.shape[0]
    length = jnp.sqrt(jnp.sum(latent * latent, axis=0, keepdims=True))
    unit_code = latent / length
    quantized = jnp.where(latent > 0, 1.0, -1.0) / math.sqrt(bit_count)
    offset = unit_code - quantized
    commit = jnp.sum(offset * offset)
    sharp_logit = SHARPNESS * math.sqrt(bit_count) * unit_code
    bit_prob = jax.nn.sigmoid(sharp_logit)
    bit_rest = jax.nn.sigmoid(-sharp_logit)
    entropy = -jnp.sum(
        bit_prob * jax.nn.log_sigmoid(sharp_logit) + bit_rest * jax.nn.log_sigmoid(-sharp_logit)
    )
    usage_sum = jnp.sum(bit_prob, axis=1)
    return (commit, entropy, usage_sum)


def binary_entropy(mean_prob):
    return -jnp.sum(mean_prob * jnp.log(mean_prob) + (1.0 - mean_prob) * jnp.log(1.0 - mean_prob))


def three_parts(values):
    first = lax.reduce_precision(values, 8, 7)
    rest = values - first
    second = lax.reduce_precision(rest, 8, 7)
    third = rest - second
    return (first, second, third)


def to_all(block, axis, count):
    return lax.all_to_all(jnp.broadcast_to(block[None], (count,) + block.shape), axis, 0, 0)


IMAGE_AXES = ("z", "core")
TEXT_AXES = ("x", "y_lo", "y_hi")
ROW_AXES = ("x", "y_lo", "core")
BLK_AXES = ("z", "y_hi")


def group_ids(sizes, axes, pair_count):
    count = math.prod(sizes[axis] for axis in axes)
    member = jnp.arange(count * pair_count, dtype=jnp.int32) // pair_count
    place = {axis: lax.axis_index(axis) for axis in ROW_AXES + BLK_AXES}
    for axis in reversed(axes):
        place[axis] = member % sizes[axis]
        member = member // sizes[axis]
    device = jnp.int32(0)
    for axis in ROW_AXES + BLK_AXES:
        device = device * sizes[axis] + place[axis]
    return device * pair_count + jnp.arange(count * pair_count, dtype=jnp.int32) % pair_count


def body(sizes, latent, w_post, w_proj, gain, text_embed, labels, logit_scale, logit_bias):
    pair_count, feat_width = text_embed.shape
    n_image = math.prod(sizes[axis] for axis in IMAGE_AXES)
    n_text = math.prod(sizes[axis] for axis in TEXT_AXES)
    total_tokens = latent.shape[1] * n_image * n_text
    scale_value = logit_scale[0]
    bias_value = logit_bias[0]

    text_unit, text_inv = unit_rows(text_embed.astype(jnp.float32))
    text_bf = text_unit.astype(jnp.bfloat16)
    group_text = to_all(text_bf, TEXT_AXES, n_text).reshape(n_text * pair_count, feat_width)

    commit, entropy, usage = code_statistics(latent)
    sums = jnp.concatenate([commit[None], entropy[None], usage])
    side = jnp.zeros((pair_count, SIDE), jnp.float32)
    parts = jnp.concatenate(three_parts(sums))
    side = side.at[0, : parts.shape[0]].set(parts)
    label_high = labels // 32
    side = side.at[:, SIDE - 2].set(label_high.astype(jnp.float32))
    side = side.at[:, SIDE - 1].set((labels - label_high * 32).astype(jnp.float32))

    code_bits = jnp.where(latent > 0, 1.0, -1.0).astype(jnp.bfloat16)
    embeds = embed_block(code_bits, w_post, w_proj, gain, pair_count)
    image_unit, image_inv = unit_rows(embeds)
    image_bf = image_unit.astype(jnp.bfloat16)
    image_block = jnp.concatenate([image_bf, side.astype(jnp.bfloat16)], axis=1)
    image_block, group_text = lax.optimization_barrier((image_block, group_text))
    group_block = to_all(image_block, IMAGE_AXES, n_image)
    group_block = group_block.reshape(n_image * pair_count, feat_width + SIDE)
    group_image = group_block[:, :feat_width]
    group_side = group_block[:, feat_width:].astype(jnp.float32)
    group_labels = (group_side[:, SIDE - 2] * 32.0 + group_side[:, SIDE - 1]).astype(jnp.int32)
    group_sums = jnp.sum(group_side, axis=0, keepdims=True)

    text_count = n_text * pair_count
    text_ids = group_ids(sizes, TEXT_AXES, pair_count)
    products = jnp.dot(group_image, group_text.T, preferred_element_type=jnp.float32)
    pair_sign = jnp.where(
        group_labels[:, None] == text_ids[None, :], jnp.float32(1.0), jnp.float32(-1.0)
    )
    margin = pair_sign * (scale_value * products + bias_value)
    grad_bf = (-pair_sign * jax.nn.sigmoid(-margin)).astype(jnp.bfloat16)
    image_part = jnp.dot(grad_bf, group_text, preferred_element_type=jnp.float32)
    text_part = jnp.dot(grad_bf.T, group_image, preferred_element_type=jnp.float32)
    text_part = jnp.concatenate(
        [text_part, jnp.broadcast_to(group_sums, (text_count, SIDE))], axis=1
    )

    def owner_sum(parts, axis, count):
        parts = parts.reshape(count, pair_count, parts.shape[-1])
        return jnp.sum(lax.all_to_all(parts, axis, 0, 0), axis=0)

    def finish(direction, unit, inverse):
        direction = scale_value * direction
        return (direction - unit * jnp.sum(unit * direction, axis=-1, keepdims=True)) * inverse

    image_dir = owner_sum(image_part, IMAGE_AXES, n_image)
    text_dir = owner_sum(text_part, TEXT_AXES, n_text)
    grad_image = finish(image_dir, image_unit, image_inv)
    grad_text = finish(text_dir[:, :feat_width], text_unit, text_inv)

    totals = text_dir[0, feat_width:]
    count = BITS + 2
    totals = totals[:count] + totals[count : 2 * count] + totals[2 * count : 3 * count]
    means = totals / total_tokens
    scalars = jnp.stack([means[0], means[1], binary_entropy(means[2:])])
    return (grad_image, grad_text, scalars)


def solution(mesh):
    sizes = {"x": 4, "y_lo": 2, "core": 2, "z": 8, "y_hi": 4}
    names = ROW_AXES + BLK_AXES
    fine = Mesh(mesh.devices.reshape([sizes[axis] for axis in names]), names)
    return jax.shard_map(
        functools.partial(body, sizes),
        mesh=fine,
        in_specs=(P(None, names), P(), P(), P(), P(names, None), P(names), P(), P()),
        out_specs=(P(names, None), P(names, None), P()),
        check_vma=False,
    )
```

```python
import functools
import math

import jax
import jax.numpy as jnp
from jax import lax
from jax.experimental import pallas as pl
from jax.experimental.pallas import tpu as pltpu
from jax.sharding import Mesh
from jax.sharding import PartitionSpec as P

EPS = 1e-06
SHARPNESS = 4.0
BITS = 28
SIDE = 128
CHUNK = 256

ROW_AXES = ("x", "y_lo", "core")
BLK_AXES = ("z", "y_hi")
Y_AXES = ("y_hi", "y_lo")
TEXT_AXES = ("x",) + Y_AXES


def code_sums(latent):
    bit_count = latent.shape[0]
    length = jnp.sqrt(jnp.sum(latent * latent, axis=0, keepdims=True))
    unit_code = latent / length
    root = 1.0 / math.sqrt(bit_count)
    offset = unit_code - jnp.where(latent > 0, root, -root)
    sharp = SHARPNESS * math.sqrt(bit_count) * unit_code
    size = jnp.abs(sharp)
    small = jnp.exp(-size)
    inverse = 1.0 / (1.0 + small)
    rest = small * inverse
    entropy = jnp.log1p(small) + size * rest
    prob = jnp.where(sharp > 0, inverse, rest)

    def total(values):
        return jnp.sum(jnp.sum(values, axis=1, keepdims=True), axis=0, keepdims=True)

    usage = jnp.sum(prob, axis=1, keepdims=True)
    return (total(offset * offset), total(entropy), usage)


def round_bf(values):
    return values.astype(jnp.bfloat16).astype(jnp.float32)


def gelu(x):
    inner = x * (math.sqrt(2.0 / math.pi) + (math.sqrt(2.0 / math.pi) * 0.044715) * (x * x))
    half = 0.5 * x
    return half + half * jnp.tanh(inner)


def image_kernel(
    copies, latent_ref, post_ref, proj_ref, gain_ref, label_ref, block_ref, unit_ref, inv_ref
):
    latent = latent_ref[...]
    bit_count, token_count = latent.shape
    image_count, feat_width = unit_ref.shape
    patch = token_count // image_count

    codes = jnp.where(latent > 0, 1.0, -1.0)
    codes = jnp.transpose(codes, (1, 0)).astype(jnp.bfloat16)
    post = post_ref[...]
    proj = proj_ref[...]
    sums = []
    for first in range(0, token_count, CHUNK):
        pre_act = jnp.dot(codes[first : first + CHUNK], post, preferred_element_type=jnp.float32)
        hidden = gelu(pre_act).astype(jnp.bfloat16)
        projected = jnp.dot(hidden, proj, preferred_element_type=jnp.float32)
        square = jnp.sum(projected * projected, axis=-1, keepdims=True)
        scaled = projected * lax.rsqrt(square * (1.0 / feat_width) + EPS)
        sums.append(jnp.sum(scaled, axis=0, keepdims=True))
    steps = patch // CHUNK
    rows = [functools.reduce(jnp.add, sums[i * steps : (i + 1) * steps]) for i in range(image_count)]
    embeds = jnp.concatenate(rows, axis=0) * gain_ref[...] * (1.0 / patch)
    inverse = lax.rsqrt(jnp.sum(embeds * embeds, axis=-1, keepdims=True) + EPS)
    unit = embeds * inverse
    unit_ref[...] = unit
    inv_ref[...] = jnp.broadcast_to(inverse, inv_ref.shape)

    commit, entropy, usage = code_sums(latent)
    lane = lax.broadcasted_iota(jnp.int32, (bit_count, SIDE), 1)
    bit = lax.broadcasted_iota(jnp.int32, (bit_count, SIDE), 0)
    first = round_bf(usage)
    second = round_bf(usage - first)
    third = usage - first - second
    spread = jnp.where(lane == bit, first, 0.0)
    spread = jnp.where(lane == bit + 32, second, spread)
    spread = jnp.where(lane == bit + 64, third, spread)
    side = jnp.sum(spread, axis=0, keepdims=True)
    place = lax.broadcasted_iota(jnp.int32, (1, SIDE), 1)
    for at, value in ((BITS, commit), (BITS + 1, entropy)):
        first = round_bf(value)
        second = round_bf(value - first)
        third = value - first - second
        side = jnp.where(place == at, first, side)
        side = jnp.where(place == at + 32, second, side)
        side = jnp.where(place == at + 64, third, side)
    sides = []
    for i in range(image_count):
        label = label_ref[i]
        high = (label // 32).astype(jnp.float32)
        low = (label % 32).astype(jnp.float32)
        own = side if i == 0 else jnp.zeros_like(side)
        own = jnp.where(place == SIDE - 2, high, own)
        sides.append(jnp.where(place == SIDE - 1, low, own))
    block = jnp.concatenate([unit, jnp.concatenate(sides, axis=0)], axis=1).astype(jnp.bfloat16)
    block_ref[...] = jnp.broadcast_to(block[None], (copies,) + block.shape)


def embed_images(latent, w_post, w_proj, gain, labels, copies):
    image_count = labels.shape[0]
    feat_width = w_proj.shape[1]
    vmem = pl.BlockSpec(memory_space=pltpu.VMEM)
    return pl.pallas_call(
        functools.partial(image_kernel, copies),
        out_shape=(
            jax.ShapeDtypeStruct((copies, image_count, feat_width + SIDE), jnp.bfloat16),
            jax.ShapeDtypeStruct((image_count, feat_width), jnp.float32),
            jax.ShapeDtypeStruct((image_count, 128), jnp.float32),
        ),
        in_specs=[vmem, vmem, vmem, vmem, pl.BlockSpec(memory_space=pltpu.SMEM)],
        out_specs=(vmem, vmem, vmem),
        compiler_params=pltpu.CompilerParams(vmem_limit_bytes=32 * 1024 * 1024),
        cost_estimate=pl.CostEstimate(
            flops=2_200_000_000, bytes_accessed=1_800_000, transcendentals=1_100_000
        ),
        name="embed_images",
    )(latent, w_post, w_proj, gain.reshape(1, -1), labels)


def unit_rows(values):
    inverse = lax.rsqrt(jnp.sum(values * values, axis=-1, keepdims=True) + EPS)
    return (values * inverse, inverse)


def binary_entropy(mean_prob):
    return -jnp.sum(mean_prob * jnp.log(mean_prob) + (1.0 - mean_prob) * jnp.log(1.0 - mean_prob))


def to_all(block, axes, count):
    return lax.all_to_all(jnp.broadcast_to(block[None], (count,) + block.shape), axes, 0, 0)


def swap_cores(block):
    return lax.ppermute(block, "core", [(0, 1), (1, 0)])


def group_ids(sizes, axes, pair_count):
    count = math.prod(sizes[axis] for axis in axes)
    member = jnp.arange(count * pair_count, dtype=jnp.int32) // pair_count
    place = {axis: lax.axis_index(axis) for axis in ROW_AXES + BLK_AXES}
    for axis in reversed(axes):
        place[axis] = member % sizes[axis]
        member = member // sizes[axis]
    device = jnp.int32(0)
    for axis in ROW_AXES + BLK_AXES:
        device = device * sizes[axis] + place[axis]
    return device * pair_count + jnp.arange(count * pair_count, dtype=jnp.int32) % pair_count


def body(sizes, latent, w_post, w_proj, gain, text_embed, labels, logit_scale, logit_bias):
    pair_count, feat_width = text_embed.shape
    n_x = sizes["x"]
    n_y = sizes["y_hi"] * sizes["y_lo"]
    n_z = sizes["z"]
    text_count = n_x * n_y * pair_count
    total_tokens = latent.shape[1] * math.prod(sizes.values())
    scale_value = logit_scale[0]
    bias_value = logit_bias[0]

    text_unit, text_inv = unit_rows(text_embed.astype(jnp.float32))
    text_bf = text_unit.astype(jnp.bfloat16)
    group_text = to_all(text_bf, TEXT_AXES, n_x * n_y).reshape(text_count, feat_width)

    image_block, image_unit, image_inv = embed_images(latent, w_post, w_proj, gain, labels, n_z)
    image_inv = image_inv[:, :1]
    image_block, group_text = lax.optimization_barrier((image_block, group_text))
    mine = lax.all_to_all(image_block, "z", 0, 0)
    group_block = jnp.concatenate([mine, swap_cores(mine)], axis=0)
    group_block = group_block.reshape(2 * n_z * pair_count, feat_width + SIDE)
    group_image = group_block[:, :feat_width]
    group_side = group_block[:, feat_width:].astype(jnp.float32)
    group_labels = (group_side[:, SIDE - 2] * 32.0 + group_side[:, SIDE - 1]).astype(jnp.int32)
    group_sums = jnp.sum(group_side, axis=0, keepdims=True)

    text_ids = group_ids(sizes, TEXT_AXES, pair_count)
    products = jnp.dot(group_image, group_text.T, preferred_element_type=jnp.float32)
    pair_sign = jnp.where(
        group_labels[:, None] == text_ids[None, :], jnp.float32(1.0), jnp.float32(-1.0)
    )
    margin = pair_sign * (scale_value * products + bias_value)
    grad_bf = (-pair_sign * jax.nn.sigmoid(-margin)).astype(jnp.bfloat16)
    image_part = jnp.dot(grad_bf, group_text, preferred_element_type=jnp.float32)
    text_part = jnp.dot(grad_bf.T, group_image, preferred_element_type=jnp.float32)
    text_part = jnp.concatenate(
        [text_part, jnp.broadcast_to(group_sums, (text_count, SIDE))], axis=1
    )

    def owner_sum(parts, axes):
        return jnp.sum(lax.all_to_all(parts, axes, 0, 0), axis=0)

    def finish(direction, unit, inverse):
        direction = scale_value * direction
        return (direction - unit * jnp.sum(unit * direction, axis=-1, keepdims=True)) * inverse

    image_part = image_part.reshape(2, n_z, pair_count, feat_width)
    image_part = image_part[0] + swap_cores(image_part[1])
    text_part = owner_sum(text_part.reshape(n_x, n_y, pair_count, feat_width + SIDE), "x")
    image_dir = owner_sum(image_part, "z")
    text_dir = owner_sum(text_part, Y_AXES)
    grad_image = finish(image_dir, image_unit, image_inv)
    grad_text = finish(text_dir[:, :feat_width], text_unit, text_inv)

    totals = text_dir[0, feat_width:]
    totals = totals[:32] + totals[32:64] + totals[64:96]
    means = totals / total_tokens
    scalars = jnp.stack([means[BITS], means[BITS + 1], binary_entropy(means[:BITS])])
    return (grad_image, grad_text, scalars)


def solution(mesh):
    sizes = {"x": 4, "y_lo": 2, "core": 2, "z": 8, "y_hi": 4}
    names = ROW_AXES + BLK_AXES
    fine = Mesh(mesh.devices.reshape([sizes[axis] for axis in names]), names)
    return jax.shard_map(
        functools.partial(body, sizes),
        mesh=fine,
        in_specs=(P(None, names), P(), P(), P(), P(names, None), P(names), P(), P()),
        out_specs=(P(names, None), P(names, None), P()),
        check_vma=False,
    )
```

```python
import functools
import math

import jax
import jax.numpy as jnp
from jax import lax
from jax.experimental import pallas as pl
from jax.experimental.pallas import tpu as pltpu
from jax.sharding import PartitionSpec as P

EPS = 1e-06
SHARPNESS = 4.0
BITS = 28
SIDE = 128
CHUNK = 256


def code_sums(latent):
    bit_count = latent.shape[0]
    length = jnp.sqrt(jnp.sum(latent * latent, axis=0, keepdims=True))
    unit_code = latent / length
    root = 1.0 / math.sqrt(bit_count)
    offset = unit_code - jnp.where(latent > 0, root, -root)
    sharp = SHARPNESS * math.sqrt(bit_count) * unit_code
    size = jnp.abs(sharp)
    small = jnp.exp(-size)
    inverse = 1.0 / (1.0 + small)
    rest = small * inverse
    entropy = jnp.log1p(small) + size * rest
    prob = jnp.where(sharp > 0, inverse, rest)

    def total(values):
        return jnp.sum(jnp.sum(values, axis=1, keepdims=True), axis=0, keepdims=True)

    usage = jnp.sum(prob, axis=1, keepdims=True)
    return (total(offset * offset), total(entropy), usage)


def round_bf(values):
    return values.astype(jnp.bfloat16).astype(jnp.float32)


def gelu(x):
    inner = x * (math.sqrt(2.0 / math.pi) + (math.sqrt(2.0 / math.pi) * 0.044715) * (x * x))
    half = 0.5 * x
    return half + half * jnp.tanh(inner)


def image_kernel(
    copies,
    latent_hbm,
    post_hbm,
    proj_hbm,
    gain_ref,
    label_ref,
    block_ref,
    unit_ref,
    inv_ref,
    latent_ref,
    post_ref,
    proj_ref,
    sems,
):
    fetch_latent = pltpu.make_async_copy(latent_hbm, latent_ref, sems.at[0])
    fetch_post = pltpu.make_async_copy(post_hbm, post_ref, sems.at[1])
    fetch_proj = pltpu.make_async_copy(proj_hbm, proj_ref, sems.at[2])
    fetch_latent.start()
    fetch_post.start()
    fetch_proj.start()
    fetch_latent.wait()
    latent = latent_ref[...]
    bit_count, token_count = latent.shape
    image_count, feat_width = unit_ref.shape
    patch = token_count // image_count

    commit, entropy, usage = code_sums(latent)
    lane = lax.broadcasted_iota(jnp.int32, (bit_count, SIDE), 1)
    bit = lax.broadcasted_iota(jnp.int32, (bit_count, SIDE), 0)
    first = round_bf(usage)
    second = round_bf(usage - first)
    third = usage - first - second
    spread = jnp.where(lane == bit, first, 0.0)
    spread = jnp.where(lane == bit + 32, second, spread)
    spread = jnp.where(lane == bit + 64, third, spread)
    side = jnp.sum(spread, axis=0, keepdims=True)
    place = lax.broadcasted_iota(jnp.int32, (1, SIDE), 1)
    for at, value in ((BITS, commit), (BITS + 1, entropy)):
        first = round_bf(value)
        second = round_bf(value - first)
        third = value - first - second
        side = jnp.where(place == at, first, side)
        side = jnp.where(place == at + 32, second, side)
        side = jnp.where(place == at + 64, third, side)
    sides = []
    for i in range(image_count):
        label = label_ref[i]
        high = (label // 32).astype(jnp.float32)
        low = (label % 32).astype(jnp.float32)
        own = side if i == 0 else jnp.zeros_like(side)
        own = jnp.where(place == SIDE - 2, high, own)
        sides.append(jnp.where(place == SIDE - 1, low, own))
    codes = jnp.where(latent > 0, 1.0, -1.0)
    codes = jnp.transpose(codes, (1, 0)).astype(jnp.bfloat16)
    fetch_post.wait()
    post = post_ref[...]
    fetch_proj.wait()
    proj = proj_ref[...]
    sums = []
    for first in range(0, token_count, CHUNK):
        pre_act = jnp.dot(codes[first : first + CHUNK], post, preferred_element_type=jnp.float32)
        hidden = gelu(pre_act).astype(jnp.bfloat16)
        projected = jnp.dot(hidden, proj, preferred_element_type=jnp.float32)
        square = jnp.sum(projected * projected, axis=-1, keepdims=True)
        scaled = projected * lax.rsqrt(square * (1.0 / feat_width) + EPS)
        sums.append(jnp.sum(scaled, axis=0, keepdims=True))
    steps = patch // CHUNK
    rows = [functools.reduce(jnp.add, sums[i * steps : (i + 1) * steps]) for i in range(image_count)]
    embeds = jnp.concatenate(rows, axis=0) * gain_ref[...] * (1.0 / patch)
    inverse = lax.rsqrt(jnp.sum(embeds * embeds, axis=-1, keepdims=True) + EPS)
    unit = embeds * inverse
    unit_ref[...] = unit
    inv_ref[...] = jnp.broadcast_to(inverse, inv_ref.shape)

    block = jnp.concatenate([unit, jnp.concatenate(sides, axis=0)], axis=1).astype(jnp.bfloat16)
    block_ref[...] = jnp.broadcast_to(block[None], (copies,) + block.shape)


def embed_images(latent, w_post, w_proj, gain, labels, copies):
    image_count = labels.shape[0]
    feat_width = w_proj.shape[1]
    vmem = pl.BlockSpec(memory_space=pltpu.VMEM)
    hbm = pl.BlockSpec(memory_space=pl.ANY)
    return pl.pallas_call(
        functools.partial(image_kernel, copies),
        out_shape=(
            jax.ShapeDtypeStruct((copies, image_count, feat_width + SIDE), jnp.bfloat16),
            jax.ShapeDtypeStruct((image_count, feat_width), jnp.float32),
            jax.ShapeDtypeStruct((image_count, 128), jnp.float32),
        ),
        in_specs=[hbm, hbm, hbm, vmem, pl.BlockSpec(memory_space=pltpu.SMEM)],
        out_specs=(vmem, vmem, vmem),
        scratch_shapes=[
            pltpu.VMEM(latent.shape, latent.dtype),
            pltpu.VMEM(w_post.shape, w_post.dtype),
            pltpu.VMEM(w_proj.shape, w_proj.dtype),
            pltpu.SemaphoreType.DMA((3,)),
        ],
        compiler_params=pltpu.CompilerParams(vmem_limit_bytes=56 * 1024 * 1024),
        cost_estimate=pl.CostEstimate(
            flops=2_200_000_000, bytes_accessed=1_800_000, transcendentals=1_100_000
        ),
        name="embed_images",
    )(latent, w_post, w_proj, gain.reshape(1, -1), labels)


def unit_rows(values):
    inverse = lax.rsqrt(jnp.sum(values * values, axis=-1, keepdims=True) + EPS)
    return (values * inverse, inverse)


def tangent(direction, unit, inverse):
    return (direction - unit * jnp.sum(unit * direction, axis=-1, keepdims=True)) * inverse


def text_kernel(text_ref, block_ref):
    unit, _ = unit_rows(text_ref[...].astype(jnp.float32))
    block_ref[...] = jnp.broadcast_to(unit.astype(jnp.bfloat16)[None], block_ref.shape)


def text_blocks(text_embed, copies):
    return pl.pallas_call(
        text_kernel,
        out_shape=jax.ShapeDtypeStruct((copies,) + text_embed.shape, jnp.bfloat16),
        in_specs=[pl.BlockSpec(memory_space=pltpu.VMEM)],
        out_specs=pl.BlockSpec(memory_space=pltpu.VMEM),
        name="text_blocks",
    )(text_embed)


def finish_kernel(total_tokens, parts_ref, text_ref, scale_ref, grad_ref, scalar_ref):
    feat_width = text_ref.shape[-1]
    total = parts_ref[0]
    for member in range(1, parts_ref.shape[0]):
        total = total + parts_ref[member]
    unit, inverse = unit_rows(text_ref[...].astype(jnp.float32))
    grad_ref[...] = tangent(scale_ref[0] * total[:, :feat_width], unit, inverse)
    side = total[:1, feat_width:]
    means = side[:, :32] + side[:, 32:64] + side[:, 64:96]
    means = means * (1.0 / total_tokens)
    place = lax.broadcasted_iota(jnp.int32, means.shape, 1)
    usage = jnp.where(place < BITS, means, 0.5)
    spread = -(usage * jnp.log(usage) + (1.0 - usage) * jnp.log(1.0 - usage))
    scalar_ref[0] = jnp.sum(jnp.where(place == BITS, means, 0.0))
    scalar_ref[1] = jnp.sum(jnp.where(place == BITS + 1, means, 0.0))
    scalar_ref[2] = jnp.sum(jnp.where(place < BITS, spread, 0.0))


def finish_text(parts, text_embed, logit_scale, total_tokens):
    vmem = pl.BlockSpec(memory_space=pltpu.VMEM)
    smem = pl.BlockSpec(memory_space=pltpu.SMEM)
    return pl.pallas_call(
        functools.partial(finish_kernel, total_tokens),
        out_shape=(
            jax.ShapeDtypeStruct(text_embed.shape, jnp.float32),
            jax.ShapeDtypeStruct((3,), jnp.float32),
        ),
        in_specs=[vmem, vmem, smem],
        out_specs=(vmem, smem),
        name="finish_text",
    )(parts, text_embed, logit_scale)


def body(latent, w_post, w_proj, gain, text_embed, labels, logit_scale, logit_bias):
    pair_count, feat_width = text_embed.shape
    n_row = lax.axis_size("row")
    n_blk = lax.axis_size("blk")
    text_count = n_blk * pair_count
    total_tokens = latent.shape[1] * n_row * n_blk
    scale_value = logit_scale[0]
    bias_value = logit_bias[0]

    group_text = lax.all_to_all(text_blocks(text_embed, n_blk), "blk", 0, 0)

    image_block, image_unit, image_inv = embed_images(latent, w_post, w_proj, gain, labels, n_row)
    image_block, group_text = lax.optimization_barrier((image_block, group_text))
    group_text = group_text.reshape(text_count, feat_width)
    group_block = lax.all_to_all(image_block, "row", 0, 0)
    group_block = group_block.reshape(n_row * pair_count, feat_width + SIDE)
    group_image = group_block[:, :feat_width]
    group_side = group_block[:, feat_width:].astype(jnp.float32)
    group_labels = (group_side[:, SIDE - 2] * 32.0 + group_side[:, SIDE - 1]).astype(jnp.int32)
    group_sums = jnp.sum(group_side, axis=0, keepdims=True)

    text_ids = lax.axis_index("row") * text_count + jnp.arange(text_count, dtype=jnp.int32)
    products = jnp.dot(group_image, group_text.T, preferred_element_type=jnp.float32)
    pair_sign = jnp.where(
        group_labels[:, None] == text_ids[None, :], jnp.float32(1.0), jnp.float32(-1.0)
    )
    margin = pair_sign * (scale_value * products + bias_value)
    grad_bf = (-pair_sign * jax.nn.sigmoid(-margin)).astype(jnp.bfloat16)
    image_part = jnp.dot(grad_bf, group_text, preferred_element_type=jnp.float32)
    text_part = jnp.dot(grad_bf.T, group_image, preferred_element_type=jnp.float32)
    text_part = jnp.concatenate(
        [text_part, jnp.broadcast_to(group_sums, (text_count, SIDE))], axis=1
    )

    image_part = image_part.reshape(n_row, pair_count, feat_width)
    image_dir = scale_value * jnp.sum(lax.all_to_all(image_part, "row", 0, 0), axis=0)
    grad_image = tangent(image_dir, image_unit, image_inv[:, :1])

    text_part = text_part.reshape(n_blk, pair_count, feat_width + SIDE)
    text_part = lax.all_to_all(text_part, "blk", 0, 0)
    grad_text, scalars = finish_text(text_part, text_embed, logit_scale, total_tokens)
    return (grad_image, grad_text, scalars)


def solution(mesh):
    return jax.shard_map(
        body,
        mesh=mesh,
        in_specs=(
            P(None, ("row", "blk")),
            P(),
            P(),
            P(),
            P(("row", "blk"), None),
            P(("row", "blk")),
            P(),
            P(),
        ),
        out_specs=(P(("row", "blk"), None), P(("row", "blk"), None), P()),
        check_vma=False,
    )
```

```python
import functools
import math

import jax
import jax.numpy as jnp
from jax import lax
from jax.experimental import pallas as pl
from jax.experimental.pallas import tpu as pltpu
from jax.sharding import Mesh
from jax.sharding import PartitionSpec as P

EPS = 1e-06
SHARPNESS = 4.0
BITS = 28
SIDE = 128
CHUNK = 256

ROW_AXES = ("x", "y_lo", "core")
BLK_AXES = ("z", "y_hi")
TEXT_AXES = ("x", "y_hi")
IMAGE_AXES = ("z", "y_lo")


def code_sums(latent):
    bit_count = latent.shape[0]
    length = jnp.sqrt(jnp.sum(latent * latent, axis=0, keepdims=True))
    unit_code = latent / length
    root = 1.0 / math.sqrt(bit_count)
    offset = unit_code - jnp.where(latent > 0, root, -root)
    sharp = SHARPNESS * math.sqrt(bit_count) * unit_code
    size = jnp.abs(sharp)
    small = jnp.exp(-size)
    inverse = 1.0 / (1.0 + small)
    rest = small * inverse
    entropy = jnp.log1p(small) + size * rest
    prob = jnp.where(sharp > 0, inverse, rest)

    def total(values):
        return jnp.sum(jnp.sum(values, axis=1, keepdims=True), axis=0, keepdims=True)

    usage = jnp.sum(prob, axis=1, keepdims=True)
    return (total(offset * offset), total(entropy), usage)


def round_bf(values):
    return values.astype(jnp.bfloat16).astype(jnp.float32)


def gelu(x):
    inner = x * (math.sqrt(2.0 / math.pi) + (math.sqrt(2.0 / math.pi) * 0.044715) * (x * x))
    half = 0.5 * x
    return half + half * jnp.tanh(inner)


def image_kernel(
    latent_hbm,
    post_hbm,
    proj_hbm,
    gain_ref,
    label_ref,
    block_ref,
    unit_ref,
    inv_ref,
    latent_ref,
    post_ref,
    proj_ref,
    sems,
):
    fetch_latent = pltpu.make_async_copy(latent_hbm, latent_ref, sems.at[0])
    fetch_post = pltpu.make_async_copy(post_hbm, post_ref, sems.at[1])
    fetch_proj = pltpu.make_async_copy(proj_hbm, proj_ref, sems.at[2])
    fetch_latent.start()
    fetch_post.start()
    fetch_proj.start()
    fetch_latent.wait()
    latent = latent_ref[...]
    bit_count, token_count = latent.shape
    image_count, feat_width = unit_ref.shape
    patch = token_count // image_count

    commit, entropy, usage = code_sums(latent)
    lane = lax.broadcasted_iota(jnp.int32, (bit_count, SIDE), 1)
    bit = lax.broadcasted_iota(jnp.int32, (bit_count, SIDE), 0)
    first = round_bf(usage)
    second = round_bf(usage - first)
    third = usage - first - second
    spread = jnp.where(lane == bit, first, 0.0)
    spread = jnp.where(lane == bit + 32, second, spread)
    spread = jnp.where(lane == bit + 64, third, spread)
    side = jnp.sum(spread, axis=0, keepdims=True)
    place = lax.broadcasted_iota(jnp.int32, (1, SIDE), 1)
    for at, value in ((BITS, commit), (BITS + 1, entropy)):
        first = round_bf(value)
        second = round_bf(value - first)
        third = value - first - second
        side = jnp.where(place == at, first, side)
        side = jnp.where(place == at + 32, second, side)
        side = jnp.where(place == at + 64, third, side)
    sides = []
    for i in range(image_count):
        label = label_ref[i]
        high = (label // 32).astype(jnp.float32)
        low = (label % 32).astype(jnp.float32)
        own = side if i == 0 else jnp.zeros_like(side)
        own = jnp.where(place == SIDE - 2, high, own)
        sides.append(jnp.where(place == SIDE - 1, low, own))
    codes = jnp.where(latent > 0, 1.0, -1.0)
    codes = jnp.transpose(codes, (1, 0)).astype(jnp.bfloat16)
    fetch_post.wait()
    post = post_ref[...]
    fetch_proj.wait()
    proj = proj_ref[...]
    sums = []
    for first in range(0, token_count, CHUNK):
        pre_act = jnp.dot(codes[first : first + CHUNK], post, preferred_element_type=jnp.float32)
        hidden = gelu(pre_act).astype(jnp.bfloat16)
        projected = jnp.dot(hidden, proj, preferred_element_type=jnp.float32)
        square = jnp.sum(projected * projected, axis=-1, keepdims=True)
        scaled = projected * lax.rsqrt(square * (1.0 / feat_width) + EPS)
        sums.append(jnp.sum(scaled, axis=0, keepdims=True))
    steps = patch // CHUNK
    rows = [functools.reduce(jnp.add, sums[i * steps : (i + 1) * steps]) for i in range(image_count)]
    embeds = jnp.concatenate(rows, axis=0) * gain_ref[...][None, :] * (1.0 / patch)
    inverse = lax.rsqrt(jnp.sum(embeds * embeds, axis=-1, keepdims=True) + EPS)
    unit = embeds * inverse
    unit_ref[...] = unit
    inv_ref[...] = jnp.broadcast_to(inverse, inv_ref.shape)

    block = jnp.concatenate([unit, jnp.concatenate(sides, axis=0)], axis=1)
    block_ref[...] = block.astype(jnp.bfloat16)


def embed_images(latent, w_post, w_proj, gain, labels):
    image_count = labels.shape[0]
    feat_width = w_proj.shape[1]
    vmem = pl.BlockSpec(memory_space=pltpu.VMEM)
    hbm = pl.BlockSpec(memory_space=pl.ANY)
    return pl.pallas_call(
        image_kernel,
        out_shape=(
            jax.ShapeDtypeStruct((image_count, feat_width + SIDE), jnp.bfloat16),
            jax.ShapeDtypeStruct((image_count, feat_width), jnp.float32),
            jax.ShapeDtypeStruct((image_count, 128), jnp.float32),
        ),
        in_specs=[hbm, hbm, hbm, vmem, pl.BlockSpec(memory_space=pltpu.SMEM)],
        out_specs=(vmem, vmem, vmem),
        scratch_shapes=[
            pltpu.VMEM(latent.shape, latent.dtype),
            pltpu.VMEM(w_post.shape, w_post.dtype),
            pltpu.VMEM(w_proj.shape, w_proj.dtype),
            pltpu.SemaphoreType.DMA((3,)),
        ],
        compiler_params=pltpu.CompilerParams(vmem_limit_bytes=56 * 1024 * 1024),
        cost_estimate=pl.CostEstimate(
            flops=2_200_000_000, bytes_accessed=1_800_000, transcendentals=1_100_000
        ),
        name="embed_images",
    )(latent, w_post, w_proj, gain, labels)


def unit_rows(values):
    inverse = lax.rsqrt(jnp.sum(values * values, axis=-1, keepdims=True) + EPS)
    return (values * inverse, inverse)


def tangent(direction, unit, inverse):
    return (direction - unit * jnp.sum(unit * direction, axis=-1, keepdims=True)) * inverse


def text_kernel(text_ref, block_ref, unit_ref, inv_ref):
    unit, inverse = unit_rows(text_ref[...].astype(jnp.float32))
    block_ref[...] = jnp.broadcast_to(unit.astype(jnp.bfloat16)[None], block_ref.shape)
    unit_ref[...] = unit
    inv_ref[...] = jnp.broadcast_to(inverse, inv_ref.shape)


def text_blocks(text_embed, copies):
    rows = text_embed.shape[0]
    vmem = pl.BlockSpec(memory_space=pltpu.VMEM)
    return pl.pallas_call(
        text_kernel,
        out_shape=(
            jax.ShapeDtypeStruct((copies,) + text_embed.shape, jnp.bfloat16),
            jax.ShapeDtypeStruct(text_embed.shape, jnp.float32),
            jax.ShapeDtypeStruct((rows, 128), jnp.float32),
        ),
        in_specs=[vmem],
        out_specs=(vmem, vmem, vmem),
        name="text_blocks",
    )(text_embed)


def finish_kernel(total_tokens, parts_ref, unit_ref, inv_ref, scale_ref, grad_ref, scalar_ref):
    feat_width = unit_ref.shape[-1]
    total = parts_ref[0]
    for member in range(1, parts_ref.shape[0]):
        total = total + parts_ref[member]
    direction = scale_ref[0] * total[:, :feat_width]
    grad_ref[...] = tangent(direction, unit_ref[...], inv_ref[...][:, :1])
    side = total[:1, feat_width:]
    means = side[:, :32] + side[:, 32:64] + side[:, 64:96]
    means = means * (1.0 / total_tokens)
    place = lax.broadcasted_iota(jnp.int32, means.shape, 1)
    usage = jnp.where(place < BITS, means, 0.5)
    spread = -(usage * jnp.log(usage) + (1.0 - usage) * jnp.log(1.0 - usage))
    scalar_ref[0] = jnp.sum(jnp.where(place == BITS, means, 0.0))
    scalar_ref[1] = jnp.sum(jnp.where(place == BITS + 1, means, 0.0))
    scalar_ref[2] = jnp.sum(jnp.where(place < BITS, spread, 0.0))


def finish_text(parts, text_unit, text_inv, logit_scale, total_tokens):
    vmem = pl.BlockSpec(memory_space=pltpu.VMEM)
    smem = pl.BlockSpec(memory_space=pltpu.SMEM)
    return pl.pallas_call(
        functools.partial(finish_kernel, total_tokens),
        out_shape=(
            jax.ShapeDtypeStruct(text_unit.shape, jnp.float32),
            jax.ShapeDtypeStruct((3,), jnp.float32),
        ),
        in_specs=[vmem, vmem, vmem, smem],
        out_specs=(vmem, smem),
        name="finish_text",
    )(parts, text_unit, text_inv, logit_scale)


def swap_cores(block):
    return lax.ppermute(block, "core", [(0, 1), (1, 0)])


def group_ids(sizes, axes, pair_count):
    count = math.prod(sizes[axis] for axis in axes)
    member = jnp.arange(count * pair_count, dtype=jnp.int32) // pair_count
    place = {axis: lax.axis_index(axis) for axis in ROW_AXES + BLK_AXES}
    for axis in reversed(axes):
        place[axis] = member % sizes[axis]
        member = member // sizes[axis]
    device = jnp.int32(0)
    for axis in ROW_AXES + BLK_AXES:
        device = device * sizes[axis] + place[axis]
    return device * pair_count + jnp.arange(count * pair_count, dtype=jnp.int32) % pair_count


def body(sizes, latent, w_post, w_proj, gain, text_embed, labels, logit_scale, logit_bias):
    pair_count, feat_width = text_embed.shape
    n_image = math.prod(sizes[axis] for axis in IMAGE_AXES)
    n_text = math.prod(sizes[axis] for axis in TEXT_AXES)
    text_count = n_text * pair_count
    total_tokens = latent.shape[1] * math.prod(sizes.values())
    scale_value = logit_scale[0]
    bias_value = logit_bias[0]

    text_block, text_unit, text_inv = text_blocks(text_embed, n_text)
    group_text = lax.all_to_all(text_block, TEXT_AXES, 0, 0)

    image_block, image_unit, image_inv = embed_images(latent, w_post, w_proj, gain, labels)
    chip_block = jnp.concatenate([image_block, swap_cores(image_block)], axis=0)
    image_copies = jnp.broadcast_to(chip_block[None], (n_image,) + chip_block.shape)
    image_copies, group_text = lax.optimization_barrier((image_copies, group_text))
    group_text = group_text.reshape(text_count, feat_width)
    group_block = lax.all_to_all(image_copies, IMAGE_AXES, 0, 0)
    group_block = group_block.reshape(n_image * 2 * pair_count, feat_width + SIDE)
    group_image = group_block[:, :feat_width]
    group_side = group_block[:, feat_width:].astype(jnp.float32)
    group_labels = (group_side[:, SIDE - 2] * 32.0 + group_side[:, SIDE - 1]).astype(jnp.int32)
    group_sums = jnp.sum(group_side, axis=0, keepdims=True)

    text_ids = group_ids(sizes, TEXT_AXES, pair_count)
    products = jnp.dot(group_image, group_text.T, preferred_element_type=jnp.float32)
    pair_sign = jnp.where(
        group_labels[:, None] == text_ids[None, :], jnp.float32(1.0), jnp.float32(-1.0)
    )
    margin = pair_sign * (scale_value * products + bias_value)
    grad_bf = (-pair_sign * jax.nn.sigmoid(-margin)).astype(jnp.bfloat16)
    text_part = jnp.dot(grad_bf.T, group_image, preferred_element_type=jnp.float32)
    text_part = jnp.concatenate(
        [text_part, jnp.broadcast_to(group_sums, (text_count, SIDE))], axis=1
    )
    text_part = text_part.reshape(n_text, pair_count, feat_width + SIDE)
    text_part = lax.all_to_all(text_part, TEXT_AXES, 0, 0)

    image_part = jnp.dot(grad_bf, group_text, preferred_element_type=jnp.float32)
    image_part = image_part.reshape(n_image, 2, pair_count, feat_width)
    image_part = image_part[:, 0] + swap_cores(image_part[:, 1])
    image_part, text_part = lax.optimization_barrier((image_part, text_part))
    image_part = lax.all_to_all(image_part, IMAGE_AXES, 0, 0)
    grad_text, scalars = finish_text(text_part, text_unit, text_inv, logit_scale, total_tokens)
    image_dir = scale_value * jnp.sum(image_part, axis=0)
    grad_image = tangent(image_dir, image_unit, image_inv[:, :1])
    return (grad_image, grad_text, scalars)


def solution(mesh):
    sizes = {"x": 4, "y_lo": 2, "core": 2, "z": 8, "y_hi": 4}
    names = ROW_AXES + BLK_AXES
    fine = Mesh(mesh.devices.reshape([sizes[axis] for axis in names]), names)
    return jax.shard_map(
        functools.partial(body, sizes),
        mesh=fine,
        in_specs=(P(None, names), P(), P(), P(), P(names, None), P(names), P(), P()),
        out_specs=(P(names, None), P(names, None), P()),
        check_vma=False,
    )
```

```python
import functools
import math

import jax
import jax.numpy as jnp
from jax import lax
from jax.experimental import pallas as pl
from jax.experimental.pallas import tpu as pltpu
from jax.sharding import Mesh
from jax.sharding import PartitionSpec as P

EPS = 1e-06
SHARPNESS = 4.0
BITS = 28
SIDE = 128
CHUNK = 256

Z_AXIS, Y_AXIS = "z", "y_hi"
BLK_AXES = (Z_AXIS, Y_AXIS)


def code_sums(latent):
    bit_count = latent.shape[0]
    length = jnp.sqrt(jnp.sum(latent * latent, axis=0, keepdims=True))
    unit_code = latent / length
    root = 1.0 / math.sqrt(bit_count)
    offset = unit_code - jnp.where(latent > 0, root, -root)
    sharp = SHARPNESS * math.sqrt(bit_count) * unit_code
    size = jnp.abs(sharp)
    small = jnp.exp(-size)
    inverse = 1.0 / (1.0 + small)
    rest = small * inverse
    entropy = jnp.log1p(small) + size * rest
    prob = jnp.where(sharp > 0, inverse, rest)

    def total(values):
        return jnp.sum(jnp.sum(values, axis=1, keepdims=True), axis=0, keepdims=True)

    usage = jnp.sum(prob, axis=1, keepdims=True)
    return (total(offset * offset), total(entropy), usage)


def round_bf(values):
    return values.astype(jnp.bfloat16).astype(jnp.float32)


def gelu(x):
    inner = x * (math.sqrt(2.0 / math.pi) + (math.sqrt(2.0 / math.pi) * 0.044715) * (x * x))
    half = 0.5 * x
    return half + half * jnp.tanh(inner)


def image_kernel(
    latent_hbm,
    post_hbm,
    proj_hbm,
    gain_ref,
    label_ref,
    block_ref,
    unit_ref,
    inv_ref,
    latent_ref,
    post_ref,
    proj_ref,
    sems,
):
    fetch_latent = pltpu.make_async_copy(latent_hbm, latent_ref, sems.at[0])
    fetch_post = pltpu.make_async_copy(post_hbm, post_ref, sems.at[1])
    fetch_proj = pltpu.make_async_copy(proj_hbm, proj_ref, sems.at[2])
    fetch_latent.start()
    fetch_post.start()
    fetch_proj.start()
    fetch_latent.wait()
    latent = latent_ref[...]
    bit_count, token_count = latent.shape
    image_count, feat_width = unit_ref.shape
    patch = token_count // image_count

    commit, entropy, usage = code_sums(latent)
    lane = lax.broadcasted_iota(jnp.int32, (bit_count, SIDE), 1)
    bit = lax.broadcasted_iota(jnp.int32, (bit_count, SIDE), 0)
    first = round_bf(usage)
    second = round_bf(usage - first)
    third = usage - first - second
    spread = jnp.where(lane == bit, first, 0.0)
    spread = jnp.where(lane == bit + 32, second, spread)
    spread = jnp.where(lane == bit + 64, third, spread)
    side = jnp.sum(spread, axis=0, keepdims=True)
    place = lax.broadcasted_iota(jnp.int32, (1, SIDE), 1)
    for at, value in ((BITS, commit), (BITS + 1, entropy)):
        first = round_bf(value)
        second = round_bf(value - first)
        third = value - first - second
        side = jnp.where(place == at, first, side)
        side = jnp.where(place == at + 32, second, side)
        side = jnp.where(place == at + 64, third, side)
    sides = []
    for i in range(image_count):
        label = label_ref[i]
        high = (label // 32).astype(jnp.float32)
        low = (label % 32).astype(jnp.float32)
        own = side if i == 0 else jnp.zeros_like(side)
        own = jnp.where(place == SIDE - 2, high, own)
        sides.append(jnp.where(place == SIDE - 1, low, own))
    codes = jnp.where(latent > 0, 1.0, -1.0)
    codes = jnp.transpose(codes, (1, 0)).astype(jnp.bfloat16)
    fetch_post.wait()
    post = post_ref[...]
    fetch_proj.wait()
    proj = proj_ref[...]
    sums = []
    for first in range(0, token_count, CHUNK):
        pre_act = jnp.dot(codes[first : first + CHUNK], post, preferred_element_type=jnp.float32)
        hidden = gelu(pre_act).astype(jnp.bfloat16)
        projected = jnp.dot(hidden, proj, preferred_element_type=jnp.float32)
        square = jnp.sum(projected * projected, axis=-1, keepdims=True)
        scaled = projected * lax.rsqrt(square * (1.0 / feat_width) + EPS)
        sums.append(jnp.sum(scaled, axis=0, keepdims=True))
    steps = patch // CHUNK
    rows = [functools.reduce(jnp.add, sums[i * steps : (i + 1) * steps]) for i in range(image_count)]
    embeds = jnp.concatenate(rows, axis=0) * gain_ref[...][None, :] * (1.0 / patch)
    inverse = lax.rsqrt(jnp.sum(embeds * embeds, axis=-1, keepdims=True) + EPS)
    unit = embeds * inverse
    unit_ref[...] = unit
    inv_ref[...] = jnp.broadcast_to(inverse, inv_ref.shape)

    block = jnp.concatenate([unit, jnp.concatenate(sides, axis=0)], axis=1)
    block_ref[...] = block.astype(jnp.bfloat16)


def embed_images(latent, w_post, w_proj, gain, labels):
    image_count = labels.shape[0]
    feat_width = w_proj.shape[1]
    vmem = pl.BlockSpec(memory_space=pltpu.VMEM)
    hbm = pl.BlockSpec(memory_space=pl.ANY)
    return pl.pallas_call(
        image_kernel,
        out_shape=(
            jax.ShapeDtypeStruct((image_count, feat_width + SIDE), jnp.bfloat16),
            jax.ShapeDtypeStruct((image_count, feat_width), jnp.float32),
            jax.ShapeDtypeStruct((image_count, 128), jnp.float32),
        ),
        in_specs=[hbm, hbm, hbm, vmem, pl.BlockSpec(memory_space=pltpu.SMEM)],
        out_specs=(vmem, vmem, vmem),
        scratch_shapes=[
            pltpu.VMEM(latent.shape, latent.dtype),
            pltpu.VMEM(w_post.shape, w_post.dtype),
            pltpu.VMEM(w_proj.shape, w_proj.dtype),
            pltpu.SemaphoreType.DMA((3,)),
        ],
        compiler_params=pltpu.CompilerParams(vmem_limit_bytes=56 * 1024 * 1024),
        cost_estimate=pl.CostEstimate(
            flops=2_200_000_000, bytes_accessed=1_800_000, transcendentals=1_100_000
        ),
        name="embed_images",
    )(latent, w_post, w_proj, gain, labels)


def unit_rows(values):
    inverse = lax.rsqrt(jnp.sum(values * values, axis=-1, keepdims=True) + EPS)
    return (values * inverse, inverse)


def tangent(direction, unit, inverse):
    return (direction - unit * jnp.sum(unit * direction, axis=-1, keepdims=True)) * inverse


def text_kernel(text_ref, block_ref, unit_ref, inv_ref):
    unit, inverse = unit_rows(text_ref[...].astype(jnp.float32))
    block_ref[...] = jnp.broadcast_to(unit.astype(jnp.bfloat16)[None], block_ref.shape)
    unit_ref[...] = unit
    inv_ref[...] = jnp.broadcast_to(inverse, inv_ref.shape)


def text_blocks(text_embed, copies):
    rows = text_embed.shape[0]
    vmem = pl.BlockSpec(memory_space=pltpu.VMEM)
    return pl.pallas_call(
        text_kernel,
        out_shape=(
            jax.ShapeDtypeStruct((copies,) + text_embed.shape, jnp.bfloat16),
            jax.ShapeDtypeStruct(text_embed.shape, jnp.float32),
            jax.ShapeDtypeStruct((rows, 128), jnp.float32),
        ),
        in_specs=[vmem],
        out_specs=(vmem, vmem, vmem),
        name="text_blocks",
    )(text_embed)


def finish_kernel(total_tokens, parts_ref, unit_ref, inv_ref, scale_ref, grad_ref, scalar_ref):
    feat_width = unit_ref.shape[-1]
    total = parts_ref[0]
    for member in range(1, parts_ref.shape[0]):
        total = total + parts_ref[member]
    direction = scale_ref[0] * total[:, :feat_width]
    grad_ref[...] = tangent(direction, unit_ref[...], inv_ref[...][:, :1])
    side = total[:1, feat_width:]
    means = side[:, :32] + side[:, 32:64] + side[:, 64:96]
    means = means * (1.0 / total_tokens)
    place = lax.broadcasted_iota(jnp.int32, means.shape, 1)
    usage = jnp.where(place < BITS, means, 0.5)
    spread = -(usage * jnp.log(usage) + (1.0 - usage) * jnp.log(1.0 - usage))
    scalar_ref[0] = jnp.sum(jnp.where(place == BITS, means, 0.0))
    scalar_ref[1] = jnp.sum(jnp.where(place == BITS + 1, means, 0.0))
    scalar_ref[2] = jnp.sum(jnp.where(place < BITS, spread, 0.0))


def finish_text(parts, text_unit, text_inv, logit_scale, total_tokens):
    vmem = pl.BlockSpec(memory_space=pltpu.VMEM)
    smem = pl.BlockSpec(memory_space=pltpu.SMEM)
    return pl.pallas_call(
        functools.partial(finish_kernel, total_tokens),
        out_shape=(
            jax.ShapeDtypeStruct(text_unit.shape, jnp.float32),
            jax.ShapeDtypeStruct((3,), jnp.float32),
        ),
        in_specs=[vmem, vmem, vmem, smem],
        out_specs=(vmem, smem),
        name="finish_text",
    )(parts, text_unit, text_inv, logit_scale)


def pair_grad(products, match, scale_value, bias_value):
    pair_sign = jnp.where(match, jnp.float32(1.0), jnp.float32(-1.0))
    margin = pair_sign * (scale_value * products + bias_value)
    return (-pair_sign * jax.nn.sigmoid(-margin)).astype(jnp.bfloat16)


def body(latent, w_post, w_proj, gain, text_embed, labels, logit_scale, logit_bias):
    pair_count, feat_width = text_embed.shape
    n_row = lax.axis_size("row")
    n_z = lax.axis_size(Z_AXIS)
    n_y = lax.axis_size(Y_AXIS)
    n_blk = n_z * n_y
    my_blk = lax.axis_index(Z_AXIS) * n_y + lax.axis_index(Y_AXIS)
    text_count = n_row * pair_count
    total_tokens = latent.shape[1] * n_row * n_blk
    scale_value = logit_scale[0]
    bias_value = logit_bias[0]

    text_block, text_unit, text_inv = text_blocks(text_embed, n_row)
    group_text = lax.all_to_all(text_block, "row", 0, 0).reshape(text_count, feat_width)
    text_pos = jnp.arange(text_count, dtype=jnp.int32)
    first_ids = text_pos // pair_count * (n_blk * pair_count) + text_pos % pair_count

    image_block, image_unit, image_inv = embed_images(latent, w_post, w_proj, gain, labels)
    image_copies = jnp.broadcast_to(image_block[None], (n_blk,) + image_block.shape)
    image_copies, group_text = lax.optimization_barrier((image_copies, group_text))
    all_text = lax.all_gather(lax.all_gather(group_text, Y_AXIS, axis=0), Z_AXIS, axis=0)
    all_text = all_text.reshape(n_blk * text_count, feat_width)

    group_block = lax.all_to_all(image_copies, BLK_AXES, 0, 0)
    group_block = group_block.reshape(n_blk * pair_count, feat_width + SIDE)
    group_image = group_block[:, :feat_width]
    group_side = group_block[:, feat_width:].astype(jnp.float32)
    group_labels = (group_side[:, SIDE - 2] * 32.0 + group_side[:, SIDE - 1]).astype(jnp.int32)
    group_sums = jnp.sum(group_side, axis=0, keepdims=True)

    group_ids = first_ids + my_blk * pair_count
    products = jnp.dot(group_image, group_text.T, preferred_element_type=jnp.float32)
    match = group_labels[:, None] == group_ids[None, :]
    grad_bf = pair_grad(products, match, scale_value, bias_value)
    text_part = jnp.dot(grad_bf.T, group_image, preferred_element_type=jnp.float32)
    text_part = jnp.concatenate(
        [text_part, jnp.broadcast_to(group_sums, (text_count, SIDE))], axis=1
    )
    text_part = text_part.reshape(n_row, pair_count, feat_width + SIDE)
    text_part = lax.all_to_all(text_part, "row", 0, 0)
    grad_text, scalars = finish_text(text_part, text_unit, text_inv, logit_scale, total_tokens)

    image_bf = image_block[:, :feat_width]
    all_ids = jnp.arange(n_blk, dtype=jnp.int32)[:, None] * pair_count + first_ids[None, :]
    products = jnp.dot(image_bf, all_text.T, preferred_element_type=jnp.float32)
    match = labels[:, None] == all_ids.reshape(1, -1)
    grad_bf = pair_grad(products, match, scale_value, bias_value)
    image_dir = jnp.dot(grad_bf, all_text, preferred_element_type=jnp.float32)
    grad_image = tangent(scale_value * image_dir, image_unit, image_inv[:, :1])
    return (grad_image, grad_text, scalars)


def solution(mesh):
    n_row, n_blk = mesh.devices.shape
    names = ("row", Z_AXIS, Y_AXIS)
    fine = Mesh(mesh.devices.reshape(n_row, n_blk // 4, 4), names)
    return jax.shard_map(
        body,
        mesh=fine,
        in_specs=(P(None, names), P(), P(), P(), P(names, None), P(names), P(), P()),
        out_specs=(P(names, None), P(names, None), P()),
        check_vma=False,
    )
```

```python
import functools
import math

import jax
import jax.numpy as jnp
from jax import lax
from jax.experimental import pallas as pl
from jax.experimental.pallas import tpu as pltpu
from jax.sharding import Mesh
from jax.sharding import PartitionSpec as P

EPS = 1e-06
SHARPNESS = 4.0
BITS = 28
SIDE = 128
CHUNK = 256

ROW_AXES = ("x", "y_lo", "core")
BLK_AXES = ("z", "y_hi")
TEXT_AXES = ("z", "y_hi", "y_lo")


def code_sums(latent):
    bit_count = latent.shape[0]
    length = jnp.sqrt(jnp.sum(latent * latent, axis=0, keepdims=True))
    unit_code = latent / length
    root = 1.0 / math.sqrt(bit_count)
    offset = unit_code - jnp.where(latent > 0, root, -root)
    sharp = SHARPNESS * math.sqrt(bit_count) * unit_code
    size = jnp.abs(sharp)
    small = jnp.exp(-size)
    inverse = 1.0 / (1.0 + small)
    rest = small * inverse
    entropy = jnp.log1p(small) + size * rest
    prob = jnp.where(sharp > 0, inverse, rest)

    def total(values):
        return jnp.sum(jnp.sum(values, axis=1, keepdims=True), axis=0, keepdims=True)

    usage = jnp.sum(prob, axis=1, keepdims=True)
    return (total(offset * offset), total(entropy), usage)


def round_bf(values):
    return values.astype(jnp.bfloat16).astype(jnp.float32)


def gelu(x):
    inner = x * (math.sqrt(2.0 / math.pi) + (math.sqrt(2.0 / math.pi) * 0.044715) * (x * x))
    half = 0.5 * x
    return half + half * jnp.tanh(inner)


def image_kernel(
    latent_hbm,
    post_hbm,
    proj_hbm,
    gain_ref,
    label_ref,
    block_ref,
    unit_ref,
    inv_ref,
    latent_ref,
    post_ref,
    proj_ref,
    sems,
):
    fetch_latent = pltpu.make_async_copy(latent_hbm, latent_ref, sems.at[0])
    fetch_post = pltpu.make_async_copy(post_hbm, post_ref, sems.at[1])
    fetch_proj = pltpu.make_async_copy(proj_hbm, proj_ref, sems.at[2])
    fetch_latent.start()
    fetch_post.start()
    fetch_proj.start()
    fetch_latent.wait()
    latent = latent_ref[...]
    bit_count, token_count = latent.shape
    image_count, feat_width = unit_ref.shape
    patch = token_count // image_count

    commit, entropy, usage = code_sums(latent)
    lane = lax.broadcasted_iota(jnp.int32, (bit_count, SIDE), 1)
    bit = lax.broadcasted_iota(jnp.int32, (bit_count, SIDE), 0)
    first = round_bf(usage)
    second = round_bf(usage - first)
    third = usage - first - second
    spread = jnp.where(lane == bit, first, 0.0)
    spread = jnp.where(lane == bit + 32, second, spread)
    spread = jnp.where(lane == bit + 64, third, spread)
    side = jnp.sum(spread, axis=0, keepdims=True)
    place = lax.broadcasted_iota(jnp.int32, (1, SIDE), 1)
    for at, value in ((BITS, commit), (BITS + 1, entropy)):
        first = round_bf(value)
        second = round_bf(value - first)
        third = value - first - second
        side = jnp.where(place == at, first, side)
        side = jnp.where(place == at + 32, second, side)
        side = jnp.where(place == at + 64, third, side)
    sides = []
    for i in range(image_count):
        label = label_ref[i]
        high = (label // 32).astype(jnp.float32)
        low = (label % 32).astype(jnp.float32)
        own = side if i == 0 else jnp.zeros_like(side)
        own = jnp.where(place == SIDE - 2, high, own)
        sides.append(jnp.where(place == SIDE - 1, low, own))
    codes = jnp.where(latent > 0, 1.0, -1.0)
    codes = jnp.transpose(codes, (1, 0)).astype(jnp.bfloat16)
    fetch_post.wait()
    post = post_ref[...]
    fetch_proj.wait()
    proj = proj_ref[...]
    sums = []
    for first in range(0, token_count, CHUNK):
        pre_act = jnp.dot(codes[first : first + CHUNK], post, preferred_element_type=jnp.float32)
        hidden = gelu(pre_act).astype(jnp.bfloat16)
        projected = jnp.dot(hidden, proj, preferred_element_type=jnp.float32)
        square = jnp.sum(projected * projected, axis=-1, keepdims=True)
        scaled = projected * lax.rsqrt(square * (1.0 / feat_width) + EPS)
        sums.append(jnp.sum(scaled, axis=0, keepdims=True))
    steps = patch // CHUNK
    rows = [functools.reduce(jnp.add, sums[i * steps : (i + 1) * steps]) for i in range(image_count)]
    embeds = jnp.concatenate(rows, axis=0) * gain_ref[...][None, :] * (1.0 / patch)
    inverse = lax.rsqrt(jnp.sum(embeds * embeds, axis=-1, keepdims=True) + EPS)
    unit = embeds * inverse
    unit_ref[...] = unit
    inv_ref[...] = jnp.broadcast_to(inverse, inv_ref.shape)

    block = jnp.concatenate([unit, jnp.concatenate(sides, axis=0)], axis=1)
    block_ref[...] = block.astype(jnp.bfloat16)


def embed_images(latent, w_post, w_proj, gain, labels):
    image_count = labels.shape[0]
    feat_width = w_proj.shape[1]
    vmem = pl.BlockSpec(memory_space=pltpu.VMEM)
    hbm = pl.BlockSpec(memory_space=pl.ANY)
    return pl.pallas_call(
        image_kernel,
        out_shape=(
            jax.ShapeDtypeStruct((image_count, feat_width + SIDE), jnp.bfloat16),
            jax.ShapeDtypeStruct((image_count, feat_width), jnp.float32),
            jax.ShapeDtypeStruct((image_count, 128), jnp.float32),
        ),
        in_specs=[hbm, hbm, hbm, vmem, pl.BlockSpec(memory_space=pltpu.SMEM)],
        out_specs=(vmem, vmem, vmem),
        scratch_shapes=[
            pltpu.VMEM(latent.shape, latent.dtype),
            pltpu.VMEM(w_post.shape, w_post.dtype),
            pltpu.VMEM(w_proj.shape, w_proj.dtype),
            pltpu.SemaphoreType.DMA((3,)),
        ],
        compiler_params=pltpu.CompilerParams(vmem_limit_bytes=56 * 1024 * 1024),
        cost_estimate=pl.CostEstimate(
            flops=220_000_000, bytes_accessed=180_000, transcendentals=110_000
        ),
        name="embed_images",
    )(latent, w_post, w_proj, gain, labels)


def unit_rows(values):
    inverse = lax.rsqrt(jnp.sum(values * values, axis=-1, keepdims=True) + EPS)
    return (values * inverse, inverse)


def tangent(direction, unit, inverse):
    return (direction - unit * jnp.sum(unit * direction, axis=-1, keepdims=True)) * inverse


def text_kernel(text_ref, block_ref, unit_ref, inv_ref):
    unit, inverse = unit_rows(text_ref[...].astype(jnp.float32))
    block_ref[...] = jnp.broadcast_to(unit.astype(jnp.bfloat16)[None], block_ref.shape)
    unit_ref[...] = unit
    inv_ref[...] = jnp.broadcast_to(inverse, inv_ref.shape)


def text_blocks(text_embed, copies):
    rows = text_embed.shape[0]
    vmem = pl.BlockSpec(memory_space=pltpu.VMEM)
    return pl.pallas_call(
        text_kernel,
        out_shape=(
            jax.ShapeDtypeStruct((copies,) + text_embed.shape, jnp.bfloat16),
            jax.ShapeDtypeStruct(text_embed.shape, jnp.float32),
            jax.ShapeDtypeStruct((rows, 128), jnp.float32),
        ),
        in_specs=[vmem],
        out_specs=(vmem, vmem, vmem),
        name="text_blocks",
    )(text_embed)


def finish_kernel(total_tokens, parts_ref, unit_ref, inv_ref, scale_ref, grad_ref, scalar_ref):
    feat_width = unit_ref.shape[-1]
    total = parts_ref[0]
    for member in range(1, parts_ref.shape[0]):
        total = total + parts_ref[member]
    direction = scale_ref[0] * total[:, :feat_width]
    grad_ref[...] = tangent(direction, unit_ref[...], inv_ref[...][:, :1])
    side = total[:1, feat_width:]
    means = side[:, :32] + side[:, 32:64] + side[:, 64:96]
    means = means * (1.0 / total_tokens)
    place = lax.broadcasted_iota(jnp.int32, means.shape, 1)
    usage = jnp.where(place < BITS, means, 0.5)
    spread = -(usage * jnp.log(usage) + (1.0 - usage) * jnp.log(1.0 - usage))
    scalar_ref[0] = jnp.sum(jnp.where(place == BITS, means, 0.0))
    scalar_ref[1] = jnp.sum(jnp.where(place == BITS + 1, means, 0.0))
    scalar_ref[2] = jnp.sum(jnp.where(place < BITS, spread, 0.0))


def finish_text(parts, text_unit, text_inv, logit_scale, total_tokens):
    vmem = pl.BlockSpec(memory_space=pltpu.VMEM)
    smem = pl.BlockSpec(memory_space=pltpu.SMEM)
    return pl.pallas_call(
        functools.partial(finish_kernel, total_tokens),
        out_shape=(
            jax.ShapeDtypeStruct(text_unit.shape, jnp.float32),
            jax.ShapeDtypeStruct((3,), jnp.float32),
        ),
        in_specs=[vmem, vmem, vmem, smem],
        out_specs=(vmem, smem),
        name="finish_text",
    )(parts, text_unit, text_inv, logit_scale)


def swap_cores(block):
    return lax.ppermute(block, "core", [(0, 1), (1, 0)])


def along_x(block, distance, count):
    return lax.ppermute(block, "x", [(i, (i + distance) % count) for i in range(count)])


def group_ids(sizes, axes, pair_count):
    count = math.prod(sizes[axis] for axis in axes)
    member = jnp.arange(count * pair_count, dtype=jnp.int32) // pair_count
    place = {axis: lax.axis_index(axis) for axis in ROW_AXES + BLK_AXES}
    for axis in reversed(axes):
        place[axis] = member % sizes[axis]
        member = member // sizes[axis]
    device = jnp.int32(0)
    for axis in ROW_AXES + BLK_AXES:
        device = device * sizes[axis] + place[axis]
    return device * pair_count + jnp.arange(count * pair_count, dtype=jnp.int32) % pair_count


def body(sizes, latent, w_post, w_proj, gain, text_embed, labels, logit_scale, logit_bias):
    pair_count, feat_width = text_embed.shape
    n_x = sizes["x"]
    n_text = math.prod(sizes[axis] for axis in TEXT_AXES)
    text_count = n_text * pair_count
    chip_count = 2 * pair_count
    total_tokens = latent.shape[1] * math.prod(sizes.values())
    scale_value = logit_scale[0]
    bias_value = logit_bias[0]

    text_block, text_unit, text_inv = text_blocks(text_embed, n_text)
    group_text = lax.all_to_all(text_block, TEXT_AXES, 0, 0)
    group_text = group_text.reshape(text_count, feat_width)

    image_block, image_unit, image_inv = embed_images(latent, w_post, w_proj, gain, labels)
    chip_block = jnp.concatenate([image_block, swap_cores(image_block)], axis=0)
    moved = [along_x(chip_block, distance, n_x) for distance in range(1, n_x)]
    group_block = jnp.concatenate([chip_block] + moved, axis=0)
    group_image = group_block[:, :feat_width]
    group_side = group_block[:, feat_width:].astype(jnp.float32)
    group_labels = (group_side[:, SIDE - 2] * 32.0 + group_side[:, SIDE - 1]).astype(jnp.int32)
    group_sums = jnp.sum(group_side, axis=0, keepdims=True)

    text_ids = group_ids(sizes, TEXT_AXES, pair_count)
    products = jnp.dot(group_image, group_text.T, preferred_element_type=jnp.float32)
    pair_sign = jnp.where(
        group_labels[:, None] == text_ids[None, :], jnp.float32(1.0), jnp.float32(-1.0)
    )
    margin = pair_sign * (scale_value * products + bias_value)
    grad_bf = (-pair_sign * jax.nn.sigmoid(-margin)).astype(jnp.bfloat16)
    text_part = jnp.dot(grad_bf.T, group_image, preferred_element_type=jnp.float32)
    text_part = jnp.concatenate(
        [text_part, jnp.broadcast_to(group_sums, (text_count, SIDE))], axis=1
    )
    text_part = text_part.reshape(n_text, pair_count, feat_width + SIDE)
    text_part = lax.all_to_all(text_part, TEXT_AXES, 0, 0)

    image_part = jnp.dot(grad_bf, group_text, preferred_element_type=jnp.float32)
    chip_part = image_part[:chip_count]
    for distance in range(1, n_x):
        rows = image_part[distance * chip_count : (distance + 1) * chip_count]
        chip_part = chip_part + along_x(rows, -distance, n_x)
    image_dir = scale_value * (chip_part[:pair_count] + swap_cores(chip_part[pair_count:]))
    grad_image = tangent(image_dir, image_unit, image_inv[:, :1])
    grad_text, scalars = finish_text(text_part, text_unit, text_inv, logit_scale, total_tokens)
    return (grad_image, grad_text, scalars)


def solution(mesh):
    sizes = {"x": 4, "y_lo": 2, "core": 2, "z": 8, "y_hi": 4}
    names = ROW_AXES + BLK_AXES
    fine = Mesh(mesh.devices.reshape([sizes[axis] for axis in names]), names)
    return jax.shard_map(
        functools.partial(body, sizes),
        mesh=fine,
        in_specs=(P(None, names), P(), P(), P(), P(names, None), P(names), P(), P()),
        out_specs=(P(names, None), P(names, None), P()),
        check_vma=False,
    )
```

```python
import functools
import math

import jax
import jax.numpy as jnp
from jax import lax
from jax.experimental import pallas as pl
from jax.experimental.pallas import tpu as pltpu
from jax.sharding import Mesh
from jax.sharding import PartitionSpec as P

EPS = 1e-06
SHARPNESS = 4.0
BITS = 28
SIDE = 128
CHUNK = 256

ROW_AXES = ("x", "y_lo", "core")
BLK_AXES = ("z", "y_hi")
TEXT_AXES = ("z", "y_hi", "y_lo")
IMAGE_AXES = ("x", "core")


def code_sums(latent):
    bit_count = latent.shape[0]
    length = jnp.sqrt(jnp.sum(latent * latent, axis=0, keepdims=True))
    unit_code = latent / length
    root = 1.0 / math.sqrt(bit_count)
    offset = unit_code - jnp.where(latent > 0, root, -root)
    sharp = SHARPNESS * math.sqrt(bit_count) * unit_code
    size = jnp.abs(sharp)
    small = jnp.exp(-size)
    inverse = 1.0 / (1.0 + small)
    rest = small * inverse
    entropy = jnp.log1p(small) + size * rest
    prob = jnp.where(sharp > 0, inverse, rest)

    def total(values):
        return jnp.sum(jnp.sum(values, axis=1, keepdims=True), axis=0, keepdims=True)

    usage = jnp.sum(prob, axis=1, keepdims=True)
    return (total(offset * offset), total(entropy), usage)


def round_bf(values):
    return values.astype(jnp.bfloat16).astype(jnp.float32)


def gelu(x):
    inner = x * (math.sqrt(2.0 / math.pi) + (math.sqrt(2.0 / math.pi) * 0.044715) * (x * x))
    half = 0.5 * x
    return half + half * jnp.tanh(inner)


def image_kernel(
    copies,
    latent_hbm,
    post_hbm,
    proj_hbm,
    gain_ref,
    label_ref,
    block_ref,
    unit_ref,
    inv_ref,
    latent_ref,
    post_ref,
    proj_ref,
    sems,
):
    fetch_latent = pltpu.make_async_copy(latent_hbm, latent_ref, sems.at[0])
    fetch_post = pltpu.make_async_copy(post_hbm, post_ref, sems.at[1])
    fetch_proj = pltpu.make_async_copy(proj_hbm, proj_ref, sems.at[2])
    fetch_latent.start()
    fetch_post.start()
    fetch_proj.start()
    fetch_latent.wait()
    latent = latent_ref[...]
    bit_count, token_count = latent.shape
    image_count, feat_width = unit_ref.shape
    patch = token_count // image_count

    commit, entropy, usage = code_sums(latent)
    lane = lax.broadcasted_iota(jnp.int32, (bit_count, SIDE), 1)
    bit = lax.broadcasted_iota(jnp.int32, (bit_count, SIDE), 0)
    first = round_bf(usage)
    second = round_bf(usage - first)
    third = usage - first - second
    spread = jnp.where(lane == bit, first, 0.0)
    spread = jnp.where(lane == bit + 32, second, spread)
    spread = jnp.where(lane == bit + 64, third, spread)
    side = jnp.sum(spread, axis=0, keepdims=True)
    place = lax.broadcasted_iota(jnp.int32, (1, SIDE), 1)
    for at, value in ((BITS, commit), (BITS + 1, entropy)):
        first = round_bf(value)
        second = round_bf(value - first)
        third = value - first - second
        side = jnp.where(place == at, first, side)
        side = jnp.where(place == at + 32, second, side)
        side = jnp.where(place == at + 64, third, side)
    sides = []
    for i in range(image_count):
        label = label_ref[i]
        high = (label // 32).astype(jnp.float32)
        low = (label % 32).astype(jnp.float32)
        own = side if i == 0 else jnp.zeros_like(side)
        own = jnp.where(place == SIDE - 2, high, own)
        sides.append(jnp.where(place == SIDE - 1, low, own))
    codes = jnp.where(latent > 0, 1.0, -1.0)
    codes = jnp.transpose(codes, (1, 0)).astype(jnp.bfloat16)
    fetch_post.wait()
    post = post_ref[...]
    fetch_proj.wait()
    proj = proj_ref[...]
    sums = []
    for first in range(0, token_count, CHUNK):
        pre_act = jnp.dot(codes[first : first + CHUNK], post, preferred_element_type=jnp.float32)
        hidden = gelu(pre_act).astype(jnp.bfloat16)
        projected = jnp.dot(hidden, proj, preferred_element_type=jnp.float32)
        square = jnp.sum(projected * projected, axis=-1, keepdims=True)
        scaled = projected * lax.rsqrt(square * (1.0 / feat_width) + EPS)
        sums.append(jnp.sum(scaled, axis=0, keepdims=True))
    steps = patch // CHUNK
    rows = [functools.reduce(jnp.add, sums[i * steps : (i + 1) * steps]) for i in range(image_count)]
    embeds = jnp.concatenate(rows, axis=0) * gain_ref[...][None, :] * (1.0 / patch)
    inverse = lax.rsqrt(jnp.sum(embeds * embeds, axis=-1, keepdims=True) + EPS)
    unit = embeds * inverse
    unit_ref[...] = unit
    inv_ref[...] = jnp.broadcast_to(inverse, inv_ref.shape)

    block = jnp.concatenate([unit, jnp.concatenate(sides, axis=0)], axis=1)
    block = block.astype(jnp.bfloat16)
    for member in range(copies):
        block_ref[member] = block


def embed_images(latent, w_post, w_proj, gain, labels, copies):
    image_count = labels.shape[0]
    feat_width = w_proj.shape[1]
    vmem = pl.BlockSpec(memory_space=pltpu.VMEM)
    hbm = pl.BlockSpec(memory_space=pl.ANY)
    return pl.pallas_call(
        functools.partial(image_kernel, copies),
        out_shape=(
            jax.ShapeDtypeStruct((copies, image_count, feat_width + SIDE), jnp.bfloat16),
            jax.ShapeDtypeStruct((image_count, feat_width), jnp.float32),
            jax.ShapeDtypeStruct((image_count, 128), jnp.float32),
        ),
        in_specs=[hbm, hbm, hbm, vmem, pl.BlockSpec(memory_space=pltpu.SMEM)],
        out_specs=(vmem, vmem, vmem),
        scratch_shapes=[
            pltpu.VMEM(latent.shape, latent.dtype),
            pltpu.VMEM(w_post.shape, w_post.dtype),
            pltpu.VMEM(w_proj.shape, w_proj.dtype),
            pltpu.SemaphoreType.DMA((3,)),
        ],
        compiler_params=pltpu.CompilerParams(vmem_limit_bytes=56 * 1024 * 1024),
        cost_estimate=pl.CostEstimate(
            flops=2_200_000_000, bytes_accessed=1_800_000, transcendentals=1_100_000
        ),
        name="embed_images",
    )(latent, w_post, w_proj, gain, labels)


def unit_rows(values):
    inverse = lax.rsqrt(jnp.sum(values * values, axis=-1, keepdims=True) + EPS)
    return (values * inverse, inverse)


def tangent(direction, unit, inverse):
    return (direction - unit * jnp.sum(unit * direction, axis=-1, keepdims=True)) * inverse


def text_kernel(text_ref, block_ref, unit_ref, inv_ref):
    unit, inverse = unit_rows(text_ref[...].astype(jnp.float32))
    block_ref[...] = jnp.broadcast_to(unit.astype(jnp.bfloat16)[None], block_ref.shape)
    unit_ref[...] = unit
    inv_ref[...] = jnp.broadcast_to(inverse, inv_ref.shape)


def text_blocks(text_embed, copies):
    rows = text_embed.shape[0]
    vmem = pl.BlockSpec(memory_space=pltpu.VMEM)
    return pl.pallas_call(
        text_kernel,
        out_shape=(
            jax.ShapeDtypeStruct((copies,) + text_embed.shape, jnp.bfloat16),
            jax.ShapeDtypeStruct(text_embed.shape, jnp.float32),
            jax.ShapeDtypeStruct((rows, 128), jnp.float32),
        ),
        in_specs=[vmem],
        out_specs=(vmem, vmem, vmem),
        name="text_blocks",
    )(text_embed)


def finish_kernel(total_tokens, parts_ref, unit_ref, inv_ref, scale_ref, grad_ref, scalar_ref):
    feat_width = unit_ref.shape[-1]
    total = parts_ref[0]
    for member in range(1, parts_ref.shape[0]):
        total = total + parts_ref[member]
    direction = scale_ref[0] * total[:, :feat_width]
    grad_ref[...] = tangent(direction, unit_ref[...], inv_ref[...][:, :1])
    side = total[:1, feat_width:]
    means = side[:, :32] + side[:, 32:64] + side[:, 64:96]
    means = means * (1.0 / total_tokens)
    place = lax.broadcasted_iota(jnp.int32, means.shape, 1)
    usage = jnp.where(place < BITS, means, 0.5)
    spread = -(usage * jnp.log(usage) + (1.0 - usage) * jnp.log(1.0 - usage))
    scalar_ref[0] = jnp.sum(jnp.where(place == BITS, means, 0.0))
    scalar_ref[1] = jnp.sum(jnp.where(place == BITS + 1, means, 0.0))
    scalar_ref[2] = jnp.sum(jnp.where(place < BITS, spread, 0.0))


def finish_text(parts, text_unit, text_inv, logit_scale, total_tokens):
    vmem = pl.BlockSpec(memory_space=pltpu.VMEM)
    smem = pl.BlockSpec(memory_space=pltpu.SMEM)
    return pl.pallas_call(
        functools.partial(finish_kernel, total_tokens),
        out_shape=(
            jax.ShapeDtypeStruct(text_unit.shape, jnp.float32),
            jax.ShapeDtypeStruct((3,), jnp.float32),
        ),
        in_specs=[vmem, vmem, vmem, smem],
        out_specs=(vmem, smem),
        name="finish_text",
    )(parts, text_unit, text_inv, logit_scale)


def halve(rows, axis, size, bit):
    first, last = jnp.split(rows, 2, axis=0)
    high = lax.axis_index(axis) & bit != 0
    kept = jnp.where(high, last, first)
    sent = jnp.where(high, first, last)
    return kept + lax.ppermute(sent, axis, [(i, i ^ bit) for i in range(size)])


def group_ids(sizes, axes, pair_count):
    count = math.prod(sizes[axis] for axis in axes)
    member = jnp.arange(count * pair_count, dtype=jnp.int32) // pair_count
    place = {axis: lax.axis_index(axis) for axis in ROW_AXES + BLK_AXES}
    for axis in reversed(axes):
        place[axis] = member % sizes[axis]
        member = member // sizes[axis]
    device = jnp.int32(0)
    for axis in ROW_AXES + BLK_AXES:
        device = device * sizes[axis] + place[axis]
    return device * pair_count + jnp.arange(count * pair_count, dtype=jnp.int32) % pair_count


def body(sizes, latent, w_post, w_proj, gain, text_embed, labels, logit_scale, logit_bias):
    pair_count, feat_width = text_embed.shape
    n_image = math.prod(sizes[axis] for axis in IMAGE_AXES)
    n_text = math.prod(sizes[axis] for axis in TEXT_AXES)
    text_count = n_text * pair_count
    total_tokens = latent.shape[1] * math.prod(sizes.values())
    scale_value = logit_scale[0]
    bias_value = logit_bias[0]

    text_block, text_unit, text_inv = text_blocks(text_embed, n_text)
    group_text = lax.all_to_all(text_block, TEXT_AXES, 0, 0)

    image_block, image_unit, image_inv = embed_images(
        latent, w_post, w_proj, gain, labels, n_image
    )
    image_block, group_text = lax.optimization_barrier((image_block, group_text))
    group_text = group_text.reshape(text_count, feat_width)
    group_block = lax.all_to_all(image_block, IMAGE_AXES, 0, 0)
    group_block = group_block.reshape(n_image * pair_count, feat_width + SIDE)
    group_image = group_block[:, :feat_width]
    group_side = group_block[:, feat_width:].astype(jnp.float32)
    group_labels = (group_side[:, SIDE - 2] * 32.0 + group_side[:, SIDE - 1]).astype(jnp.int32)
    group_sums = jnp.sum(group_side, axis=0, keepdims=True)

    text_ids = group_ids(sizes, TEXT_AXES, pair_count)
    products = jnp.dot(group_image, group_text.T, preferred_element_type=jnp.float32)
    pair_sign = jnp.where(
        group_labels[:, None] == text_ids[None, :], jnp.float32(1.0), jnp.float32(-1.0)
    )
    margin = pair_sign * (scale_value * products + bias_value)
    grad_bf = (-pair_sign * jax.nn.sigmoid(-margin)).astype(jnp.bfloat16)
    text_part = jnp.dot(grad_bf.T, group_image, preferred_element_type=jnp.float32)
    text_part = jnp.concatenate(
        [text_part, jnp.broadcast_to(group_sums, (text_count, SIDE))], axis=1
    )
    text_part = text_part.reshape(n_text, pair_count, feat_width + SIDE)
    text_part = lax.all_to_all(text_part, TEXT_AXES, 0, 0)

    image_part = jnp.dot(grad_bf, group_text, preferred_element_type=jnp.float32)
    image_part = halve(image_part, "x", sizes["x"], 2)
    image_part = halve(image_part, "x", sizes["x"], 1)
    image_dir = scale_value * halve(image_part, "core", sizes["core"], 1)
    grad_image = tangent(image_dir, image_unit, image_inv[:, :1])
    grad_text, scalars = finish_text(text_part, text_unit, text_inv, logit_scale, total_tokens)
    return (grad_image, grad_text, scalars)


def solution(mesh):
    sizes = {"x": 4, "y_lo": 2, "core": 2, "z": 8, "y_hi": 4}
    names = ROW_AXES + BLK_AXES
    fine = Mesh(mesh.devices.reshape([sizes[axis] for axis in names]), names)
    return jax.shard_map(
        functools.partial(body, sizes),
        mesh=fine,
        in_specs=(P(None, names), P(), P(), P(), P(names, None), P(names), P(), P()),
        out_specs=(P(names, None), P(names, None), P()),
        check_vma=False,
    )
```

```python
import functools
import math

import jax
import jax.numpy as jnp
from jax import lax
from jax.experimental import pallas as pl
from jax.experimental.pallas import tpu as pltpu
from jax.sharding import Mesh
from jax.sharding import PartitionSpec as P

EPS = 1e-06
SHARPNESS = 4.0
BITS = 28
SIDE = 128
CHUNK = 256

ROW_AXES = ("x", "y_lo", "core")
BLK_AXES = ("z", "y_hi")
TEXT_AXES = ("y_hi", "y_lo", "core")
IMAGE_AXES = ("x", "z")


def code_sums(latent):
    bit_count = latent.shape[0]
    length = jnp.sqrt(jnp.sum(latent * latent, axis=0, keepdims=True))
    unit_code = latent / length
    root = 1.0 / math.sqrt(bit_count)
    offset = unit_code - jnp.where(latent > 0, root, -root)
    sharp = SHARPNESS * math.sqrt(bit_count) * unit_code
    size = jnp.abs(sharp)
    small = jnp.exp(-size)
    inverse = 1.0 / (1.0 + small)
    rest = small * inverse
    entropy = jnp.log1p(small) + size * rest
    prob = jnp.where(sharp > 0, inverse, rest)

    def total(values):
        return jnp.sum(jnp.sum(values, axis=1, keepdims=True), axis=0, keepdims=True)

    usage = jnp.sum(prob, axis=1, keepdims=True)
    return (total(offset * offset), total(entropy), usage)


def round_bf(values):
    return values.astype(jnp.bfloat16).astype(jnp.float32)


def gelu(x):
    inner = x * (math.sqrt(2.0 / math.pi) + (math.sqrt(2.0 / math.pi) * 0.044715) * (x * x))
    half = 0.5 * x
    return half + half * jnp.tanh(inner)


def image_kernel(
    copies,
    latent_hbm,
    post_hbm,
    proj_hbm,
    gain_ref,
    label_ref,
    block_ref,
    unit_ref,
    inv_ref,
    latent_ref,
    post_ref,
    proj_ref,
    sems,
):
    fetch_latent = pltpu.make_async_copy(latent_hbm, latent_ref, sems.at[0])
    fetch_post = pltpu.make_async_copy(post_hbm, post_ref, sems.at[1])
    fetch_proj = pltpu.make_async_copy(proj_hbm, proj_ref, sems.at[2])
    fetch_latent.start()
    fetch_post.start()
    fetch_proj.start()
    fetch_latent.wait()
    latent = latent_ref[...]
    bit_count, token_count = latent.shape
    image_count, feat_width = unit_ref.shape
    patch = token_count // image_count

    commit, entropy, usage = code_sums(latent)
    lane = lax.broadcasted_iota(jnp.int32, (bit_count, SIDE), 1)
    bit = lax.broadcasted_iota(jnp.int32, (bit_count, SIDE), 0)
    first = round_bf(usage)
    second = round_bf(usage - first)
    third = usage - first - second
    spread = jnp.where(lane == bit, first, 0.0)
    spread = jnp.where(lane == bit + 32, second, spread)
    spread = jnp.where(lane == bit + 64, third, spread)
    side = jnp.sum(spread, axis=0, keepdims=True)
    place = lax.broadcasted_iota(jnp.int32, (1, SIDE), 1)
    for at, value in ((BITS, commit), (BITS + 1, entropy)):
        first = round_bf(value)
        second = round_bf(value - first)
        third = value - first - second
        side = jnp.where(place == at, first, side)
        side = jnp.where(place == at + 32, second, side)
        side = jnp.where(place == at + 64, third, side)
    sides = []
    for i in range(image_count):
        label = label_ref[i]
        high = (label // 32).astype(jnp.float32)
        low = (label % 32).astype(jnp.float32)
        own = side if i == 0 else jnp.zeros_like(side)
        own = jnp.where(place == SIDE - 2, high, own)
        sides.append(jnp.where(place == SIDE - 1, low, own))
    codes = jnp.where(latent > 0, 1.0, -1.0)
    codes = jnp.transpose(codes, (1, 0)).astype(jnp.bfloat16)
    fetch_post.wait()
    post = post_ref[...]
    fetch_proj.wait()
    proj = proj_ref[...]
    sums = []
    for first in range(0, token_count, CHUNK):
        pre_act = jnp.dot(codes[first : first + CHUNK], post, preferred_element_type=jnp.float32)
        hidden = gelu(pre_act).astype(jnp.bfloat16)
        projected = jnp.dot(hidden, proj, preferred_element_type=jnp.float32)
        square = jnp.sum(projected * projected, axis=-1, keepdims=True)
        scaled = projected * lax.rsqrt(square * (1.0 / feat_width) + EPS)
        sums.append(jnp.sum(scaled, axis=0, keepdims=True))
    steps = patch // CHUNK
    rows = [functools.reduce(jnp.add, sums[i * steps : (i + 1) * steps]) for i in range(image_count)]
    embeds = jnp.concatenate(rows, axis=0) * gain_ref[...][None, :] * (1.0 / patch)
    inverse = lax.rsqrt(jnp.sum(embeds * embeds, axis=-1, keepdims=True) + EPS)
    unit = embeds * inverse
    unit_ref[...] = unit
    inv_ref[...] = jnp.broadcast_to(inverse, inv_ref.shape)

    block = jnp.concatenate([unit, jnp.concatenate(sides, axis=0)], axis=1)
    block = block.astype(jnp.bfloat16)
    for member in range(copies):
        block_ref[member] = block


def embed_images(latent, w_post, w_proj, gain, labels, copies):
    image_count = labels.shape[0]
    feat_width = w_proj.shape[1]
    vmem = pl.BlockSpec(memory_space=pltpu.VMEM)
    hbm = pl.BlockSpec(memory_space=pl.ANY)
    return pl.pallas_call(
        functools.partial(image_kernel, copies),
        out_shape=(
            jax.ShapeDtypeStruct((copies, image_count, feat_width + SIDE), jnp.bfloat16),
            jax.ShapeDtypeStruct((image_count, feat_width), jnp.float32),
            jax.ShapeDtypeStruct((image_count, 128), jnp.float32),
        ),
        in_specs=[hbm, hbm, hbm, vmem, pl.BlockSpec(memory_space=pltpu.SMEM)],
        out_specs=(vmem, vmem, vmem),
        scratch_shapes=[
            pltpu.VMEM(latent.shape, latent.dtype),
            pltpu.VMEM(w_post.shape, w_post.dtype),
            pltpu.VMEM(w_proj.shape, w_proj.dtype),
            pltpu.SemaphoreType.DMA((3,)),
        ],
        compiler_params=pltpu.CompilerParams(vmem_limit_bytes=56 * 1024 * 1024),
        cost_estimate=pl.CostEstimate(
            flops=2_200_000_000, bytes_accessed=1_800_000, transcendentals=1_100_000
        ),
        name="embed_images",
    )(latent, w_post, w_proj, gain, labels)


def unit_rows(values):
    inverse = lax.rsqrt(jnp.sum(values * values, axis=-1, keepdims=True) + EPS)
    return (values * inverse, inverse)


def tangent(direction, unit, inverse):
    return (direction - unit * jnp.sum(unit * direction, axis=-1, keepdims=True)) * inverse


def text_kernel(text_ref, block_ref, unit_ref, inv_ref):
    unit, inverse = unit_rows(text_ref[...].astype(jnp.float32))
    block_ref[...] = jnp.broadcast_to(unit.astype(jnp.bfloat16)[None], block_ref.shape)
    unit_ref[...] = unit
    inv_ref[...] = jnp.broadcast_to(inverse, inv_ref.shape)


def text_blocks(text_embed, copies):
    rows = text_embed.shape[0]
    vmem = pl.BlockSpec(memory_space=pltpu.VMEM)
    return pl.pallas_call(
        text_kernel,
        out_shape=(
            jax.ShapeDtypeStruct((copies,) + text_embed.shape, jnp.bfloat16),
            jax.ShapeDtypeStruct(text_embed.shape, jnp.float32),
            jax.ShapeDtypeStruct((rows, 128), jnp.float32),
        ),
        in_specs=[vmem],
        out_specs=(vmem, vmem, vmem),
        name="text_blocks",
    )(text_embed)


def finish_kernel(total_tokens, parts_ref, unit_ref, inv_ref, scale_ref, grad_ref, scalar_ref):
    feat_width = unit_ref.shape[-1]
    total = parts_ref[0]
    for member in range(1, parts_ref.shape[0]):
        total = total + parts_ref[member]
    direction = scale_ref[0] * total[:, :feat_width]
    grad_ref[...] = tangent(direction, unit_ref[...], inv_ref[...][:, :1])
    side = total[:1, feat_width:]
    means = side[:, :32] + side[:, 32:64] + side[:, 64:96]
    means = means * (1.0 / total_tokens)
    place = lax.broadcasted_iota(jnp.int32, means.shape, 1)
    usage = jnp.where(place < BITS, means, 0.5)
    spread = -(usage * jnp.log(usage) + (1.0 - usage) * jnp.log(1.0 - usage))
    scalar_ref[0] = jnp.sum(jnp.where(place == BITS, means, 0.0))
    scalar_ref[1] = jnp.sum(jnp.where(place == BITS + 1, means, 0.0))
    scalar_ref[2] = jnp.sum(jnp.where(place < BITS, spread, 0.0))


def finish_text(parts, text_unit, text_inv, logit_scale, total_tokens):
    vmem = pl.BlockSpec(memory_space=pltpu.VMEM)
    smem = pl.BlockSpec(memory_space=pltpu.SMEM)
    return pl.pallas_call(
        functools.partial(finish_kernel, total_tokens),
        out_shape=(
            jax.ShapeDtypeStruct(text_unit.shape, jnp.float32),
            jax.ShapeDtypeStruct((3,), jnp.float32),
        ),
        in_specs=[vmem, vmem, vmem, smem],
        out_specs=(vmem, smem),
        name="finish_text",
    )(parts, text_unit, text_inv, logit_scale)


def group_ids(sizes, axes, pair_count):
    count = math.prod(sizes[axis] for axis in axes)
    member = jnp.arange(count * pair_count, dtype=jnp.int32) // pair_count
    place = {axis: lax.axis_index(axis) for axis in ROW_AXES + BLK_AXES}
    for axis in reversed(axes):
        place[axis] = member % sizes[axis]
        member = member // sizes[axis]
    device = jnp.int32(0)
    for axis in ROW_AXES + BLK_AXES:
        device = device * sizes[axis] + place[axis]
    return device * pair_count + jnp.arange(count * pair_count, dtype=jnp.int32) % pair_count


def body(sizes, latent, w_post, w_proj, gain, text_embed, labels, logit_scale, logit_bias):
    pair_count, feat_width = text_embed.shape
    n_image = math.prod(sizes[axis] for axis in IMAGE_AXES)
    n_text = math.prod(sizes[axis] for axis in TEXT_AXES)
    text_count = n_text * pair_count
    total_tokens = latent.shape[1] * math.prod(sizes.values())
    scale_value = logit_scale[0]
    bias_value = logit_bias[0]

    text_block, text_unit, text_inv = text_blocks(text_embed, n_text)
    group_text = lax.all_to_all(text_block, TEXT_AXES, 0, 0)

    image_block, image_unit, image_inv = embed_images(
        latent, w_post, w_proj, gain, labels, n_image
    )
    image_block, group_text = lax.optimization_barrier((image_block, group_text))
    group_text = group_text.reshape(text_count, feat_width)
    group_block = lax.all_to_all(image_block, IMAGE_AXES, 0, 0)
    group_block = group_block.reshape(n_image * pair_count, feat_width + SIDE)
    group_image = group_block[:, :feat_width]
    group_side = group_block[:, feat_width:].astype(jnp.float32)
    group_labels = (group_side[:, SIDE - 2] * 32.0 + group_side[:, SIDE - 1]).astype(jnp.int32)
    group_sums = jnp.sum(group_side, axis=0, keepdims=True)

    text_ids = group_ids(sizes, TEXT_AXES, pair_count)
    products = jnp.dot(group_image, group_text.T, preferred_element_type=jnp.float32)
    pair_sign = jnp.where(
        group_labels[:, None] == text_ids[None, :], jnp.float32(1.0), jnp.float32(-1.0)
    )
    margin = pair_sign * (scale_value * products + bias_value)
    grad_bf = (-pair_sign * jax.nn.sigmoid(-margin)).astype(jnp.bfloat16)
    text_part = jnp.dot(grad_bf.T, group_image, preferred_element_type=jnp.float32)
    text_part = jnp.concatenate(
        [text_part, jnp.broadcast_to(group_sums, (text_count, SIDE))], axis=1
    )
    text_part = text_part.reshape(n_text, pair_count, feat_width + SIDE)
    text_part = lax.all_to_all(text_part, TEXT_AXES, 0, 0)

    image_part = jnp.dot(grad_bf, group_text, preferred_element_type=jnp.float32)
    image_part = image_part.reshape(n_image, pair_count, feat_width)
    image_part, text_part = lax.optimization_barrier((image_part, text_part))
    image_part = lax.all_to_all(image_part, IMAGE_AXES, 0, 0)
    image_dir = scale_value * jnp.sum(image_part, axis=0)
    grad_image = tangent(image_dir, image_unit, image_inv[:, :1])
    grad_text, scalars = finish_text(text_part, text_unit, text_inv, logit_scale, total_tokens)
    return (grad_image, grad_text, scalars)


def solution(mesh):
    sizes = {"x": 4, "y_lo": 2, "core": 2, "z": 8, "y_hi": 4}
    names = ROW_AXES + BLK_AXES
    fine = Mesh(mesh.devices.reshape([sizes[axis] for axis in names]), names)
    return jax.shard_map(
        functools.partial(body, sizes),
        mesh=fine,
        in_specs=(P(None, names), P(), P(), P(), P(names, None), P(names), P(), P()),
        out_specs=(P(names, None), P(names, None), P()),
        check_vma=False,
    )
```

```python
import functools
import math

import jax
import jax.numpy as jnp
from jax import lax
from jax.experimental import pallas as pl
from jax.experimental.pallas import tpu as pltpu
from jax.sharding import Mesh
from jax.sharding import PartitionSpec as P

EPS = 1e-06
SHARPNESS = 4.0
BITS = 28
SIDE = 128
CHUNK = 256

ROW_AXES = ("x", "y_lo", "core")
BLK_AXES = ("z", "y_hi")
TEXT_AXES = ("y_hi", "y_lo", "core")
IMAGE_AXES = ("x", "z")


def code_sums(latent):
    bit_count = latent.shape[0]
    length = jnp.sqrt(jnp.sum(latent * latent, axis=0, keepdims=True))
    unit_code = latent / length
    root = 1.0 / math.sqrt(bit_count)
    offset = unit_code - jnp.where(latent > 0, root, -root)
    sharp = SHARPNESS * math.sqrt(bit_count) * unit_code
    size = jnp.abs(sharp)
    small = jnp.exp(-size)
    inverse = 1.0 / (1.0 + small)
    rest = small * inverse
    entropy = jnp.log1p(small) + size * rest
    prob = jnp.where(sharp > 0, inverse, rest)

    def total(values):
        return jnp.sum(jnp.sum(values, axis=1, keepdims=True), axis=0, keepdims=True)

    usage = jnp.sum(prob, axis=1, keepdims=True)
    return (total(offset * offset), total(entropy), usage)


def round_bf(values):
    return values.astype(jnp.bfloat16).astype(jnp.float32)


def gelu(x):
    inner = x * (math.sqrt(2.0 / math.pi) + (math.sqrt(2.0 / math.pi) * 0.044715) * (x * x))
    half = 0.5 * x
    return half + half * jnp.tanh(inner)


def image_kernel(
    copies,
    latent_hbm,
    post_hbm,
    proj_hbm,
    gain_ref,
    label_ref,
    block_ref,
    unit_ref,
    inv_ref,
    latent_ref,
    post_ref,
    proj_ref,
    sems,
):
    fetch_latent = pltpu.make_async_copy(latent_hbm, latent_ref, sems.at[0])
    fetch_post = pltpu.make_async_copy(post_hbm, post_ref, sems.at[1])
    fetch_proj = pltpu.make_async_copy(proj_hbm, proj_ref, sems.at[2])
    fetch_latent.start()
    fetch_post.start()
    fetch_proj.start()
    fetch_latent.wait()
    latent = latent_ref[...]
    bit_count, token_count = latent.shape
    image_count, feat_width = unit_ref.shape
    patch = token_count // image_count

    commit, entropy, usage = code_sums(latent)
    lane = lax.broadcasted_iota(jnp.int32, (bit_count, SIDE), 1)
    bit = lax.broadcasted_iota(jnp.int32, (bit_count, SIDE), 0)
    first = round_bf(usage)
    second = round_bf(usage - first)
    third = usage - first - second
    spread = jnp.where(lane == bit, first, 0.0)
    spread = jnp.where(lane == bit + 32, second, spread)
    spread = jnp.where(lane == bit + 64, third, spread)
    side = jnp.sum(spread, axis=0, keepdims=True)
    place = lax.broadcasted_iota(jnp.int32, (1, SIDE), 1)
    for at, value in ((BITS, commit), (BITS + 1, entropy)):
        first = round_bf(value)
        second = round_bf(value - first)
        third = value - first - second
        side = jnp.where(place == at, first, side)
        side = jnp.where(place == at + 32, second, side)
        side = jnp.where(place == at + 64, third, side)
    sides = []
    for i in range(image_count):
        label = label_ref[i]
        high = (label // 32).astype(jnp.float32)
        low = (label % 32).astype(jnp.float32)
        own = side if i == 0 else jnp.zeros_like(side)
        own = jnp.where(place == SIDE - 2, high, own)
        sides.append(jnp.where(place == SIDE - 1, low, own))
    codes = jnp.where(latent > 0, 1.0, -1.0)
    codes = jnp.transpose(codes, (1, 0)).astype(jnp.bfloat16)
    fetch_post.wait()
    post = post_ref[...]
    fetch_proj.wait()
    proj = proj_ref[...]
    sums = []
    for first in range(0, token_count, CHUNK):
        pre_act = jnp.dot(codes[first : first + CHUNK], post, preferred_element_type=jnp.float32)
        hidden = gelu(pre_act).astype(jnp.bfloat16)
        projected = jnp.dot(hidden, proj, preferred_element_type=jnp.float32)
        square = jnp.sum(projected * projected, axis=-1, keepdims=True)
        scaled = projected * lax.rsqrt(square * (1.0 / feat_width) + EPS)
        sums.append(jnp.sum(scaled, axis=0, keepdims=True))
    steps = patch // CHUNK
    rows = [functools.reduce(jnp.add, sums[i * steps : (i + 1) * steps]) for i in range(image_count)]
    embeds = jnp.concatenate(rows, axis=0) * gain_ref[...][None, :] * (1.0 / patch)
    inverse = lax.rsqrt(jnp.sum(embeds * embeds, axis=-1, keepdims=True) + EPS)
    unit = embeds * inverse
    unit_ref[...] = unit
    inv_ref[...] = jnp.broadcast_to(inverse, inv_ref.shape)

    block = jnp.concatenate([unit, jnp.concatenate(sides, axis=0)], axis=1)
    block = block.astype(jnp.bfloat16)
    for member in range(copies):
        block_ref[member] = block


def embed_images(latent, w_post, w_proj, gain, labels, copies):
    image_count = labels.shape[0]
    feat_width = w_proj.shape[1]
    vmem = pl.BlockSpec(memory_space=pltpu.VMEM)
    hbm = pl.BlockSpec(memory_space=pl.ANY)
    return pl.pallas_call(
        functools.partial(image_kernel, copies),
        out_shape=(
            jax.ShapeDtypeStruct((copies, image_count, feat_width + SIDE), jnp.bfloat16),
            jax.ShapeDtypeStruct((image_count, feat_width), jnp.float32),
            jax.ShapeDtypeStruct((image_count, 128), jnp.float32),
        ),
        in_specs=[hbm, hbm, hbm, vmem, pl.BlockSpec(memory_space=pltpu.SMEM)],
        out_specs=(vmem, vmem, vmem),
        scratch_shapes=[
            pltpu.VMEM(latent.shape, latent.dtype),
            pltpu.VMEM(w_post.shape, w_post.dtype),
            pltpu.VMEM(w_proj.shape, w_proj.dtype),
            pltpu.SemaphoreType.DMA((3,)),
        ],
        compiler_params=pltpu.CompilerParams(vmem_limit_bytes=56 * 1024 * 1024),
        cost_estimate=pl.CostEstimate(
            flops=2_200_000_000, bytes_accessed=1_800_000, transcendentals=1_100_000
        ),
        name="embed_images",
    )(latent, w_post, w_proj, gain, labels)


def unit_rows(values):
    inverse = lax.rsqrt(jnp.sum(values * values, axis=-1, keepdims=True) + EPS)
    return (values * inverse, inverse)


def tangent(direction, unit, inverse):
    return (direction - unit * jnp.sum(unit * direction, axis=-1, keepdims=True)) * inverse


def tile_kernel(block_ref, text_ref, id_ref, scale_ref, bias_ref, text_part_ref, image_part_ref):
    text_members, pair_count, feat_width = text_ref.shape
    image_members = block_ref.shape[0]
    block = [block_ref[member].astype(jnp.float32) for member in range(image_members)]
    block = jnp.concatenate(block, axis=0)
    image = block[:, :feat_width].astype(jnp.bfloat16)
    side = block[:, feat_width:]
    sums = jnp.broadcast_to(jnp.sum(side, axis=0, keepdims=True), (pair_count, SIDE))
    label = side[:, SIDE - 2 : SIDE - 1] * 32.0 + side[:, SIDE - 1 : SIDE]
    text = [text_ref[member].astype(jnp.float32) for member in range(text_members)]
    text, _ = unit_rows(jnp.concatenate(text, axis=0))
    text = text.astype(jnp.bfloat16)

    products = lax.dot_general(
        image, text, (((1,), (1,)), ((), ())), preferred_element_type=jnp.float32
    )
    pair_sign = jnp.where(label == id_ref[...].astype(jnp.float32), 1.0, -1.0)
    margin = pair_sign * (scale_ref[0] * products + bias_ref[0])
    grad = -pair_sign * jax.nn.sigmoid(-margin)
    text_part = jnp.dot(
        jnp.transpose(grad, (1, 0)).astype(jnp.bfloat16), image, preferred_element_type=jnp.float32
    )
    for member in range(text_members):
        rows = text_part[member * pair_count : (member + 1) * pair_count]
        text_part_ref[member] = jnp.concatenate([rows, sums], axis=1)
    image_part = jnp.dot(grad.astype(jnp.bfloat16), text, preferred_element_type=jnp.float32)
    for member in range(image_members):
        image_part_ref[member] = image_part[member * pair_count : (member + 1) * pair_count]


def score_tile(group_block, group_text, text_ids, logit_scale, logit_bias):
    image_members, pair_count, _ = group_block.shape
    text_members, _, feat_width = group_text.shape
    vmem = pl.BlockSpec(memory_space=pltpu.VMEM)
    smem = pl.BlockSpec(memory_space=pltpu.SMEM)
    return pl.pallas_call(
        tile_kernel,
        out_shape=(
            jax.ShapeDtypeStruct((text_members, pair_count, feat_width + SIDE), jnp.float32),
            jax.ShapeDtypeStruct((image_members, pair_count, feat_width), jnp.float32),
        ),
        in_specs=[vmem, vmem, vmem, smem, smem],
        out_specs=(vmem, vmem),
        name="score_tile",
    )(group_block, group_text, text_ids.reshape(1, -1), logit_scale, logit_bias)


def finish_kernel(total_tokens, parts_ref, text_ref, scale_ref, grad_ref, scalar_ref):
    feat_width = text_ref.shape[-1]
    total = parts_ref[0]
    for member in range(1, parts_ref.shape[0]):
        total = total + parts_ref[member]
    direction = scale_ref[0] * total[:, :feat_width]
    unit, inverse = unit_rows(text_ref[...].astype(jnp.float32))
    grad_ref[...] = tangent(direction, unit, inverse)
    side = total[:1, feat_width:]
    means = side[:, :32] + side[:, 32:64] + side[:, 64:96]
    means = means * (1.0 / total_tokens)
    place = lax.broadcasted_iota(jnp.int32, means.shape, 1)
    usage = jnp.where(place < BITS, means, 0.5)
    spread = -(usage * jnp.log(usage) + (1.0 - usage) * jnp.log(1.0 - usage))
    scalar_ref[0] = jnp.sum(jnp.where(place == BITS, means, 0.0))
    scalar_ref[1] = jnp.sum(jnp.where(place == BITS + 1, means, 0.0))
    scalar_ref[2] = jnp.sum(jnp.where(place < BITS, spread, 0.0))


def finish_text(parts, text_embed, logit_scale, total_tokens):
    vmem = pl.BlockSpec(memory_space=pltpu.VMEM)
    smem = pl.BlockSpec(memory_space=pltpu.SMEM)
    return pl.pallas_call(
        functools.partial(finish_kernel, total_tokens),
        out_shape=(
            jax.ShapeDtypeStruct(text_embed.shape, jnp.float32),
            jax.ShapeDtypeStruct((3,), jnp.float32),
        ),
        in_specs=[vmem, vmem, smem],
        out_specs=(vmem, smem),
        name="finish_text",
    )(parts, text_embed, logit_scale)


def group_ids(sizes, axes, pair_count):
    count = math.prod(sizes[axis] for axis in axes)
    member = jnp.arange(count * pair_count, dtype=jnp.int32) // pair_count
    place = {axis: lax.axis_index(axis) for axis in ROW_AXES + BLK_AXES}
    for axis in reversed(axes):
        place[axis] = member % sizes[axis]
        member = member // sizes[axis]
    device = jnp.int32(0)
    for axis in ROW_AXES + BLK_AXES:
        device = device * sizes[axis] + place[axis]
    return device * pair_count + jnp.arange(count * pair_count, dtype=jnp.int32) % pair_count


def body(sizes, latent, w_post, w_proj, gain, text_embed, labels, logit_scale, logit_bias):
    pair_count = text_embed.shape[0]
    n_image = math.prod(sizes[axis] for axis in IMAGE_AXES)
    n_text = math.prod(sizes[axis] for axis in TEXT_AXES)
    total_tokens = latent.shape[1] * math.prod(sizes.values())

    text_copies = jnp.broadcast_to(text_embed[None], (n_text,) + text_embed.shape)
    group_text = lax.all_to_all(text_copies, TEXT_AXES, 0, 0)

    image_block, image_unit, image_inv = embed_images(
        latent, w_post, w_proj, gain, labels, n_image
    )
    image_block, group_text = lax.optimization_barrier((image_block, group_text))
    group_block = lax.all_to_all(image_block, IMAGE_AXES, 0, 0)
    text_ids = group_ids(sizes, TEXT_AXES, pair_count)
    text_part, image_part = score_tile(
        group_block, group_text, text_ids, logit_scale, logit_bias
    )
    text_part = lax.all_to_all(text_part, TEXT_AXES, 0, 0)
    image_part, text_part = lax.optimization_barrier((image_part, text_part))
    image_part = lax.all_to_all(image_part, IMAGE_AXES, 0, 0)
    image_dir = logit_scale[0] * jnp.sum(image_part, axis=0)
    grad_image = tangent(image_dir, image_unit, image_inv[:, :1])
    grad_text, scalars = finish_text(text_part, text_embed, logit_scale, total_tokens)
    return (grad_image, grad_text, scalars)


def solution(mesh):
    sizes = {"x": 4, "y_lo": 2, "core": 2, "z": 8, "y_hi": 4}
    names = ROW_AXES + BLK_AXES
    fine = Mesh(mesh.devices.reshape([sizes[axis] for axis in names]), names)
    return jax.shard_map(
        functools.partial(body, sizes),
        mesh=fine,
        in_specs=(P(None, names), P(), P(), P(), P(names, None), P(names), P(), P()),
        out_specs=(P(names, None), P(names, None), P()),
        check_vma=False,
    )
```

```python
import functools
import math

import jax
import jax.numpy as jnp
from jax import lax
from jax.experimental import pallas as pl
from jax.experimental.pallas import tpu as pltpu
from jax.sharding import Mesh
from jax.sharding import PartitionSpec as P

EPS = 1e-06
SHARPNESS = 4.0
BITS = 28
SIDE = 128
CHUNK = 256

ROW_AXES = ("x", "y_lo", "core")
BLK_AXES = ("z", "y_hi")
TEXT_AXES = ("y_hi", "y_lo", "core")
IMAGE_AXES = ("x", "z")


def code_sums(latent):
    bit_count = latent.shape[0]
    length = jnp.sqrt(jnp.sum(latent * latent, axis=0, keepdims=True))
    unit_code = latent / length
    root = 1.0 / math.sqrt(bit_count)
    offset = unit_code - jnp.where(latent > 0, root, -root)
    sharp = SHARPNESS * math.sqrt(bit_count) * unit_code
    size = jnp.abs(sharp)
    small = jnp.exp(-size)
    inverse = 1.0 / (1.0 + small)
    rest = small * inverse
    entropy = jnp.log1p(small) + size * rest
    prob = jnp.where(sharp > 0, inverse, rest)

    def total(values):
        return jnp.sum(jnp.sum(values, axis=1, keepdims=True), axis=0, keepdims=True)

    usage = jnp.sum(prob, axis=1, keepdims=True)
    return (total(offset * offset), total(entropy), usage)


def round_bf(values):
    return values.astype(jnp.bfloat16).astype(jnp.float32)


def gelu(x):
    inner = x * (math.sqrt(2.0 / math.pi) + (math.sqrt(2.0 / math.pi) * 0.044715) * (x * x))
    half = 0.5 * x
    return half + half * jnp.tanh(inner)


def image_kernel(
    copies,
    latent_hbm,
    post_hbm,
    proj_hbm,
    gain_ref,
    label_ref,
    block_ref,
    unit_ref,
    inv_ref,
    latent_ref,
    post_ref,
    proj_ref,
    sems,
):
    fetch_latent = pltpu.make_async_copy(latent_hbm, latent_ref, sems.at[0])
    fetch_post = pltpu.make_async_copy(post_hbm, post_ref, sems.at[1])
    fetch_proj = pltpu.make_async_copy(proj_hbm, proj_ref, sems.at[2])
    fetch_latent.start()
    fetch_post.start()
    fetch_proj.start()
    fetch_latent.wait()
    latent = latent_ref[...]
    bit_count, token_count = latent.shape
    image_count, feat_width = unit_ref.shape
    patch = token_count // image_count

    commit, entropy, usage = code_sums(latent)
    lane = lax.broadcasted_iota(jnp.int32, (bit_count, SIDE), 1)
    bit = lax.broadcasted_iota(jnp.int32, (bit_count, SIDE), 0)
    first = round_bf(usage)
    second = round_bf(usage - first)
    third = usage - first - second
    spread = jnp.where(lane == bit, first, 0.0)
    spread = jnp.where(lane == bit + 32, second, spread)
    spread = jnp.where(lane == bit + 64, third, spread)
    side = jnp.sum(spread, axis=0, keepdims=True)
    place = lax.broadcasted_iota(jnp.int32, (1, SIDE), 1)
    for at, value in ((BITS, commit), (BITS + 1, entropy)):
        first = round_bf(value)
        second = round_bf(value - first)
        third = value - first - second
        side = jnp.where(place == at, first, side)
        side = jnp.where(place == at + 32, second, side)
        side = jnp.where(place == at + 64, third, side)
    sides = []
    for i in range(image_count):
        label = label_ref[i]
        high = (label // 32).astype(jnp.float32)
        low = (label % 32).astype(jnp.float32)
        own = side if i == 0 else jnp.zeros_like(side)
        own = jnp.where(place == SIDE - 2, high, own)
        sides.append(jnp.where(place == SIDE - 1, low, own))
    codes = jnp.where(latent > 0, 1.0, -1.0)
    codes = jnp.transpose(codes, (1, 0)).astype(jnp.bfloat16)
    fetch_post.wait()
    post = post_ref[...]
    fetch_proj.wait()
    proj = proj_ref[...]
    sums = []
    for first in range(0, token_count, CHUNK):
        pre_act = jnp.dot(codes[first : first + CHUNK], post, preferred_element_type=jnp.float32)
        hidden = gelu(pre_act).astype(jnp.bfloat16)
        projected = jnp.dot(hidden, proj, preferred_element_type=jnp.float32)
        square = jnp.sum(projected * projected, axis=-1, keepdims=True)
        scaled = projected * lax.rsqrt(square * (1.0 / feat_width) + EPS)
        sums.append(jnp.sum(scaled, axis=0, keepdims=True))
    steps = patch // CHUNK
    rows = [functools.reduce(jnp.add, sums[i * steps : (i + 1) * steps]) for i in range(image_count)]
    embeds = jnp.concatenate(rows, axis=0) * gain_ref[...][None, :] * (1.0 / patch)
    inverse = lax.rsqrt(jnp.sum(embeds * embeds, axis=-1, keepdims=True) + EPS)
    unit = embeds * inverse
    unit_ref[...] = unit
    inv_ref[...] = jnp.broadcast_to(inverse, inv_ref.shape)

    block = jnp.concatenate([unit, jnp.concatenate(sides, axis=0)], axis=1)
    block = block.astype(jnp.bfloat16)
    for member in range(copies):
        block_ref[member] = block


def embed_images(latent, w_post, w_proj, gain, labels, copies):
    image_count = labels.shape[0]
    feat_width = w_proj.shape[1]
    vmem = pl.BlockSpec(memory_space=pltpu.VMEM)
    hbm = pl.BlockSpec(memory_space=pl.ANY)
    return pl.pallas_call(
        functools.partial(image_kernel, copies),
        out_shape=(
            jax.ShapeDtypeStruct((copies, image_count, feat_width + SIDE), jnp.bfloat16),
            jax.ShapeDtypeStruct((image_count, feat_width), jnp.float32),
            jax.ShapeDtypeStruct((image_count, 128), jnp.float32),
        ),
        in_specs=[hbm, hbm, hbm, vmem, pl.BlockSpec(memory_space=pltpu.SMEM)],
        out_specs=(vmem, vmem, vmem),
        scratch_shapes=[
            pltpu.VMEM(latent.shape, latent.dtype),
            pltpu.VMEM(w_post.shape, w_post.dtype),
            pltpu.VMEM(w_proj.shape, w_proj.dtype),
            pltpu.SemaphoreType.DMA((3,)),
        ],
        compiler_params=pltpu.CompilerParams(vmem_limit_bytes=56 * 1024 * 1024),
        cost_estimate=pl.CostEstimate(
            flops=2_200_000_000, bytes_accessed=1_800_000, transcendentals=1_100_000
        ),
        name="embed_images",
    )(latent, w_post, w_proj, gain, labels)


def unit_rows(values):
    inverse = lax.rsqrt(jnp.sum(values * values, axis=-1, keepdims=True) + EPS)
    return (values * inverse, inverse)


def tangent(direction, unit, inverse):
    return (direction - unit * jnp.sum(unit * direction, axis=-1, keepdims=True)) * inverse


def text_kernel(text_ref, block_ref):
    unit, _ = unit_rows(text_ref[...].astype(jnp.float32))
    unit = unit.astype(jnp.bfloat16)
    for member in range(block_ref.shape[0]):
        block_ref[member] = unit


def text_blocks(text_embed, copies):
    vmem = pl.BlockSpec(memory_space=pltpu.VMEM)
    return pl.pallas_call(
        text_kernel,
        out_shape=jax.ShapeDtypeStruct((copies,) + text_embed.shape, jnp.bfloat16),
        in_specs=[vmem],
        out_specs=vmem,
        name="text_blocks",
    )(text_embed)


def image_part_kernel(grad_ref, text_ref, part_ref):
    part = jnp.dot(grad_ref[...], text_ref[...], preferred_element_type=jnp.float32)
    pair_count = part_ref.shape[1]
    for member in range(part_ref.shape[0]):
        part_ref[member] = part[member * pair_count : (member + 1) * pair_count]


def image_parts(grad_bf, group_text, members):
    vmem = pl.BlockSpec(memory_space=pltpu.VMEM)
    pair_count = grad_bf.shape[0] // members
    return pl.pallas_call(
        image_part_kernel,
        out_shape=jax.ShapeDtypeStruct((members, pair_count, group_text.shape[1]), jnp.float32),
        in_specs=[vmem, vmem],
        out_specs=vmem,
        name="image_parts",
    )(grad_bf, group_text)


def finish_kernel(total_tokens, parts_ref, text_ref, scale_ref, grad_ref, scalar_ref):
    feat_width = text_ref.shape[-1]
    total = parts_ref[0]
    for member in range(1, parts_ref.shape[0]):
        total = total + parts_ref[member]
    direction = scale_ref[0] * total[:, :feat_width]
    unit, inverse = unit_rows(text_ref[...].astype(jnp.float32))
    grad_ref[...] = tangent(direction, unit, inverse)
    side = total[:1, feat_width:]
    means = side[:, :32] + side[:, 32:64] + side[:, 64:96]
    means = means * (1.0 / total_tokens)
    place = lax.broadcasted_iota(jnp.int32, means.shape, 1)
    usage = jnp.where(place < BITS, means, 0.5)
    spread = -(usage * jnp.log(usage) + (1.0 - usage) * jnp.log(1.0 - usage))
    scalar_ref[0] = jnp.sum(jnp.where(place == BITS, means, 0.0))
    scalar_ref[1] = jnp.sum(jnp.where(place == BITS + 1, means, 0.0))
    scalar_ref[2] = jnp.sum(jnp.where(place < BITS, spread, 0.0))


def finish_text(parts, text_embed, logit_scale, total_tokens):
    vmem = pl.BlockSpec(memory_space=pltpu.VMEM)
    smem = pl.BlockSpec(memory_space=pltpu.SMEM)
    return pl.pallas_call(
        functools.partial(finish_kernel, total_tokens),
        out_shape=(
            jax.ShapeDtypeStruct(text_embed.shape, jnp.float32),
            jax.ShapeDtypeStruct((3,), jnp.float32),
        ),
        in_specs=[vmem, vmem, smem],
        out_specs=(vmem, smem),
        name="finish_text",
    )(parts, text_embed, logit_scale)


def group_ids(sizes, axes, pair_count):
    count = math.prod(sizes[axis] for axis in axes)
    member = jnp.arange(count * pair_count, dtype=jnp.int32) // pair_count
    place = {axis: lax.axis_index(axis) for axis in ROW_AXES + BLK_AXES}
    for axis in reversed(axes):
        place[axis] = member % sizes[axis]
        member = member // sizes[axis]
    device = jnp.int32(0)
    for axis in ROW_AXES + BLK_AXES:
        device = device * sizes[axis] + place[axis]
    return device * pair_count + jnp.arange(count * pair_count, dtype=jnp.int32) % pair_count


def body(sizes, latent, w_post, w_proj, gain, text_embed, labels, logit_scale, logit_bias):
    pair_count, feat_width = text_embed.shape
    n_image = math.prod(sizes[axis] for axis in IMAGE_AXES)
    n_text = math.prod(sizes[axis] for axis in TEXT_AXES)
    text_count = n_text * pair_count
    total_tokens = latent.shape[1] * math.prod(sizes.values())
    scale_value = logit_scale[0]
    bias_value = logit_bias[0]

    group_text = lax.all_to_all(text_blocks(text_embed, n_text), TEXT_AXES, 0, 0)

    image_block, image_unit, image_inv = embed_images(
        latent, w_post, w_proj, gain, labels, n_image
    )
    image_block, group_text = lax.optimization_barrier((image_block, group_text))
    group_text = group_text.reshape(text_count, feat_width)
    group_block = lax.all_to_all(image_block, IMAGE_AXES, 0, 0)
    group_block = group_block.reshape(n_image * pair_count, feat_width + SIDE)
    group_image = group_block[:, :feat_width]
    group_side = group_block[:, feat_width:].astype(jnp.float32)
    group_labels = (group_side[:, SIDE - 2] * 32.0 + group_side[:, SIDE - 1]).astype(jnp.int32)
    group_sums = jnp.sum(group_side, axis=0, keepdims=True)

    text_ids = group_ids(sizes, TEXT_AXES, pair_count)
    products = jnp.dot(group_image, group_text.T, preferred_element_type=jnp.float32)
    pair_sign = jnp.where(
        group_labels[:, None] == text_ids[None, :], jnp.float32(1.0), jnp.float32(-1.0)
    )
    margin = pair_sign * (scale_value * products + bias_value)
    grad_bf = (-pair_sign * jax.nn.sigmoid(-margin)).astype(jnp.bfloat16)
    text_part = jnp.dot(grad_bf.T, group_image, preferred_element_type=jnp.float32)
    text_part = jnp.concatenate(
        [text_part, jnp.broadcast_to(group_sums, (text_count, SIDE))], axis=1
    )
    text_part = text_part.reshape(n_text, pair_count, feat_width + SIDE)
    text_part = lax.all_to_all(text_part, TEXT_AXES, 0, 0)

    image_part = image_parts(grad_bf, group_text, n_image)
    image_part, text_part = lax.optimization_barrier((image_part, text_part))
    image_part = lax.all_to_all(image_part, IMAGE_AXES, 0, 0)
    image_dir = scale_value * jnp.sum(image_part, axis=0)
    grad_image = tangent(image_dir, image_unit, image_inv[:, :1])
    grad_text, scalars = finish_text(text_part, text_embed, logit_scale, total_tokens)
    return (grad_image, grad_text, scalars)


def solution(mesh):
    sizes = {"x": 4, "y_lo": 2, "core": 2, "z": 8, "y_hi": 4}
    names = ROW_AXES + BLK_AXES
    fine = Mesh(mesh.devices.reshape([sizes[axis] for axis in names]), names)
    return jax.shard_map(
        functools.partial(body, sizes),
        mesh=fine,
        in_specs=(P(None, names), P(), P(), P(), P(names, None), P(names), P(), P()),
        out_specs=(P(names, None), P(names, None), P()),
        check_vma=False,
    )
```

```python
import functools
import math

import jax
import jax.numpy as jnp
from jax import lax
from jax.experimental import pallas as pl
from jax.experimental.pallas import tpu as pltpu
from jax.sharding import Mesh
from jax.sharding import PartitionSpec as P

EPS = 1e-06
SHARPNESS = 4.0
BITS = 28
SIDE = 128
CHUNK = 256

ROW_AXES = ("x", "y_lo", "core")
BLK_AXES = ("z", "y_hi")
TEXT_AXES = ("x", "core")
IMAGE_AXES = ("z", "y_hi", "y_lo")


def code_sums(latent):
    bit_count = latent.shape[0]
    length = jnp.sqrt(jnp.sum(latent * latent, axis=0, keepdims=True))
    unit_code = latent / length
    root = 1.0 / math.sqrt(bit_count)
    offset = unit_code - jnp.where(latent > 0, root, -root)
    sharp = SHARPNESS * math.sqrt(bit_count) * unit_code
    size = jnp.abs(sharp)
    small = jnp.exp(-size)
    inverse = 1.0 / (1.0 + small)
    rest = small * inverse
    entropy = jnp.log1p(small) + size * rest
    prob = jnp.where(sharp > 0, inverse, rest)

    def total(values):
        return jnp.sum(jnp.sum(values, axis=1, keepdims=True), axis=0, keepdims=True)

    usage = jnp.sum(prob, axis=1, keepdims=True)
    return (total(offset * offset), total(entropy), usage)


def round_bf(values):
    return values.astype(jnp.bfloat16).astype(jnp.float32)


def gelu(x):
    inner = x * (math.sqrt(2.0 / math.pi) + (math.sqrt(2.0 / math.pi) * 0.044715) * (x * x))
    half = 0.5 * x
    return half + half * jnp.tanh(inner)


def image_kernel(
    copies,
    latent_hbm,
    post_hbm,
    proj_hbm,
    gain_ref,
    label_ref,
    block_ref,
    unit_ref,
    inv_ref,
    latent_ref,
    post_ref,
    proj_ref,
    sems,
):
    fetch_latent = pltpu.make_async_copy(latent_hbm, latent_ref, sems.at[0])
    fetch_post = pltpu.make_async_copy(post_hbm, post_ref, sems.at[1])
    fetch_proj = pltpu.make_async_copy(proj_hbm, proj_ref, sems.at[2])
    fetch_latent.start()
    fetch_post.start()
    fetch_proj.start()
    fetch_latent.wait()
    latent = latent_ref[...]
    bit_count, token_count = latent.shape
    image_count, feat_width = unit_ref.shape
    patch = token_count // image_count

    commit, entropy, usage = code_sums(latent)
    lane = lax.broadcasted_iota(jnp.int32, (bit_count, SIDE), 1)
    bit = lax.broadcasted_iota(jnp.int32, (bit_count, SIDE), 0)
    first = round_bf(usage)
    second = round_bf(usage - first)
    third = usage - first - second
    spread = jnp.where(lane == bit, first, 0.0)
    spread = jnp.where(lane == bit + 32, second, spread)
    spread = jnp.where(lane == bit + 64, third, spread)
    side = jnp.sum(spread, axis=0, keepdims=True)
    place = lax.broadcasted_iota(jnp.int32, (1, SIDE), 1)
    for at, value in ((BITS, commit), (BITS + 1, entropy)):
        first = round_bf(value)
        second = round_bf(value - first)
        third = value - first - second
        side = jnp.where(place == at, first, side)
        side = jnp.where(place == at + 32, second, side)
        side = jnp.where(place == at + 64, third, side)
    sides = []
    for i in range(image_count):
        label = label_ref[i]
        high = (label // 32).astype(jnp.float32)
        low = (label % 32).astype(jnp.float32)
        own = side if i == 0 else jnp.zeros_like(side)
        own = jnp.where(place == SIDE - 2, high, own)
        sides.append(jnp.where(place == SIDE - 1, low, own))
    codes = jnp.where(latent > 0, 1.0, -1.0)
    codes = jnp.transpose(codes, (1, 0)).astype(jnp.bfloat16)
    fetch_post.wait()
    post = post_ref[...]
    fetch_proj.wait()
    proj = proj_ref[...]
    sums = []
    for first in range(0, token_count, CHUNK):
        pre_act = jnp.dot(codes[first : first + CHUNK], post, preferred_element_type=jnp.float32)
        hidden = gelu(pre_act).astype(jnp.bfloat16)
        projected = jnp.dot(hidden, proj, preferred_element_type=jnp.float32)
        square = jnp.sum(projected * projected, axis=-1, keepdims=True)
        scaled = projected * lax.rsqrt(square * (1.0 / feat_width) + EPS)
        sums.append(jnp.sum(scaled, axis=0, keepdims=True))
    steps = patch // CHUNK
    rows = [functools.reduce(jnp.add, sums[i * steps : (i + 1) * steps]) for i in range(image_count)]
    embeds = jnp.concatenate(rows, axis=0) * gain_ref[...][None, :] * (1.0 / patch)
    inverse = lax.rsqrt(jnp.sum(embeds * embeds, axis=-1, keepdims=True) + EPS)
    unit = embeds * inverse
    unit_ref[...] = unit
    inv_ref[...] = jnp.broadcast_to(inverse, inv_ref.shape)

    block = jnp.concatenate([unit, jnp.concatenate(sides, axis=0)], axis=1)
    block = block.astype(jnp.bfloat16)
    for member in range(copies):
        block_ref[member] = block


def embed_images(latent, w_post, w_proj, gain, labels, copies):
    image_count = labels.shape[0]
    feat_width = w_proj.shape[1]
    vmem = pl.BlockSpec(memory_space=pltpu.VMEM)
    hbm = pl.BlockSpec(memory_space=pl.ANY)
    return pl.pallas_call(
        functools.partial(image_kernel, copies),
        out_shape=(
            jax.ShapeDtypeStruct((copies, image_count, feat_width + SIDE), jnp.bfloat16),
            jax.ShapeDtypeStruct((image_count, feat_width), jnp.float32),
            jax.ShapeDtypeStruct((image_count, 128), jnp.float32),
        ),
        in_specs=[hbm, hbm, hbm, vmem, pl.BlockSpec(memory_space=pltpu.SMEM)],
        out_specs=(vmem, vmem, vmem),
        scratch_shapes=[
            pltpu.VMEM(latent.shape, latent.dtype),
            pltpu.VMEM(w_post.shape, w_post.dtype),
            pltpu.VMEM(w_proj.shape, w_proj.dtype),
            pltpu.SemaphoreType.DMA((3,)),
        ],
        compiler_params=pltpu.CompilerParams(vmem_limit_bytes=56 * 1024 * 1024),
        cost_estimate=pl.CostEstimate(
            flops=2_200_000_000, bytes_accessed=1_800_000, transcendentals=1_100_000
        ),
        name="embed_images",
    )(latent, w_post, w_proj, gain, labels)


def unit_rows(values):
    inverse = lax.rsqrt(jnp.sum(values * values, axis=-1, keepdims=True) + EPS)
    return (values * inverse, inverse)


def tangent(direction, unit, inverse):
    return (direction - unit * jnp.sum(unit * direction, axis=-1, keepdims=True)) * inverse


def text_kernel(text_ref, block_ref):
    unit, _ = unit_rows(text_ref[...].astype(jnp.float32))
    unit = unit.astype(jnp.bfloat16)
    for member in range(block_ref.shape[0]):
        block_ref[member] = unit


def text_blocks(text_embed, copies):
    vmem = pl.BlockSpec(memory_space=pltpu.VMEM)
    return pl.pallas_call(
        text_kernel,
        out_shape=jax.ShapeDtypeStruct((copies,) + text_embed.shape, jnp.bfloat16),
        in_specs=[vmem],
        out_specs=vmem,
        name="text_blocks",
    )(text_embed)


def finish_kernel(total_tokens, parts_ref, text_ref, scale_ref, grad_ref, scalar_ref):
    feat_width = text_ref.shape[-1]
    total = parts_ref[0]
    for member in range(1, parts_ref.shape[0]):
        total = total + parts_ref[member]
    direction = scale_ref[0] * total[:, :feat_width]
    unit, inverse = unit_rows(text_ref[...].astype(jnp.float32))
    grad_ref[...] = tangent(direction, unit, inverse)
    side = total[:1, feat_width:]
    means = side[:, :32] + side[:, 32:64] + side[:, 64:96]
    means = means * (1.0 / total_tokens)
    place = lax.broadcasted_iota(jnp.int32, means.shape, 1)
    usage = jnp.where(place < BITS, means, 0.5)
    spread = -(usage * jnp.log(usage) + (1.0 - usage) * jnp.log(1.0 - usage))
    scalar_ref[0] = jnp.sum(jnp.where(place == BITS, means, 0.0))
    scalar_ref[1] = jnp.sum(jnp.where(place == BITS + 1, means, 0.0))
    scalar_ref[2] = jnp.sum(jnp.where(place < BITS, spread, 0.0))


def finish_text(parts, text_embed, logit_scale, total_tokens):
    vmem = pl.BlockSpec(memory_space=pltpu.VMEM)
    smem = pl.BlockSpec(memory_space=pltpu.SMEM)
    return pl.pallas_call(
        functools.partial(finish_kernel, total_tokens),
        out_shape=(
            jax.ShapeDtypeStruct(text_embed.shape, jnp.float32),
            jax.ShapeDtypeStruct((3,), jnp.float32),
        ),
        in_specs=[vmem, vmem, smem],
        out_specs=(vmem, smem),
        name="finish_text",
    )(parts, text_embed, logit_scale)


def swap_cores(block):
    return lax.ppermute(block, "core", [(0, 1), (1, 0)])


def along_x(block, distance, count):
    return lax.ppermute(block, "x", [(i, (i + distance) % count) for i in range(count)])


def from_here(members, n_x):
    members = members.reshape((n_x, 2) + members.shape[1:])
    here = lax.axis_index("x")
    other = lax.axis_index("core") == 1
    turned = [
        lax.dynamic_index_in_dim(members, (here + distance) % n_x, 0, keepdims=False)
        for distance in range(n_x)
    ]
    return [
        jnp.where(other, block[1 - core], block[core]) for block in turned for core in range(2)
    ]


def body(sizes, latent, w_post, w_proj, gain, text_embed, labels, logit_scale, logit_bias):
    pair_count, feat_width = text_embed.shape
    n_x = sizes["x"]
    n_image = math.prod(sizes[axis] for axis in IMAGE_AXES)
    n_text = math.prod(sizes[axis] for axis in TEXT_AXES)
    text_count = n_text * pair_count
    chip_count = 2 * pair_count
    total_tokens = latent.shape[1] * math.prod(sizes.values())
    scale_value = logit_scale[0]
    bias_value = logit_bias[0]

    group_text = lax.all_to_all(text_blocks(text_embed, n_text), TEXT_AXES, 0, 0)
    group_text = jnp.concatenate(from_here(group_text, n_x), axis=0)

    image_block, image_unit, image_inv = embed_images(
        latent, w_post, w_proj, gain, labels, n_image
    )
    group_block = lax.all_to_all(image_block, IMAGE_AXES, 0, 0)
    group_block = group_block.reshape(n_image * pair_count, feat_width + SIDE)
    group_image = group_block[:, :feat_width]
    group_side = group_block[:, feat_width:].astype(jnp.float32)
    group_labels = (group_side[:, SIDE - 2] * 32.0 + group_side[:, SIDE - 1]).astype(jnp.int32)
    group_sums = jnp.sum(group_side, axis=0, keepdims=True)

    row_size = sizes["y_lo"] * sizes["core"]
    blk_size = sizes["z"] * sizes["y_hi"]
    place = jnp.arange(text_count, dtype=jnp.int32)
    text_x = (lax.axis_index("x") + place // chip_count) % n_x
    text_core = lax.axis_index("core") ^ (place // pair_count % 2)
    text_row = text_x * row_size + lax.axis_index("y_lo") * sizes["core"] + text_core
    text_blk = lax.axis_index("z") * sizes["y_hi"] + lax.axis_index("y_hi")
    text_ids = (text_row * blk_size + text_blk) * pair_count + place % pair_count

    products = jnp.dot(group_image, group_text.T, preferred_element_type=jnp.float32)
    pair_sign = jnp.where(
        group_labels[:, None] == text_ids[None, :], jnp.float32(1.0), jnp.float32(-1.0)
    )
    margin = pair_sign * (scale_value * products + bias_value)
    grad_bf = (-pair_sign * jax.nn.sigmoid(-margin)).astype(jnp.bfloat16)
    image_part = jnp.dot(grad_bf, group_text, preferred_element_type=jnp.float32)
    image_part = image_part.reshape(n_image, pair_count, feat_width)
    image_part = lax.all_to_all(image_part, IMAGE_AXES, 0, 0)

    text_part = jnp.dot(grad_bf.T, group_image, preferred_element_type=jnp.float32)
    text_part = jnp.concatenate(
        [text_part, jnp.broadcast_to(group_sums, (text_count, SIDE))], axis=1
    )
    chip_part = text_part[:chip_count]
    for distance in range(1, n_x):
        rows = text_part[distance * chip_count : (distance + 1) * chip_count]
        chip_part = chip_part + along_x(rows, distance, n_x)
    text_part = chip_part[:pair_count] + swap_cores(chip_part[pair_count:])
    grad_text, scalars = finish_text(text_part[None], text_embed, logit_scale, total_tokens)

    image_dir = scale_value * jnp.sum(image_part, axis=0)
    grad_image = tangent(image_dir, image_unit, image_inv[:, :1])
    return (grad_image, grad_text, scalars)


def solution(mesh):
    sizes = {"x": 4, "y_lo": 2, "core": 2, "z": 8, "y_hi": 4}
    names = ROW_AXES + BLK_AXES
    fine = Mesh(mesh.devices.reshape([sizes[axis] for axis in names]), names)
    return jax.shard_map(
        functools.partial(body, sizes),
        mesh=fine,
        in_specs=(P(None, names), P(), P(), P(), P(names, None), P(names), P(), P()),
        out_specs=(P(names, None), P(names, None), P()),
        check_vma=False,
    )
```

```python
import functools
import math

import jax
import jax.numpy as jnp
from jax import lax
from jax.experimental import pallas as pl
from jax.experimental.pallas import tpu as pltpu
from jax.sharding import Mesh
from jax.sharding import PartitionSpec as P

EPS = 1e-06
SHARPNESS = 4.0
BITS = 28
SIDE = 128
CHUNK = 256

ROW_AXES = ("x", "y_lo", "core")
BLK_AXES = ("z", "y_hi")
TEXT_AXES = ("x", "core")
IMAGE_AXES = ("z", "y_hi", "y_lo")


def code_sums(latent):
    bit_count = latent.shape[0]
    length = jnp.sqrt(jnp.sum(latent * latent, axis=0, keepdims=True))
    unit_code = latent / length
    root = 1.0 / math.sqrt(bit_count)
    offset = unit_code - jnp.where(latent > 0, root, -root)
    sharp = SHARPNESS * math.sqrt(bit_count) * unit_code
    size = jnp.abs(sharp)
    small = jnp.exp(-size)
    inverse = 1.0 / (1.0 + small)
    rest = small * inverse
    entropy = jnp.log1p(small) + size * rest
    prob = jnp.where(sharp > 0, inverse, rest)

    def total(values):
        return jnp.sum(jnp.sum(values, axis=1, keepdims=True), axis=0, keepdims=True)

    usage = jnp.sum(prob, axis=1, keepdims=True)
    return (total(offset * offset), total(entropy), usage)


def round_bf(values):
    return values.astype(jnp.bfloat16).astype(jnp.float32)


def gelu(x):
    inner = x * (math.sqrt(2.0 / math.pi) + (math.sqrt(2.0 / math.pi) * 0.044715) * (x * x))
    half = 0.5 * x
    return half + half * jnp.tanh(inner)


def image_kernel(
    copies,
    latent_hbm,
    post_hbm,
    proj_hbm,
    gain_ref,
    label_ref,
    block_ref,
    unit_ref,
    inv_ref,
    latent_ref,
    post_ref,
    proj_ref,
    sems,
):
    fetch_latent = pltpu.make_async_copy(latent_hbm, latent_ref, sems.at[0])
    fetch_post = pltpu.make_async_copy(post_hbm, post_ref, sems.at[1])
    fetch_proj = pltpu.make_async_copy(proj_hbm, proj_ref, sems.at[2])
    fetch_latent.start()
    fetch_post.start()
    fetch_proj.start()
    fetch_latent.wait()
    latent = latent_ref[...]
    bit_count, token_count = latent.shape
    image_count, feat_width = unit_ref.shape
    patch = token_count // image_count

    commit, entropy, usage = code_sums(latent)
    lane = lax.broadcasted_iota(jnp.int32, (bit_count, SIDE), 1)
    bit = lax.broadcasted_iota(jnp.int32, (bit_count, SIDE), 0)
    first = round_bf(usage)
    second = round_bf(usage - first)
    third = usage - first - second
    spread = jnp.where(lane == bit, first, 0.0)
    spread = jnp.where(lane == bit + 32, second, spread)
    spread = jnp.where(lane == bit + 64, third, spread)
    side = jnp.sum(spread, axis=0, keepdims=True)
    place = lax.broadcasted_iota(jnp.int32, (1, SIDE), 1)
    for at, value in ((BITS, commit), (BITS + 1, entropy)):
        first = round_bf(value)
        second = round_bf(value - first)
        third = value - first - second
        side = jnp.where(place == at, first, side)
        side = jnp.where(place == at + 32, second, side)
        side = jnp.where(place == at + 64, third, side)
    sides = []
    for i in range(image_count):
        label = label_ref[i]
        high = (label // 32).astype(jnp.float32)
        low = (label % 32).astype(jnp.float32)
        own = side if i == 0 else jnp.zeros_like(side)
        own = jnp.where(place == SIDE - 2, high, own)
        sides.append(jnp.where(place == SIDE - 1, low, own))
    codes = jnp.where(latent > 0, 1.0, -1.0)
    codes = jnp.transpose(codes, (1, 0)).astype(jnp.bfloat16)
    fetch_post.wait()
    post = post_ref[...]
    fetch_proj.wait()
    proj = proj_ref[...]
    sums = []
    for first in range(0, token_count, CHUNK):
        pre_act = jnp.dot(codes[first : first + CHUNK], post, preferred_element_type=jnp.float32)
        hidden = gelu(pre_act).astype(jnp.bfloat16)
        projected = jnp.dot(hidden, proj, preferred_element_type=jnp.float32)
        square = jnp.sum(projected * projected, axis=-1, keepdims=True)
        scaled = projected * lax.rsqrt(square * (1.0 / feat_width) + EPS)
        sums.append(jnp.sum(scaled, axis=0, keepdims=True))
    steps = patch // CHUNK
    rows = [functools.reduce(jnp.add, sums[i * steps : (i + 1) * steps]) for i in range(image_count)]
    embeds = jnp.concatenate(rows, axis=0) * gain_ref[...][None, :] * (1.0 / patch)
    inverse = lax.rsqrt(jnp.sum(embeds * embeds, axis=-1, keepdims=True) + EPS)
    unit = embeds * inverse
    unit_ref[...] = unit
    inv_ref[...] = jnp.broadcast_to(inverse, inv_ref.shape)

    block = jnp.concatenate([unit, jnp.concatenate(sides, axis=0)], axis=1)
    block = block.astype(jnp.bfloat16)
    for member in range(copies):
        block_ref[member] = block


def embed_images(latent, w_post, w_proj, gain, labels, copies):
    image_count = labels.shape[0]
    feat_width = w_proj.shape[1]
    vmem = pl.BlockSpec(memory_space=pltpu.VMEM)
    hbm = pl.BlockSpec(memory_space=pl.ANY)
    return pl.pallas_call(
        functools.partial(image_kernel, copies),
        out_shape=(
            jax.ShapeDtypeStruct((copies, image_count, feat_width + SIDE), jnp.bfloat16),
            jax.ShapeDtypeStruct((image_count, feat_width), jnp.float32),
            jax.ShapeDtypeStruct((image_count, 128), jnp.float32),
        ),
        in_specs=[hbm, hbm, hbm, vmem, pl.BlockSpec(memory_space=pltpu.SMEM)],
        out_specs=(vmem, vmem, vmem),
        scratch_shapes=[
            pltpu.VMEM(latent.shape, latent.dtype),
            pltpu.VMEM(w_post.shape, w_post.dtype),
            pltpu.VMEM(w_proj.shape, w_proj.dtype),
            pltpu.SemaphoreType.DMA((3,)),
        ],
        compiler_params=pltpu.CompilerParams(vmem_limit_bytes=56 * 1024 * 1024),
        cost_estimate=pl.CostEstimate(
            flops=2_200_000_000, bytes_accessed=1_800_000, transcendentals=1_100_000
        ),
        name="embed_images",
    )(latent, w_post, w_proj, gain, labels)


def unit_rows(values):
    inverse = lax.rsqrt(jnp.sum(values * values, axis=-1, keepdims=True) + EPS)
    return (values * inverse, inverse)


def tangent(direction, unit, inverse):
    return (direction - unit * jnp.sum(unit * direction, axis=-1, keepdims=True)) * inverse


def text_kernel(text_ref, block_ref):
    unit, _ = unit_rows(text_ref[...].astype(jnp.float32))
    unit = unit.astype(jnp.bfloat16)
    for member in range(block_ref.shape[0]):
        block_ref[member] = unit


def text_blocks(text_embed, copies):
    vmem = pl.BlockSpec(memory_space=pltpu.VMEM)
    return pl.pallas_call(
        text_kernel,
        out_shape=jax.ShapeDtypeStruct((copies,) + text_embed.shape, jnp.bfloat16),
        in_specs=[vmem],
        out_specs=vmem,
        name="text_blocks",
    )(text_embed)


def finish_kernel(total_tokens, chip_ref, moved_ref, text_ref, scale_ref, grad_ref, scalar_ref):
    pair_count, feat_width = text_ref.shape
    total = chip_ref[:pair_count] + moved_ref[...]
    direction = scale_ref[0] * total[:, :feat_width]
    unit, inverse = unit_rows(text_ref[...].astype(jnp.float32))
    grad_ref[...] = tangent(direction, unit, inverse)
    side = total[:1, feat_width:]
    means = side[:, :32] + side[:, 32:64] + side[:, 64:96]
    means = means * (1.0 / total_tokens)
    place = lax.broadcasted_iota(jnp.int32, means.shape, 1)
    usage = jnp.where(place < BITS, means, 0.5)
    spread = -(usage * jnp.log(usage) + (1.0 - usage) * jnp.log(1.0 - usage))
    scalar_ref[0] = jnp.sum(jnp.where(place == BITS, means, 0.0))
    scalar_ref[1] = jnp.sum(jnp.where(place == BITS + 1, means, 0.0))
    scalar_ref[2] = jnp.sum(jnp.where(place < BITS, spread, 0.0))


def finish_text(chip_part, moved, text_embed, logit_scale, total_tokens):
    vmem = pl.BlockSpec(memory_space=pltpu.VMEM)
    smem = pl.BlockSpec(memory_space=pltpu.SMEM)
    return pl.pallas_call(
        functools.partial(finish_kernel, total_tokens),
        out_shape=(
            jax.ShapeDtypeStruct(text_embed.shape, jnp.float32),
            jax.ShapeDtypeStruct((3,), jnp.float32),
        ),
        in_specs=[vmem, vmem, vmem, smem],
        out_specs=(vmem, smem),
        name="finish_text",
    )(chip_part, moved, text_embed, logit_scale)


def swap_cores(block):
    return lax.ppermute(block, "core", [(0, 1), (1, 0)])


def along_x(block, distance, count):
    return lax.ppermute(block, "x", [(i, (i + distance) % count) for i in range(count)])


def from_here(members, n_x):
    members = members.reshape((n_x, 2) + members.shape[1:])
    here = lax.axis_index("x")
    other = lax.axis_index("core") == 1
    turned = [
        lax.dynamic_index_in_dim(members, (here + distance) % n_x, 0, keepdims=False)
        for distance in range(n_x)
    ]
    return [
        jnp.where(other, block[1 - core], block[core]) for block in turned for core in range(2)
    ]


def body(sizes, latent, w_post, w_proj, gain, text_embed, labels, logit_scale, logit_bias):
    pair_count, feat_width = text_embed.shape
    n_x = sizes["x"]
    n_image = math.prod(sizes[axis] for axis in IMAGE_AXES)
    n_text = math.prod(sizes[axis] for axis in TEXT_AXES)
    text_count = n_text * pair_count
    chip_count = 2 * pair_count
    total_tokens = latent.shape[1] * math.prod(sizes.values())
    scale_value = logit_scale[0]
    bias_value = logit_bias[0]

    group_text = lax.all_to_all(text_blocks(text_embed, n_text), TEXT_AXES, 0, 0)
    group_text = jnp.concatenate(from_here(group_text, n_x), axis=0)

    image_block, image_unit, image_inv = embed_images(
        latent, w_post, w_proj, gain, labels, n_image
    )
    group_block = lax.all_to_all(image_block, IMAGE_AXES, 0, 0)
    group_block = group_block.reshape(n_image * pair_count, feat_width + SIDE)
    group_image = group_block[:, :feat_width]
    group_side = group_block[:, feat_width:].astype(jnp.float32)
    group_labels = (group_side[:, SIDE - 2] * 32.0 + group_side[:, SIDE - 1]).astype(jnp.int32)
    group_sums = jnp.sum(group_side, axis=0, keepdims=True)

    row_size = sizes["y_lo"] * sizes["core"]
    blk_size = sizes["z"] * sizes["y_hi"]
    place = jnp.arange(text_count, dtype=jnp.int32)
    text_x = (lax.axis_index("x") + place // chip_count) % n_x
    text_core = lax.axis_index("core") ^ (place // pair_count % 2)
    text_row = text_x * row_size + lax.axis_index("y_lo") * sizes["core"] + text_core
    text_blk = lax.axis_index("z") * sizes["y_hi"] + lax.axis_index("y_hi")
    text_ids = (text_row * blk_size + text_blk) * pair_count + place % pair_count

    products = jnp.dot(group_image, group_text.T, preferred_element_type=jnp.float32)
    pair_sign = jnp.where(
        group_labels[:, None] == text_ids[None, :], jnp.float32(1.0), jnp.float32(-1.0)
    )
    margin = pair_sign * (scale_value * products + bias_value)
    grad_bf = (-pair_sign * jax.nn.sigmoid(-margin)).astype(jnp.bfloat16)
    image_part = jnp.dot(grad_bf, group_text, preferred_element_type=jnp.float32)
    image_part = image_part.reshape(n_image, pair_count, feat_width)
    image_part = lax.all_to_all(image_part, IMAGE_AXES, 0, 0)

    text_part = jnp.dot(grad_bf.T, group_image, preferred_element_type=jnp.float32)
    text_part = jnp.concatenate(
        [text_part, jnp.broadcast_to(group_sums, (text_count, SIDE))], axis=1
    )
    chip_part = text_part[:chip_count]
    for distance in range(1, n_x):
        rows = text_part[distance * chip_count : (distance + 1) * chip_count]
        chip_part = chip_part + along_x(rows, distance, n_x)
    moved = swap_cores(chip_part[pair_count:])

    image_dir = scale_value * jnp.sum(image_part, axis=0)
    grad_image = tangent(image_dir, image_unit, image_inv[:, :1])
    grad_image, moved = lax.optimization_barrier((grad_image, moved))
    grad_text, scalars = finish_text(chip_part, moved, text_embed, logit_scale, total_tokens)
    return (grad_image, grad_text, scalars)


def solution(mesh):
    sizes = {"x": 4, "y_lo": 2, "core": 2, "z": 8, "y_hi": 4}
    names = ROW_AXES + BLK_AXES
    fine = Mesh(mesh.devices.reshape([sizes[axis] for axis in names]), names)
    return jax.shard_map(
        functools.partial(body, sizes),
        mesh=fine,
        in_specs=(P(None, names), P(), P(), P(), P(names, None), P(names), P(), P()),
        out_specs=(P(names, None), P(names, None), P()),
        check_vma=False,
    )
```

```python
import functools
import math

import jax
import jax.numpy as jnp
from jax import lax
from jax.experimental import pallas as pl
from jax.experimental.pallas import tpu as pltpu
from jax.sharding import Mesh
from jax.sharding import PartitionSpec as P

EPS = 1e-06
SHARPNESS = 4.0
BITS = 28
SIDE = 128
CHUNK = 256
PROJ_COPIES = 4

ROW_AXES = ("x", "y_lo", "core")
BLK_AXES = ("z", "y_hi")
TEXT_AXES = ("x", "core")
IMAGE_AXES = ("z", "y_hi", "y_lo")


def code_sums(latent):
    bit_count = latent.shape[0]
    length = jnp.sqrt(jnp.sum(latent * latent, axis=0, keepdims=True))
    unit_code = latent / length
    root = 1.0 / math.sqrt(bit_count)
    offset = unit_code - jnp.where(latent > 0, root, -root)
    sharp = SHARPNESS * math.sqrt(bit_count) * unit_code
    size = jnp.abs(sharp)
    small = jnp.exp(-size)
    inverse = 1.0 / (1.0 + small)
    rest = small * inverse
    entropy = jnp.log1p(small) + size * rest
    prob = jnp.where(sharp > 0, inverse, rest)

    def total(values):
        return jnp.sum(jnp.sum(values, axis=1, keepdims=True), axis=0, keepdims=True)

    usage = jnp.sum(prob, axis=1, keepdims=True)
    return (total(offset * offset), total(entropy), usage)


def round_bf(values):
    return values.astype(jnp.bfloat16).astype(jnp.float32)


def gelu(x):
    inner = x * (math.sqrt(2.0 / math.pi) + (math.sqrt(2.0 / math.pi) * 0.044715) * (x * x))
    half = 0.5 * x
    return half + half * jnp.tanh(inner)


def image_kernel(
    copies,
    latent_hbm,
    post_hbm,
    proj_hbm,
    gain_ref,
    label_ref,
    block_ref,
    unit_ref,
    inv_ref,
    latent_ref,
    post_ref,
    proj_ref,
    sems,
):
    fetch_latent = pltpu.make_async_copy(latent_hbm, latent_ref, sems.at[0])
    fetch_post = pltpu.make_async_copy(post_hbm, post_ref, sems.at[1])
    depth = proj_hbm.shape[0] // PROJ_COPIES
    fetch_proj = [
        pltpu.make_async_copy(
            proj_hbm.at[pl.ds(part * depth, depth)],
            proj_ref.at[pl.ds(part * depth, depth)],
            sems.at[2 + part],
        )
        for part in range(PROJ_COPIES)
    ]
    fetch_latent.start()
    fetch_post.start()
    for fetch in fetch_proj:
        fetch.start()
    fetch_latent.wait()
    latent = latent_ref[...]
    bit_count, token_count = latent.shape
    image_count, feat_width = unit_ref.shape
    patch = token_count // image_count

    commit, entropy, usage = code_sums(latent)
    lane = lax.broadcasted_iota(jnp.int32, (bit_count, SIDE), 1)
    bit = lax.broadcasted_iota(jnp.int32, (bit_count, SIDE), 0)
    first = round_bf(usage)
    second = round_bf(usage - first)
    third = usage - first - second
    spread = jnp.where(lane == bit, first, 0.0)
    spread = jnp.where(lane == bit + 32, second, spread)
    spread = jnp.where(lane == bit + 64, third, spread)
    side = jnp.sum(spread, axis=0, keepdims=True)
    place = lax.broadcasted_iota(jnp.int32, (1, SIDE), 1)
    for at, value in ((BITS, commit), (BITS + 1, entropy)):
        first = round_bf(value)
        second = round_bf(value - first)
        third = value - first - second
        side = jnp.where(place == at, first, side)
        side = jnp.where(place == at + 32, second, side)
        side = jnp.where(place == at + 64, third, side)
    sides = []
    for i in range(image_count):
        label = label_ref[i]
        high = (label // 32).astype(jnp.float32)
        low = (label % 32).astype(jnp.float32)
        own = side if i == 0 else jnp.zeros_like(side)
        own = jnp.where(place == SIDE - 2, high, own)
        sides.append(jnp.where(place == SIDE - 1, low, own))
    codes = jnp.where(latent > 0, 1.0, -1.0)
    codes = jnp.transpose(codes, (1, 0)).astype(jnp.bfloat16)
    fetch_post.wait()
    post = post_ref[...]
    sums = []
    for first in range(0, token_count, CHUNK):
        pre_act = jnp.dot(codes[first : first + CHUNK], post, preferred_element_type=jnp.float32)
        hidden = gelu(pre_act).astype(jnp.bfloat16)
        if first == 0:
            for fetch in fetch_proj:
                fetch.wait()
        projected = jnp.dot(hidden, proj_ref[...], preferred_element_type=jnp.float32)
        square = jnp.sum(projected * projected, axis=-1, keepdims=True)
        scaled = projected * lax.rsqrt(square * (1.0 / feat_width) + EPS)
        sums.append(jnp.sum(scaled, axis=0, keepdims=True))
    steps = patch // CHUNK
    rows = [functools.reduce(jnp.add, sums[i * steps : (i + 1) * steps]) for i in range(image_count)]
    embeds = jnp.concatenate(rows, axis=0) * gain_ref[...][None, :] * (1.0 / patch)
    inverse = lax.rsqrt(jnp.sum(embeds * embeds, axis=-1, keepdims=True) + EPS)
    unit = embeds * inverse
    unit_ref[...] = unit
    inv_ref[...] = jnp.broadcast_to(inverse, inv_ref.shape)

    block = jnp.concatenate([unit, jnp.concatenate(sides, axis=0)], axis=1)
    block = block.astype(jnp.bfloat16)
    for member in range(copies):
        block_ref[member] = block


def embed_images(latent, w_post, w_proj, gain, labels, copies):
    image_count = labels.shape[0]
    feat_width = w_proj.shape[1]
    vmem = pl.BlockSpec(memory_space=pltpu.VMEM)
    hbm = pl.BlockSpec(memory_space=pl.ANY)
    return pl.pallas_call(
        functools.partial(image_kernel, copies),
        out_shape=(
            jax.ShapeDtypeStruct((copies, image_count, feat_width + SIDE), jnp.bfloat16),
            jax.ShapeDtypeStruct((image_count, feat_width), jnp.float32),
            jax.ShapeDtypeStruct((image_count, 128), jnp.float32),
        ),
        in_specs=[hbm, hbm, hbm, vmem, pl.BlockSpec(memory_space=pltpu.SMEM)],
        out_specs=(vmem, vmem, vmem),
        scratch_shapes=[
            pltpu.VMEM(latent.shape, latent.dtype),
            pltpu.VMEM(w_post.shape, w_post.dtype),
            pltpu.VMEM(w_proj.shape, w_proj.dtype),
            pltpu.SemaphoreType.DMA((2 + PROJ_COPIES,)),
        ],
        compiler_params=pltpu.CompilerParams(vmem_limit_bytes=56 * 1024 * 1024),
        cost_estimate=pl.CostEstimate(
            flops=2_200_000_000, bytes_accessed=1_800_000, transcendentals=1_100_000
        ),
        name="embed_images",
    )(latent, w_post, w_proj, gain, labels)


def unit_rows(values):
    inverse = lax.rsqrt(jnp.sum(values * values, axis=-1, keepdims=True) + EPS)
    return (values * inverse, inverse)


def tangent(direction, unit, inverse):
    return (direction - unit * jnp.sum(unit * direction, axis=-1, keepdims=True)) * inverse


def text_kernel(text_ref, block_ref, unit_ref, inv_ref):
    unit, inverse = unit_rows(text_ref[...].astype(jnp.float32))
    unit_ref[...] = unit
    inv_ref[...] = jnp.broadcast_to(inverse, inv_ref.shape)
    unit = unit.astype(jnp.bfloat16)
    for member in range(block_ref.shape[0]):
        block_ref[member] = unit


def text_blocks(text_embed, copies):
    rows = text_embed.shape[0]
    vmem = pl.BlockSpec(memory_space=pltpu.VMEM)
    return pl.pallas_call(
        text_kernel,
        out_shape=(
            jax.ShapeDtypeStruct((copies,) + text_embed.shape, jnp.bfloat16),
            jax.ShapeDtypeStruct(text_embed.shape, jnp.float32),
            jax.ShapeDtypeStruct((rows, 128), jnp.float32),
        ),
        in_specs=[vmem],
        out_specs=(vmem, vmem, vmem),
        name="text_blocks",
    )(text_embed)


def finish_kernel(
    total_tokens, chip_ref, moved_ref, unit_ref, inv_ref, scale_ref, grad_ref, scalar_ref
):
    pair_count, feat_width = unit_ref.shape
    total = chip_ref[:pair_count] + moved_ref[...]
    direction = scale_ref[0] * total[:, :feat_width]
    grad_ref[...] = tangent(direction, unit_ref[...], inv_ref[...][:, :1])
    side = total[:1, feat_width:]
    means = side[:, :32] + side[:, 32:64] + side[:, 64:96]
    means = means * (1.0 / total_tokens)
    place = lax.broadcasted_iota(jnp.int32, means.shape, 1)
    usage = jnp.where(place < BITS, means, 0.5)
    spread = -(usage * jnp.log(usage) + (1.0 - usage) * jnp.log(1.0 - usage))
    scalar_ref[0] = jnp.sum(jnp.where(place == BITS, means, 0.0))
    scalar_ref[1] = jnp.sum(jnp.where(place == BITS + 1, means, 0.0))
    scalar_ref[2] = jnp.sum(jnp.where(place < BITS, spread, 0.0))


def finish_text(chip_part, moved, text_unit, text_inv, logit_scale, total_tokens):
    vmem = pl.BlockSpec(memory_space=pltpu.VMEM)
    smem = pl.BlockSpec(memory_space=pltpu.SMEM)
    return pl.pallas_call(
        functools.partial(finish_kernel, total_tokens),
        out_shape=(
            jax.ShapeDtypeStruct(text_unit.shape, jnp.float32),
            jax.ShapeDtypeStruct((3,), jnp.float32),
        ),
        in_specs=[vmem, vmem, vmem, vmem, smem],
        out_specs=(vmem, smem),
        name="finish_text",
    )(chip_part, moved, text_unit, text_inv, logit_scale)


def swap_cores(block):
    return lax.ppermute(block, "core", [(0, 1), (1, 0)])


def along_x(block, distance, count):
    return lax.ppermute(block, "x", [(i, (i + distance) % count) for i in range(count)])


def from_here(members, n_x):
    members = members.reshape((n_x, 2) + members.shape[1:])
    here = lax.axis_index("x")
    other = lax.axis_index("core") == 1
    turned = [
        lax.dynamic_index_in_dim(members, (here + distance) % n_x, 0, keepdims=False)
        for distance in range(n_x)
    ]
    return [
        jnp.where(other, block[1 - core], block[core]) for block in turned for core in range(2)
    ]


def body(sizes, latent, w_post, w_proj, gain, text_embed, labels, logit_scale, logit_bias):
    pair_count, feat_width = text_embed.shape
    n_x = sizes["x"]
    n_image = math.prod(sizes[axis] for axis in IMAGE_AXES)
    n_text = math.prod(sizes[axis] for axis in TEXT_AXES)
    text_count = n_text * pair_count
    chip_count = 2 * pair_count
    total_tokens = latent.shape[1] * math.prod(sizes.values())
    scale_value = logit_scale[0]
    bias_value = logit_bias[0]

    text_block, text_unit, text_inv = text_blocks(text_embed, n_text)
    group_text = lax.all_to_all(text_block, TEXT_AXES, 0, 0)
    group_text = jnp.concatenate(from_here(group_text, n_x), axis=0)

    image_block, image_unit, image_inv = embed_images(
        latent, w_post, w_proj, gain, labels, n_image
    )
    group_block = lax.all_to_all(image_block, IMAGE_AXES, 0, 0)
    group_block = group_block.reshape(n_image * pair_count, feat_width + SIDE)
    group_image = group_block[:, :feat_width]
    group_side = group_block[:, feat_width:].astype(jnp.float32)
    group_labels = (group_side[:, SIDE - 2] * 32.0 + group_side[:, SIDE - 1]).astype(jnp.int32)
    group_sums = jnp.sum(group_side, axis=0, keepdims=True)

    row_size = sizes["y_lo"] * sizes["core"]
    blk_size = sizes["z"] * sizes["y_hi"]
    place = jnp.arange(text_count, dtype=jnp.int32)
    text_x = (lax.axis_index("x") + place // chip_count) % n_x
    text_core = lax.axis_index("core") ^ (place // pair_count % 2)
    text_row = text_x * row_size + lax.axis_index("y_lo") * sizes["core"] + text_core
    text_blk = lax.axis_index("z") * sizes["y_hi"] + lax.axis_index("y_hi")
    text_ids = (text_row * blk_size + text_blk) * pair_count + place % pair_count

    products = jnp.dot(group_image, group_text.T, preferred_element_type=jnp.float32)
    pair_sign = jnp.where(
        group_labels[:, None] == text_ids[None, :], jnp.float32(1.0), jnp.float32(-1.0)
    )
    margin = pair_sign * (scale_value * products + bias_value)
    grad_bf = (-pair_sign * jax.nn.sigmoid(-margin)).astype(jnp.bfloat16)
    image_part = jnp.dot(grad_bf, group_text, preferred_element_type=jnp.float32)
    image_part = image_part.reshape(n_image, pair_count, feat_width)
    image_part = lax.all_to_all(image_part, IMAGE_AXES, 0, 0)

    text_part = jnp.dot(grad_bf.T, group_image, preferred_element_type=jnp.float32)
    text_part = jnp.concatenate(
        [text_part, jnp.broadcast_to(group_sums, (text_count, SIDE))], axis=1
    )
    chip_part = text_part[:chip_count]
    for distance in range(1, n_x):
        rows = text_part[distance * chip_count : (distance + 1) * chip_count]
        chip_part = chip_part + along_x(rows, distance, n_x)
    moved = swap_cores(chip_part[pair_count:])

    image_dir = scale_value * jnp.sum(image_part, axis=0)
    grad_image = tangent(image_dir, image_unit, image_inv[:, :1])
    grad_image, moved = lax.optimization_barrier((grad_image, moved))
    grad_text, scalars = finish_text(
        chip_part, moved, text_unit, text_inv, logit_scale, total_tokens
    )
    return (grad_image, grad_text, scalars)


def solution(mesh):
    sizes = {"x": 4, "y_lo": 2, "core": 2, "z": 8, "y_hi": 4}
    names = ROW_AXES + BLK_AXES
    fine = Mesh(mesh.devices.reshape([sizes[axis] for axis in names]), names)
    return jax.shard_map(
        functools.partial(body, sizes),
        mesh=fine,
        in_specs=(P(None, names), P(), P(), P(), P(names, None), P(names), P(), P()),
        out_specs=(P(names, None), P(names, None), P()),
        check_vma=False,
    )
```

```python
import functools
import math

import jax
import jax.numpy as jnp
from jax import lax
from jax.experimental import pallas as pl
from jax.experimental.pallas import tpu as pltpu
from jax.sharding import Mesh
from jax.sharding import PartitionSpec as P

EPS = 1e-06
SHARPNESS = 4.0
BITS = 28
SIDE = 128
CHUNK = 256
PROJ_COPIES = 4

ROW_AXES = ("x", "y_lo", "core")
BLK_AXES = ("z", "y_hi")
TEXT_AXES = ("x", "core")
IMAGE_AXES = ("z", "y_hi", "y_lo")


def code_sums(latent):
    bit_count = latent.shape[0]
    length = jnp.sqrt(jnp.sum(latent * latent, axis=0, keepdims=True))
    unit_code = latent / length
    root = 1.0 / math.sqrt(bit_count)
    offset = unit_code - jnp.where(latent > 0, root, -root)
    sharp = SHARPNESS * math.sqrt(bit_count) * unit_code
    size = jnp.abs(sharp)
    small = jnp.exp(-size)
    inverse = 1.0 / (1.0 + small)
    rest = small * inverse
    entropy = jnp.log1p(small) + size * rest
    prob = jnp.where(sharp > 0, inverse, rest)

    def total(values):
        return jnp.sum(jnp.sum(values, axis=1, keepdims=True), axis=0, keepdims=True)

    usage = jnp.sum(prob, axis=1, keepdims=True)
    return (total(offset * offset), total(entropy), usage)


def round_bf(values):
    return values.astype(jnp.bfloat16).astype(jnp.float32)


def gelu(x):
    inner = x * (math.sqrt(2.0 / math.pi) + (math.sqrt(2.0 / math.pi) * 0.044715) * (x * x))
    half = 0.5 * x
    return half + half * jnp.tanh(inner)


def image_kernel(
    copies,
    latent_hbm,
    post_hbm,
    proj_hbm,
    gain_ref,
    label_ref,
    block_ref,
    unit_ref,
    inv_ref,
    latent_ref,
    post_ref,
    proj_ref,
    sems,
):
    fetch_latent = pltpu.make_async_copy(latent_hbm, latent_ref, sems.at[0])
    fetch_post = pltpu.make_async_copy(post_hbm, post_ref, sems.at[1])
    depth = proj_hbm.shape[0] // PROJ_COPIES
    fetch_proj = [
        pltpu.make_async_copy(
            proj_hbm.at[pl.ds(part * depth, depth)],
            proj_ref.at[pl.ds(part * depth, depth)],
            sems.at[2 + part],
        )
        for part in range(PROJ_COPIES)
    ]
    fetch_latent.start()
    fetch_post.start()
    for fetch in fetch_proj:
        fetch.start()
    fetch_latent.wait()
    latent = latent_ref[...]
    bit_count, token_count = latent.shape
    image_count, feat_width = unit_ref.shape
    patch = token_count // image_count

    commit, entropy, usage = code_sums(latent)
    lane = lax.broadcasted_iota(jnp.int32, (bit_count, SIDE), 1)
    bit = lax.broadcasted_iota(jnp.int32, (bit_count, SIDE), 0)
    first = round_bf(usage)
    second = round_bf(usage - first)
    third = usage - first - second
    spread = jnp.where(lane == bit, first, 0.0)
    spread = jnp.where(lane == bit + 32, second, spread)
    spread = jnp.where(lane == bit + 64, third, spread)
    side = jnp.sum(spread, axis=0, keepdims=True)
    place = lax.broadcasted_iota(jnp.int32, (1, SIDE), 1)
    for at, value in ((BITS, commit), (BITS + 1, entropy)):
        first = round_bf(value)
        second = round_bf(value - first)
        third = value - first - second
        side = jnp.where(place == at, first, side)
        side = jnp.where(place == at + 32, second, side)
        side = jnp.where(place == at + 64, third, side)
    sides = []
    for i in range(image_count):
        label = label_ref[i]
        high = (label // 32).astype(jnp.float32)
        low = (label % 32).astype(jnp.float32)
        own = side if i == 0 else jnp.zeros_like(side)
        own = jnp.where(place == SIDE - 2, high, own)
        sides.append(jnp.where(place == SIDE - 1, low, own))
    codes = jnp.where(latent > 0, 1.0, -1.0)
    codes = jnp.transpose(codes, (1, 0)).astype(jnp.bfloat16)
    fetch_post.wait()
    post = post_ref[...]
    sums = []
    for first in range(0, token_count, CHUNK):
        pre_act = jnp.dot(codes[first : first + CHUNK], post, preferred_element_type=jnp.float32)
        hidden = gelu(pre_act).astype(jnp.bfloat16)
        if first == 0:
            for fetch in fetch_proj:
                fetch.wait()
        projected = jnp.dot(hidden, proj_ref[...], preferred_element_type=jnp.float32)
        square = jnp.sum(projected * projected, axis=-1, keepdims=True)
        scaled = projected * lax.rsqrt(square * (1.0 / feat_width) + EPS)
        sums.append(jnp.sum(scaled, axis=0, keepdims=True))
    steps = patch // CHUNK
    rows = [functools.reduce(jnp.add, sums[i * steps : (i + 1) * steps]) for i in range(image_count)]
    embeds = jnp.concatenate(rows, axis=0) * gain_ref[...][None, :] * (1.0 / patch)
    inverse = lax.rsqrt(jnp.sum(embeds * embeds, axis=-1, keepdims=True) + EPS)
    unit = embeds * inverse
    unit_ref[...] = unit
    inv_ref[...] = jnp.broadcast_to(inverse, inv_ref.shape)

    block = jnp.concatenate([unit, jnp.concatenate(sides, axis=0)], axis=1)
    block = block.astype(jnp.bfloat16)
    for member in range(copies):
        block_ref[member] = block


def embed_images(latent, w_post, w_proj, gain, labels, copies):
    image_count = labels.shape[0]
    feat_width = w_proj.shape[1]
    vmem = pl.BlockSpec(memory_space=pltpu.VMEM)
    hbm = pl.BlockSpec(memory_space=pl.ANY)
    return pl.pallas_call(
        functools.partial(image_kernel, copies),
        out_shape=(
            jax.ShapeDtypeStruct((copies, image_count, feat_width + SIDE), jnp.bfloat16),
            jax.ShapeDtypeStruct((image_count, feat_width), jnp.float32),
            jax.ShapeDtypeStruct((image_count, 128), jnp.float32),
        ),
        in_specs=[hbm, hbm, hbm, vmem, pl.BlockSpec(memory_space=pltpu.SMEM)],
        out_specs=(vmem, vmem, vmem),
        scratch_shapes=[
            pltpu.VMEM(latent.shape, latent.dtype),
            pltpu.VMEM(w_post.shape, w_post.dtype),
            pltpu.VMEM(w_proj.shape, w_proj.dtype),
            pltpu.SemaphoreType.DMA((2 + PROJ_COPIES,)),
        ],
        compiler_params=pltpu.CompilerParams(vmem_limit_bytes=56 * 1024 * 1024),
        cost_estimate=pl.CostEstimate(
            flops=2_200_000_000, bytes_accessed=1_800_000, transcendentals=1_100_000
        ),
        name="embed_images",
    )(latent, w_post, w_proj, gain, labels)


def unit_rows(values):
    inverse = lax.rsqrt(jnp.sum(values * values, axis=-1, keepdims=True) + EPS)
    return (values * inverse, inverse)


def tangent(direction, unit, inverse):
    return (direction - unit * jnp.sum(unit * direction, axis=-1, keepdims=True)) * inverse


def text_kernel(text_ref, block_ref, unit_ref, inv_ref):
    unit, inverse = unit_rows(text_ref[...].astype(jnp.float32))
    unit_ref[...] = unit
    inv_ref[...] = jnp.broadcast_to(inverse, inv_ref.shape)
    unit = unit.astype(jnp.bfloat16)
    for member in range(block_ref.shape[0]):
        block_ref[member] = unit


def text_blocks(text_embed, copies):
    rows = text_embed.shape[0]
    vmem = pl.BlockSpec(memory_space=pltpu.VMEM)
    return pl.pallas_call(
        text_kernel,
        out_shape=(
            jax.ShapeDtypeStruct((copies,) + text_embed.shape, jnp.bfloat16),
            jax.ShapeDtypeStruct(text_embed.shape, jnp.float32),
            jax.ShapeDtypeStruct((rows, 128), jnp.float32),
        ),
        in_specs=[vmem],
        out_specs=(vmem, vmem, vmem),
        name="text_blocks",
    )(text_embed)


def finish_kernel(
    total_tokens,
    chip_any,
    moved_any,
    unit_ref,
    inv_ref,
    scale_ref,
    grad_ref,
    scalar_ref,
    chip_ref,
    moved_ref,
    sems,
):
    pair_count, feat_width = unit_ref.shape
    fetch_chip = pltpu.make_async_copy(chip_any, chip_ref, sems.at[0])
    fetch_moved = pltpu.make_async_copy(moved_any, moved_ref, sems.at[1])
    fetch_chip.start()
    fetch_moved.start()
    fetch_chip.wait()
    fetch_moved.wait()
    total = chip_ref[...][:pair_count] + moved_ref[...]
    direction = scale_ref[0] * total[:, :feat_width]
    grad_ref[...] = tangent(direction, unit_ref[...], inv_ref[...][:, :1])
    side = total[:1, feat_width:]
    means = side[:, :32] + side[:, 32:64] + side[:, 64:96]
    means = means * (1.0 / total_tokens)
    place = lax.broadcasted_iota(jnp.int32, means.shape, 1)
    usage = jnp.where(place < BITS, means, 0.5)
    spread = -(usage * jnp.log(usage) + (1.0 - usage) * jnp.log(1.0 - usage))
    scalar_ref[0] = jnp.sum(jnp.where(place == BITS, means, 0.0))
    scalar_ref[1] = jnp.sum(jnp.where(place == BITS + 1, means, 0.0))
    scalar_ref[2] = jnp.sum(jnp.where(place < BITS, spread, 0.0))


def finish_text(chip_part, moved, text_unit, text_inv, logit_scale, total_tokens):
    vmem = pl.BlockSpec(memory_space=pltpu.VMEM)
    smem = pl.BlockSpec(memory_space=pltpu.SMEM)
    where = pl.BlockSpec(memory_space=pl.ANY)
    return pl.pallas_call(
        functools.partial(finish_kernel, total_tokens),
        out_shape=(
            jax.ShapeDtypeStruct(text_unit.shape, jnp.float32),
            jax.ShapeDtypeStruct((3,), jnp.float32),
        ),
        in_specs=[where, where, vmem, vmem, smem],
        out_specs=(vmem, smem),
        scratch_shapes=[
            pltpu.VMEM(chip_part.shape, chip_part.dtype),
            pltpu.VMEM(moved.shape, moved.dtype),
            pltpu.SemaphoreType.DMA((2,)),
        ],
        name="finish_text",
    )(chip_part, moved, text_unit, text_inv, logit_scale)


def swap_cores(block):
    return lax.ppermute(block, "core", [(0, 1), (1, 0)])


def along_x(block, distance, count):
    return lax.ppermute(block, "x", [(i, (i + distance) % count) for i in range(count)])


def from_here(members, n_x):
    members = members.reshape((n_x, 2) + members.shape[1:])
    here = lax.axis_index("x")
    other = lax.axis_index("core") == 1
    turned = [
        lax.dynamic_index_in_dim(members, (here + distance) % n_x, 0, keepdims=False)
        for distance in range(n_x)
    ]
    return [
        jnp.where(other, block[1 - core], block[core]) for block in turned for core in range(2)
    ]


def body(sizes, latent, w_post, w_proj, gain, text_embed, labels, logit_scale, logit_bias):
    pair_count, feat_width = text_embed.shape
    n_x = sizes["x"]
    n_image = math.prod(sizes[axis] for axis in IMAGE_AXES)
    n_text = math.prod(sizes[axis] for axis in TEXT_AXES)
    text_count = n_text * pair_count
    chip_count = 2 * pair_count
    total_tokens = latent.shape[1] * math.prod(sizes.values())
    scale_value = logit_scale[0]
    bias_value = logit_bias[0]

    text_block, text_unit, text_inv = text_blocks(text_embed, n_text)
    group_text = lax.all_to_all(text_block, TEXT_AXES, 0, 0)
    group_text = jnp.concatenate(from_here(group_text, n_x), axis=0)

    image_block, image_unit, image_inv = embed_images(
        latent, w_post, w_proj, gain, labels, n_image
    )
    group_block = lax.all_to_all(image_block, IMAGE_AXES, 0, 0)
    group_block = group_block.reshape(n_image * pair_count, feat_width + SIDE)
    group_image = group_block[:, :feat_width]
    group_side = group_block[:, feat_width:].astype(jnp.float32)
    group_labels = (group_side[:, SIDE - 2] * 32.0 + group_side[:, SIDE - 1]).astype(jnp.int32)
    group_sums = jnp.sum(group_side, axis=0, keepdims=True)

    row_size = sizes["y_lo"] * sizes["core"]
    blk_size = sizes["z"] * sizes["y_hi"]
    place = jnp.arange(text_count, dtype=jnp.int32)
    text_x = (lax.axis_index("x") + place // chip_count) % n_x
    text_core = lax.axis_index("core") ^ (place // pair_count % 2)
    text_row = text_x * row_size + lax.axis_index("y_lo") * sizes["core"] + text_core
    text_blk = lax.axis_index("z") * sizes["y_hi"] + lax.axis_index("y_hi")
    text_ids = (text_row * blk_size + text_blk) * pair_count + place % pair_count

    products = jnp.dot(group_image, group_text.T, preferred_element_type=jnp.float32)
    pair_sign = jnp.where(
        group_labels[:, None] == text_ids[None, :], jnp.float32(1.0), jnp.float32(-1.0)
    )
    margin = pair_sign * (scale_value * products + bias_value)
    grad_bf = (-pair_sign * jax.nn.sigmoid(-margin)).astype(jnp.bfloat16)
    image_part = jnp.dot(grad_bf, group_text, preferred_element_type=jnp.float32)
    image_part = image_part.reshape(n_image, pair_count, feat_width)
    image_part = lax.all_to_all(image_part, IMAGE_AXES, 0, 0)

    text_part = jnp.dot(grad_bf.T, group_image, preferred_element_type=jnp.float32)
    text_part = jnp.concatenate(
        [text_part, jnp.broadcast_to(group_sums, (text_count, SIDE))], axis=1
    )
    chip_part = text_part[:chip_count]
    for distance in range(1, n_x):
        rows = text_part[distance * chip_count : (distance + 1) * chip_count]
        chip_part = chip_part + along_x(rows, distance, n_x)
    moved = swap_cores(chip_part[pair_count:])

    image_dir = scale_value * jnp.sum(image_part, axis=0)
    grad_image = tangent(image_dir, image_unit, image_inv[:, :1])
    grad_image, moved = lax.optimization_barrier((grad_image, moved))
    grad_text, scalars = finish_text(
        chip_part, moved, text_unit, text_inv, logit_scale, total_tokens
    )
    return (grad_image, grad_text, scalars)


def solution(mesh):
    sizes = {"x": 4, "y_lo": 2, "core": 2, "z": 8, "y_hi": 4}
    names = ROW_AXES + BLK_AXES
    fine = Mesh(mesh.devices.reshape([sizes[axis] for axis in names]), names)
    return jax.shard_map(
        functools.partial(body, sizes),
        mesh=fine,
        in_specs=(P(None, names), P(), P(), P(), P(names, None), P(names), P(), P()),
        out_specs=(P(names, None), P(names, None), P()),
        check_vma=False,
    )
```

```python
import functools
import math

import jax
import jax.numpy as jnp
from jax import lax
from jax.experimental import pallas as pl
from jax.experimental.pallas import tpu as pltpu
from jax.sharding import Mesh
from jax.sharding import PartitionSpec as P

EPS = 1e-06
SHARPNESS = 4.0
BITS = 28
SIDE = 128
CHUNK = 512
PROJ_COPIES = 4

ROW_AXES = ("x", "y_lo", "core")
BLK_AXES = ("z", "y_hi")
TEXT_AXES = ("x", "core")
IMAGE_AXES = ("z", "y_hi", "y_lo")


def code_sums(latent):
    bit_count = latent.shape[0]
    length = jnp.sqrt(jnp.sum(latent * latent, axis=0, keepdims=True))
    unit_code = latent / length
    root = 1.0 / math.sqrt(bit_count)
    offset = unit_code - jnp.where(latent > 0, root, -root)
    sharp = SHARPNESS * math.sqrt(bit_count) * unit_code
    size = jnp.abs(sharp)
    small = jnp.exp(-size)
    inverse = 1.0 / (1.0 + small)
    rest = small * inverse
    entropy = jnp.log1p(small) + size * rest
    prob = jnp.where(sharp > 0, inverse, rest)

    def total(values):
        return jnp.sum(jnp.sum(values, axis=1, keepdims=True), axis=0, keepdims=True)

    usage = jnp.sum(prob, axis=1, keepdims=True)
    return (total(offset * offset), total(entropy), usage)


def round_bf(values):
    return values.astype(jnp.bfloat16).astype(jnp.float32)


def gelu(x):
    inner = x * (math.sqrt(2.0 / math.pi) + (math.sqrt(2.0 / math.pi) * 0.044715) * (x * x))
    half = 0.5 * x
    return half + half * jnp.tanh(inner)


def image_kernel(
    copies,
    latent_hbm,
    post_hbm,
    proj_hbm,
    gain_ref,
    label_ref,
    block_ref,
    unit_ref,
    inv_ref,
    latent_ref,
    post_ref,
    proj_ref,
    sems,
):
    fetch_latent = pltpu.make_async_copy(latent_hbm, latent_ref, sems.at[0])
    fetch_post = pltpu.make_async_copy(post_hbm, post_ref, sems.at[1])
    depth = proj_hbm.shape[0] // PROJ_COPIES
    fetch_proj = [
        pltpu.make_async_copy(
            proj_hbm.at[pl.ds(part * depth, depth)],
            proj_ref.at[pl.ds(part * depth, depth)],
            sems.at[2 + part],
        )
        for part in range(PROJ_COPIES)
    ]
    fetch_latent.start()
    fetch_post.start()
    for fetch in fetch_proj:
        fetch.start()
    fetch_latent.wait()
    latent = latent_ref[...]
    bit_count, token_count = latent.shape
    image_count, feat_width = unit_ref.shape
    patch = token_count // image_count

    commit, entropy, usage = code_sums(latent)
    lane = lax.broadcasted_iota(jnp.int32, (bit_count, SIDE), 1)
    bit = lax.broadcasted_iota(jnp.int32, (bit_count, SIDE), 0)
    first = round_bf(usage)
    second = round_bf(usage - first)
    third = usage - first - second
    spread = jnp.where(lane == bit, first, 0.0)
    spread = jnp.where(lane == bit + 32, second, spread)
    spread = jnp.where(lane == bit + 64, third, spread)
    side = jnp.sum(spread, axis=0, keepdims=True)
    place = lax.broadcasted_iota(jnp.int32, (1, SIDE), 1)
    for at, value in ((BITS, commit), (BITS + 1, entropy)):
        first = round_bf(value)
        second = round_bf(value - first)
        third = value - first - second
        side = jnp.where(place == at, first, side)
        side = jnp.where(place == at + 32, second, side)
        side = jnp.where(place == at + 64, third, side)
    sides = []
    for i in range(image_count):
        label = label_ref[i]
        high = (label // 32).astype(jnp.float32)
        low = (label % 32).astype(jnp.float32)
        own = side if i == 0 else jnp.zeros_like(side)
        own = jnp.where(place == SIDE - 2, high, own)
        sides.append(jnp.where(place == SIDE - 1, low, own))
    codes = jnp.where(latent > 0, 1.0, -1.0)
    codes = jnp.transpose(codes, (1, 0)).astype(jnp.bfloat16)
    fetch_post.wait()
    post = post_ref[...]
    sums = []
    for first in range(0, token_count, CHUNK):
        pre_act = jnp.dot(codes[first : first + CHUNK], post, preferred_element_type=jnp.float32)
        hidden = gelu(pre_act).astype(jnp.bfloat16)
        if first == 0:
            for fetch in fetch_proj:
                fetch.wait()
        projected = jnp.dot(hidden, proj_ref[...], preferred_element_type=jnp.float32)
        square = jnp.sum(projected * projected, axis=-1, keepdims=True)
        scaled = projected * lax.rsqrt(square * (1.0 / feat_width) + EPS)
        sums.append(jnp.sum(scaled, axis=0, keepdims=True))
    steps = patch // CHUNK
    rows = [functools.reduce(jnp.add, sums[i * steps : (i + 1) * steps]) for i in range(image_count)]
    embeds = jnp.concatenate(rows, axis=0) * gain_ref[...][None, :] * (1.0 / patch)
    inverse = lax.rsqrt(jnp.sum(embeds * embeds, axis=-1, keepdims=True) + EPS)
    unit = embeds * inverse
    unit_ref[...] = unit
    inv_ref[...] = jnp.broadcast_to(inverse, inv_ref.shape)

    block = jnp.concatenate([unit, jnp.concatenate(sides, axis=0)], axis=1)
    block = block.astype(jnp.bfloat16)
    for member in range(copies):
        block_ref[member] = block


def embed_images(latent, w_post, w_proj, gain, labels, copies):
    image_count = labels.shape[0]
    feat_width = w_proj.shape[1]
    vmem = pl.BlockSpec(memory_space=pltpu.VMEM)
    hbm = pl.BlockSpec(memory_space=pl.ANY)
    return pl.pallas_call(
        functools.partial(image_kernel, copies),
        out_shape=(
            jax.ShapeDtypeStruct((copies, image_count, feat_width + SIDE), jnp.bfloat16),
            jax.ShapeDtypeStruct((image_count, feat_width), jnp.float32),
            jax.ShapeDtypeStruct((image_count, 128), jnp.float32),
        ),
        in_specs=[hbm, hbm, hbm, vmem, pl.BlockSpec(memory_space=pltpu.SMEM)],
        out_specs=(vmem, vmem, vmem),
        scratch_shapes=[
            pltpu.VMEM(latent.shape, latent.dtype),
            pltpu.VMEM(w_post.shape, w_post.dtype),
            pltpu.VMEM(w_proj.shape, w_proj.dtype),
            pltpu.SemaphoreType.DMA((2 + PROJ_COPIES,)),
        ],
        compiler_params=pltpu.CompilerParams(vmem_limit_bytes=56 * 1024 * 1024),
        cost_estimate=pl.CostEstimate(
            flops=2_200_000_000, bytes_accessed=1_800_000, transcendentals=1_100_000
        ),
        name="embed_images",
    )(latent, w_post, w_proj, gain, labels)


def unit_rows(values):
    inverse = lax.rsqrt(jnp.sum(values * values, axis=-1, keepdims=True) + EPS)
    return (values * inverse, inverse)


def tangent(direction, unit, inverse):
    return (direction - unit * jnp.sum(unit * direction, axis=-1, keepdims=True)) * inverse


def text_kernel(text_ref, block_ref, unit_ref, inv_ref):
    unit, inverse = unit_rows(text_ref[...].astype(jnp.float32))
    unit_ref[...] = unit
    inv_ref[...] = jnp.broadcast_to(inverse, inv_ref.shape)
    unit = unit.astype(jnp.bfloat16)
    for member in range(block_ref.shape[0]):
        block_ref[member] = unit


def text_blocks(text_embed, copies):
    rows = text_embed.shape[0]
    vmem = pl.BlockSpec(memory_space=pltpu.VMEM)
    return pl.pallas_call(
        text_kernel,
        out_shape=(
            jax.ShapeDtypeStruct((copies,) + text_embed.shape, jnp.bfloat16),
            jax.ShapeDtypeStruct(text_embed.shape, jnp.float32),
            jax.ShapeDtypeStruct((rows, 128), jnp.float32),
        ),
        in_specs=[vmem],
        out_specs=(vmem, vmem, vmem),
        name="text_blocks",
    )(text_embed)


def finish_kernel(
    total_tokens, chip_ref, moved_ref, unit_ref, inv_ref, scale_ref, grad_ref, scalar_ref
):
    pair_count, feat_width = unit_ref.shape
    total = chip_ref[:pair_count] + moved_ref[...]
    direction = scale_ref[0] * total[:, :feat_width]
    grad_ref[...] = tangent(direction, unit_ref[...], inv_ref[...][:, :1])
    side = total[:1, feat_width:]
    means = side[:, :32] + side[:, 32:64] + side[:, 64:96]
    means = means * (1.0 / total_tokens)
    place = lax.broadcasted_iota(jnp.int32, means.shape, 1)
    usage = jnp.where(place < BITS, means, 0.5)
    spread = -(usage * jnp.log(usage) + (1.0 - usage) * jnp.log(1.0 - usage))
    scalar_ref[0] = jnp.sum(jnp.where(place == BITS, means, 0.0))
    scalar_ref[1] = jnp.sum(jnp.where(place == BITS + 1, means, 0.0))
    scalar_ref[2] = jnp.sum(jnp.where(place < BITS, spread, 0.0))


def finish_text(chip_part, moved, text_unit, text_inv, logit_scale, total_tokens):
    vmem = pl.BlockSpec(memory_space=pltpu.VMEM)
    smem = pl.BlockSpec(memory_space=pltpu.SMEM)
    return pl.pallas_call(
        functools.partial(finish_kernel, total_tokens),
        out_shape=(
            jax.ShapeDtypeStruct(text_unit.shape, jnp.float32),
            jax.ShapeDtypeStruct((3,), jnp.float32),
        ),
        in_specs=[vmem, vmem, vmem, vmem, smem],
        out_specs=(vmem, smem),
        name="finish_text",
    )(chip_part, moved, text_unit, text_inv, logit_scale)


def swap_cores(block):
    return lax.ppermute(block, "core", [(0, 1), (1, 0)])


def along_x(block, distance, count):
    return lax.ppermute(block, "x", [(i, (i + distance) % count) for i in range(count)])


def from_here(members, n_x):
    members = members.reshape((n_x, 2) + members.shape[1:])
    here = lax.axis_index("x")
    other = lax.axis_index("core") == 1
    turned = [
        lax.dynamic_index_in_dim(members, (here + distance) % n_x, 0, keepdims=False)
        for distance in range(n_x)
    ]
    return [
        jnp.where(other, block[1 - core], block[core]) for block in turned for core in range(2)
    ]


def body(sizes, latent, w_post, w_proj, gain, text_embed, labels, logit_scale, logit_bias):
    pair_count, feat_width = text_embed.shape
    n_x = sizes["x"]
    n_image = math.prod(sizes[axis] for axis in IMAGE_AXES)
    n_text = math.prod(sizes[axis] for axis in TEXT_AXES)
    text_count = n_text * pair_count
    chip_count = 2 * pair_count
    total_tokens = latent.shape[1] * math.prod(sizes.values())
    scale_value = logit_scale[0]
    bias_value = logit_bias[0]

    text_block, text_unit, text_inv = text_blocks(text_embed, n_text)
    group_text = lax.all_to_all(text_block, TEXT_AXES, 0, 0)
    group_text = jnp.concatenate(from_here(group_text, n_x), axis=0)

    image_block, image_unit, image_inv = embed_images(
        latent, w_post, w_proj, gain, labels, n_image
    )
    group_block = lax.all_to_all(image_block, IMAGE_AXES, 0, 0)
    group_block = group_block.reshape(n_image * pair_count, feat_width + SIDE)
    group_image = group_block[:, :feat_width]
    group_side = group_block[:, feat_width:].astype(jnp.float32)
    group_labels = (group_side[:, SIDE - 2] * 32.0 + group_side[:, SIDE - 1]).astype(jnp.int32)
    group_sums = jnp.sum(group_side, axis=0, keepdims=True)

    row_size = sizes["y_lo"] * sizes["core"]
    blk_size = sizes["z"] * sizes["y_hi"]
    place = jnp.arange(text_count, dtype=jnp.int32)
    text_x = (lax.axis_index("x") + place // chip_count) % n_x
    text_core = lax.axis_index("core") ^ (place // pair_count % 2)
    text_row = text_x * row_size + lax.axis_index("y_lo") * sizes["core"] + text_core
    text_blk = lax.axis_index("z") * sizes["y_hi"] + lax.axis_index("y_hi")
    text_ids = (text_row * blk_size + text_blk) * pair_count + place % pair_count

    products = jnp.dot(group_image, group_text.T, preferred_element_type=jnp.float32)
    pair_sign = jnp.where(
        group_labels[:, None] == text_ids[None, :], jnp.float32(1.0), jnp.float32(-1.0)
    )
    margin = pair_sign * (scale_value * products + bias_value)
    grad_bf = (-pair_sign * jax.nn.sigmoid(-margin)).astype(jnp.bfloat16)
    image_part = jnp.dot(grad_bf, group_text, preferred_element_type=jnp.float32)
    image_part = image_part.reshape(n_image, pair_count, feat_width)
    image_part = lax.all_to_all(image_part, IMAGE_AXES, 0, 0)

    text_part = jnp.dot(grad_bf.T, group_image, preferred_element_type=jnp.float32)
    text_part = jnp.concatenate(
        [text_part, jnp.broadcast_to(group_sums, (text_count, SIDE))], axis=1
    )
    chip_part = text_part[:chip_count]
    for distance in range(1, n_x):
        rows = text_part[distance * chip_count : (distance + 1) * chip_count]
        chip_part = chip_part + along_x(rows, distance, n_x)
    moved = swap_cores(chip_part[pair_count:])

    image_dir = scale_value * jnp.sum(image_part, axis=0)
    grad_image = tangent(image_dir, image_unit, image_inv[:, :1])
    grad_image, moved = lax.optimization_barrier((grad_image, moved))
    grad_text, scalars = finish_text(
        chip_part, moved, text_unit, text_inv, logit_scale, total_tokens
    )
    return (grad_image, grad_text, scalars)


def solution(mesh):
    sizes = {"x": 4, "y_lo": 2, "core": 2, "z": 8, "y_hi": 4}
    names = ROW_AXES + BLK_AXES
    fine = Mesh(mesh.devices.reshape([sizes[axis] for axis in names]), names)
    return jax.shard_map(
        functools.partial(body, sizes),
        mesh=fine,
        in_specs=(P(None, names), P(), P(), P(), P(names, None), P(names), P(), P()),
        out_specs=(P(names, None), P(names, None), P()),
        check_vma=False,
    )
```

```python
import functools
import math

import jax
import jax.numpy as jnp
from jax import lax
from jax.experimental import pallas as pl
from jax.experimental.pallas import tpu as pltpu
from jax.sharding import Mesh
from jax.sharding import PartitionSpec as P

EPS = 1e-06
SHARPNESS = 4.0
BITS = 28
SIDE = 128
CHUNK = 256
PROJ_COPIES = 4

ROW_AXES = ("x", "y_lo", "core")
BLK_AXES = ("z", "y_hi")
TEXT_AXES = ("x", "core")
IMAGE_AXES = ("y_hi", "y_lo", "z")


def code_sums(latent):
    bit_count = latent.shape[0]
    length = jnp.sqrt(jnp.sum(latent * latent, axis=0, keepdims=True))
    unit_code = latent / length
    root = 1.0 / math.sqrt(bit_count)
    offset = unit_code - jnp.where(latent > 0, root, -root)
    sharp = SHARPNESS * math.sqrt(bit_count) * unit_code
    size = jnp.abs(sharp)
    small = jnp.exp(-size)
    inverse = 1.0 / (1.0 + small)
    rest = small * inverse
    entropy = jnp.log1p(small) + size * rest
    prob = jnp.where(sharp > 0, inverse, rest)

    def total(values):
        return jnp.sum(jnp.sum(values, axis=1, keepdims=True), axis=0, keepdims=True)

    usage = jnp.sum(prob, axis=1, keepdims=True)
    return (total(offset * offset), total(entropy), usage)


def round_bf(values):
    return values.astype(jnp.bfloat16).astype(jnp.float32)


def gelu(x):
    inner = x * (math.sqrt(2.0 / math.pi) + (math.sqrt(2.0 / math.pi) * 0.044715) * (x * x))
    half = 0.5 * x
    return half + half * jnp.tanh(inner)


def image_kernel(
    copies,
    latent_hbm,
    post_hbm,
    proj_hbm,
    gain_ref,
    label_ref,
    block_ref,
    unit_ref,
    inv_ref,
    latent_ref,
    post_ref,
    proj_ref,
    sems,
):
    fetch_latent = pltpu.make_async_copy(latent_hbm, latent_ref, sems.at[0])
    fetch_post = pltpu.make_async_copy(post_hbm, post_ref, sems.at[1])
    depth = proj_hbm.shape[0] // PROJ_COPIES
    fetch_proj = [
        pltpu.make_async_copy(
            proj_hbm.at[pl.ds(part * depth, depth)],
            proj_ref.at[pl.ds(part * depth, depth)],
            sems.at[2 + part],
        )
        for part in range(PROJ_COPIES)
    ]
    fetch_latent.start()
    fetch_post.start()
    for fetch in fetch_proj:
        fetch.start()
    fetch_latent.wait()
    latent = latent_ref[...]
    bit_count, token_count = latent.shape
    image_count, feat_width = unit_ref.shape
    patch = token_count // image_count

    commit, entropy, usage = code_sums(latent)
    lane = lax.broadcasted_iota(jnp.int32, (bit_count, SIDE), 1)
    bit = lax.broadcasted_iota(jnp.int32, (bit_count, SIDE), 0)
    first = round_bf(usage)
    second = round_bf(usage - first)
    third = usage - first - second
    spread = jnp.where(lane == bit, first, 0.0)
    spread = jnp.where(lane == bit + 32, second, spread)
    spread = jnp.where(lane == bit + 64, third, spread)
    side = jnp.sum(spread, axis=0, keepdims=True)
    place = lax.broadcasted_iota(jnp.int32, (1, SIDE), 1)
    for at, value in ((BITS, commit), (BITS + 1, entropy)):
        first = round_bf(value)
        second = round_bf(value - first)
        third = value - first - second
        side = jnp.where(place == at, first, side)
        side = jnp.where(place == at + 32, second, side)
        side = jnp.where(place == at + 64, third, side)
    sides = []
    for i in range(image_count):
        label = label_ref[i]
        high = (label // 32).astype(jnp.float32)
        low = (label % 32).astype(jnp.float32)
        own = side if i == 0 else jnp.zeros_like(side)
        own = jnp.where(place == SIDE - 2, high, own)
        sides.append(jnp.where(place == SIDE - 1, low, own))
    codes = jnp.where(latent > 0, 1.0, -1.0)
    codes = jnp.transpose(codes, (1, 0)).astype(jnp.bfloat16)
    fetch_post.wait()
    post = post_ref[...]
    sums = []
    for first in range(0, token_count, CHUNK):
        pre_act = jnp.dot(codes[first : first + CHUNK], post, preferred_element_type=jnp.float32)
        hidden = gelu(pre_act).astype(jnp.bfloat16)
        if first == 0:
            for fetch in fetch_proj:
                fetch.wait()
        projected = jnp.dot(hidden, proj_ref[...], preferred_element_type=jnp.float32)
        square = jnp.sum(projected * projected, axis=-1, keepdims=True)
        scaled = projected * lax.rsqrt(square * (1.0 / feat_width) + EPS)
        sums.append(jnp.sum(scaled, axis=0, keepdims=True))
    steps = patch // CHUNK
    rows = [functools.reduce(jnp.add, sums[i * steps : (i + 1) * steps]) for i in range(image_count)]
    embeds = jnp.concatenate(rows, axis=0) * gain_ref[...][None, :] * (1.0 / patch)
    inverse = lax.rsqrt(jnp.sum(embeds * embeds, axis=-1, keepdims=True) + EPS)
    unit = embeds * inverse
    unit_ref[...] = unit
    inv_ref[...] = jnp.broadcast_to(inverse, inv_ref.shape)

    block = jnp.concatenate([unit, jnp.concatenate(sides, axis=0)], axis=1)
    block = block.astype(jnp.bfloat16)
    for member in range(copies):
        block_ref[member] = block


def embed_images(latent, w_post, w_proj, gain, labels, copies):
    image_count = labels.shape[0]
    feat_width = w_proj.shape[1]
    vmem = pl.BlockSpec(memory_space=pltpu.VMEM)
    hbm = pl.BlockSpec(memory_space=pl.ANY)
    return pl.pallas_call(
        functools.partial(image_kernel, copies),
        out_shape=(
            jax.ShapeDtypeStruct((copies, image_count, feat_width + SIDE), jnp.bfloat16),
            jax.ShapeDtypeStruct((image_count, feat_width), jnp.float32),
            jax.ShapeDtypeStruct((image_count, 128), jnp.float32),
        ),
        in_specs=[hbm, hbm, hbm, vmem, pl.BlockSpec(memory_space=pltpu.SMEM)],
        out_specs=(vmem, vmem, vmem),
        scratch_shapes=[
            pltpu.VMEM(latent.shape, latent.dtype),
            pltpu.VMEM(w_post.shape, w_post.dtype),
            pltpu.VMEM(w_proj.shape, w_proj.dtype),
            pltpu.SemaphoreType.DMA((2 + PROJ_COPIES,)),
        ],
        compiler_params=pltpu.CompilerParams(vmem_limit_bytes=56 * 1024 * 1024),
        cost_estimate=pl.CostEstimate(
            flops=2_200_000_000, bytes_accessed=1_800_000, transcendentals=1_100_000
        ),
        name="embed_images",
    )(latent, w_post, w_proj, gain, labels)


def unit_rows(values):
    inverse = lax.rsqrt(jnp.sum(values * values, axis=-1, keepdims=True) + EPS)
    return (values * inverse, inverse)


def tangent(direction, unit, inverse):
    return (direction - unit * jnp.sum(unit * direction, axis=-1, keepdims=True)) * inverse


def text_kernel(text_ref, block_ref, unit_ref, inv_ref):
    unit, inverse = unit_rows(text_ref[...].astype(jnp.float32))
    unit_ref[...] = unit
    inv_ref[...] = jnp.broadcast_to(inverse, inv_ref.shape)
    unit = unit.astype(jnp.bfloat16)
    for member in range(block_ref.shape[0]):
        block_ref[member] = unit


def text_blocks(text_embed, copies):
    rows = text_embed.shape[0]
    vmem = pl.BlockSpec(memory_space=pltpu.VMEM)
    return pl.pallas_call(
        text_kernel,
        out_shape=(
            jax.ShapeDtypeStruct((copies,) + text_embed.shape, jnp.bfloat16),
            jax.ShapeDtypeStruct(text_embed.shape, jnp.float32),
            jax.ShapeDtypeStruct((rows, 128), jnp.float32),
        ),
        in_specs=[vmem],
        out_specs=(vmem, vmem, vmem),
        name="text_blocks",
    )(text_embed)


def finish_kernel(
    total_tokens, chip_ref, moved_ref, unit_ref, inv_ref, scale_ref, grad_ref, scalar_ref
):
    pair_count, feat_width = unit_ref.shape
    total = chip_ref[:pair_count] + moved_ref[...]
    direction = scale_ref[0] * total[:, :feat_width]
    grad_ref[...] = tangent(direction, unit_ref[...], inv_ref[...][:, :1])
    side = total[:1, feat_width:]
    means = side[:, :32] + side[:, 32:64] + side[:, 64:96]
    means = means * (1.0 / total_tokens)
    place = lax.broadcasted_iota(jnp.int32, means.shape, 1)
    usage = jnp.where(place < BITS, means, 0.5)
    spread = -(usage * jnp.log(usage) + (1.0 - usage) * jnp.log(1.0 - usage))
    scalar_ref[0] = jnp.sum(jnp.where(place == BITS, means, 0.0))
    scalar_ref[1] = jnp.sum(jnp.where(place == BITS + 1, means, 0.0))
    scalar_ref[2] = jnp.sum(jnp.where(place < BITS, spread, 0.0))


def finish_text(chip_part, moved, text_unit, text_inv, logit_scale, total_tokens):
    vmem = pl.BlockSpec(memory_space=pltpu.VMEM)
    smem = pl.BlockSpec(memory_space=pltpu.SMEM)
    return pl.pallas_call(
        functools.partial(finish_kernel, total_tokens),
        out_shape=(
            jax.ShapeDtypeStruct(text_unit.shape, jnp.float32),
            jax.ShapeDtypeStruct((3,), jnp.float32),
        ),
        in_specs=[vmem, vmem, vmem, vmem, smem],
        out_specs=(vmem, smem),
        name="finish_text",
    )(chip_part, moved, text_unit, text_inv, logit_scale)


def swap_cores(block):
    return lax.ppermute(block, "core", [(0, 1), (1, 0)])


def along_x(block, distance, count):
    return lax.ppermute(block, "x", [(i, (i + distance) % count) for i in range(count)])


def from_here(members, n_x):
    members = members.reshape((n_x, 2) + members.shape[1:])
    here = lax.axis_index("x")
    other = lax.axis_index("core") == 1
    turned = [
        lax.dynamic_index_in_dim(members, (here + distance) % n_x, 0, keepdims=False)
        for distance in range(n_x)
    ]
    return [
        jnp.where(other, block[1 - core], block[core]) for block in turned for core in range(2)
    ]


def body(sizes, latent, w_post, w_proj, gain, text_embed, labels, logit_scale, logit_bias):
    pair_count, feat_width = text_embed.shape
    n_x = sizes["x"]
    n_image = math.prod(sizes[axis] for axis in IMAGE_AXES)
    n_text = math.prod(sizes[axis] for axis in TEXT_AXES)
    text_count = n_text * pair_count
    chip_count = 2 * pair_count
    total_tokens = latent.shape[1] * math.prod(sizes.values())
    scale_value = logit_scale[0]
    bias_value = logit_bias[0]

    text_block, text_unit, text_inv = text_blocks(text_embed, n_text)
    group_text = lax.all_to_all(text_block, TEXT_AXES, 0, 0)
    group_text = jnp.concatenate(from_here(group_text, n_x), axis=0)

    image_block, image_unit, image_inv = embed_images(
        latent, w_post, w_proj, gain, labels, n_image
    )
    group_block = lax.all_to_all(image_block, IMAGE_AXES, 0, 0)
    group_block = group_block.reshape(n_image * pair_count, feat_width + SIDE)
    group_image = group_block[:, :feat_width]
    group_side = group_block[:, feat_width:].astype(jnp.float32)
    group_labels = (group_side[:, SIDE - 2] * 32.0 + group_side[:, SIDE - 1]).astype(jnp.int32)
    group_sums = jnp.sum(group_side, axis=0, keepdims=True)

    row_size = sizes["y_lo"] * sizes["core"]
    blk_size = sizes["z"] * sizes["y_hi"]
    place = jnp.arange(text_count, dtype=jnp.int32)
    text_x = (lax.axis_index("x") + place // chip_count) % n_x
    text_core = lax.axis_index("core") ^ (place // pair_count % 2)
    text_row = text_x * row_size + lax.axis_index("y_lo") * sizes["core"] + text_core
    text_blk = lax.axis_index("z") * sizes["y_hi"] + lax.axis_index("y_hi")
    text_ids = (text_row * blk_size + text_blk) * pair_count + place % pair_count

    products = jnp.dot(group_image, group_text.T, preferred_element_type=jnp.float32)
    pair_sign = jnp.where(
        group_labels[:, None] == text_ids[None, :], jnp.float32(1.0), jnp.float32(-1.0)
    )
    margin = pair_sign * (scale_value * products + bias_value)
    grad_bf = (-pair_sign * jax.nn.sigmoid(-margin)).astype(jnp.bfloat16)
    image_part = jnp.dot(grad_bf, group_text, preferred_element_type=jnp.float32)
    image_part = image_part.reshape(n_image, pair_count, feat_width)
    image_part = lax.all_to_all(image_part, IMAGE_AXES, 0, 0)

    text_part = jnp.dot(grad_bf.T, group_image, preferred_element_type=jnp.float32)
    text_part = jnp.concatenate(
        [text_part, jnp.broadcast_to(group_sums, (text_count, SIDE))], axis=1
    )
    chip_part = text_part[:chip_count]
    for distance in range(1, n_x):
        rows = text_part[distance * chip_count : (distance + 1) * chip_count]
        chip_part = chip_part + along_x(rows, distance, n_x)
    moved = swap_cores(chip_part[pair_count:])

    image_dir = scale_value * jnp.sum(image_part, axis=0)
    grad_image = tangent(image_dir, image_unit, image_inv[:, :1])
    grad_image, moved = lax.optimization_barrier((grad_image, moved))
    grad_text, scalars = finish_text(
        chip_part, moved, text_unit, text_inv, logit_scale, total_tokens
    )
    return (grad_image, grad_text, scalars)


def solution(mesh):
    sizes = {"x": 4, "y_lo": 2, "core": 2, "z": 8, "y_hi": 4}
    names = ROW_AXES + BLK_AXES
    fine = Mesh(mesh.devices.reshape([sizes[axis] for axis in names]), names)
    return jax.shard_map(
        functools.partial(body, sizes),
        mesh=fine,
        in_specs=(P(None, names), P(), P(), P(), P(names, None), P(names), P(), P()),
        out_specs=(P(names, None), P(names, None), P()),
        check_vma=False,
    )
```
